32 devices in a mesh: dp: 32 (over z, y, x, core).
Axes of the slice: x: 2, y: 2, z: 4, core: 2. Of those that a mesh axis runs over, the one named last changes fastest.
Arguments:
- big_crops: bfloat16 [1024, 7, 7, 2048], P('dp'), may hold values from -6 to 6
- small_crops: bfloat16 [4096, 3, 3, 2048], P('dp'), may hold values from -6 to 6
- small_count: int32 [512], P('dp'), may hold values from 2 to 8
- w_reduce: bfloat16 [2048, 512], replicated, may hold values from -0.125 to 0.125
- w_spatial: bfloat16 [512, 9, 512], replicated, may hold values from -0.09375 to 0.09375
- w_expand: bfloat16 [512, 2048], replicated, may hold values from -0.25 to 0.25
- gain_mid: float32 [2, 512], replicated, may hold values from 0.5 to 1.5
- bias_mid: float32 [2, 512], replicated, may hold values from -3 to 3
- gain_wide: float32 [2048], replicated, may hold values from 0.5 to 1.5
- bias_wide: float32 [2048], replicated, may hold values from -3 to 3
- w_hidden: bfloat16 [2048, 2048], replicated, may hold values from -0.125 to 0.125
- gain_head: float32 [2048], replicated, may hold values from 0.5 to 1.5
- bias_head: float32 [2048], replicated, may hold values from -3 to 3
- w_project: bfloat16 [2048, 128], replicated, may hold values from -0.125 to 0.125
- prototypes: bfloat16 [128, 3000], replicated, may hold values from -0.8984375 to 0.8984375
- queue: bfloat16 [2, 960, 128], P(None, 'dp'), may hold values from -6 to 6
Outputs:
- loss: float32 [], replicated
- grad_big: bfloat16 [1024, 7, 7, 2048], P('dp')
- grad_small: bfloat16 [4096, 3, 3, 2048], P('dp')
- grad_w_reduce: float32 [2048, 512], P('dp')
- grad_w_spatial: float32 [512, 9, 512], P('dp')
- grad_w_expand: float32 [512, 2048], P('dp')
- grad_gain_mid: float32 [2, 512], replicated
- grad_bias_mid: float32 [2, 512], replicated
- grad_gain_wide: float32 [2048], replicated
- grad_bias_wide: float32 [2048], replicated
- grad_w_hidden: float32 [2048, 2048], P('dp')
- grad_gain_head: float32 [2048], replicated
- grad_bias_head: float32 [2048], replicated
- grad_w_project: float32 [2048, 128], P('dp')
- grad_prototypes: float32 [128, 3000], P('dp')
The draws below stay inside these ranges and needn't reach their ends.
All inputs are finite; a program needn't handle non-finite values.
Results may differ from the reference program's by a relative error of at most 0.025.
Values sent between devices are 32-bit elements; how exact they have to be, the bound alone decides.
No kernel may reach another device: no remote copies, remote signals or barrier semaphores. Data moves between devices by JAX's collectives and lax.ppermute only.
A program may use at most 320 MiB of HBM per device.

```python
import jax
import jax.numpy as jnp
from jax import lax

WIDE = 2048
MID = 512
HID = 2048
PROJ = 128
PROTO = 3000
VIEWS = 2
BIG_SIDE = 7
SMALL_SIDE = 3
SLOTS = 8
ITERS = 3
IMAGES = 512
BIG = 1024
SMALL = 4096
QUEUE = 960


def with_ends(entries, key, smallest, high):
    spot = [jax.random.randint(jax.random.fold_in(key, axis), (), 0, length) for axis, length in enumerate(entries.shape)]
    main_axis = entries.shape.index(max(entries.shape))
    next_to = spot[:main_axis] + [(spot[main_axis] + 1) % entries.shape[main_axis]] + spot[main_axis + 1:]
    return entries.at[tuple(spot)].set(smallest).at[tuple(next_to)].set(high)


def strengthened(values, key, source, target, blocks, factor):
    def block_of(dim):
        return (jnp.arange(values.shape[dim]) // (values.shape[dim] // blocks)).reshape((-1,) + (1,) * (values.ndim - 1 - dim))

    first = jax.random.permutation(key, blocks)[block_of(target)]
    other_side = (block_of(target) + blocks // 2) % blocks
    return jnp.where((block_of(source) == first) | (block_of(source) == other_side), factor * values, values)


def level_of(rng, extent, pieces, least, top_value):
    level = 1.0
    for dim, blocks in pieces:
        steps = jax.random.uniform(jax.random.fold_in(jax.random.fold_in(rng, 6), dim), (blocks,), jnp.float32, least / len(pieces), top_value / len(pieces))
        level = level * jnp.repeat(jnp.exp(steps), extent[dim] // blocks).reshape((-1,) + (1,) * (len(extent) - 1 - dim))
    return level


def scatter_about(own_key, dims, scale, reach, split=(), dtype=jnp.bfloat16):
    array = jax.random.normal(own_key, dims, jnp.float32) * scale
    if len(split) > 0:
        array = level_of(own_key, dims, split, -0.22, 0.18) * array
    return jnp.clip(array, min=-reach, max=reach).astype(dtype)


def heavy_noise(own_key, dims, scale, reach, split, heavy, held_as=jnp.bfloat16):
    array = scale * jax.random.normal(own_key, dims, jnp.float32)
    if split:
        array = array * level_of(own_key, dims, split, -0.22, 0.18)
    return jnp.clip(strengthened(array, jax.random.fold_in(own_key, 3), *heavy), -reach, reach).astype(held_as)


def setup_inputs(seed: int = 0) -> dict:
    splits = jax.random.split(jax.random.key(seed), 17)
    return {
        "big_crops": heavy_noise(splits[0], (BIG, BIG_SIDE, BIG_SIDE, WIDE), 1.0, 6.0, ((0, 32),), (0, 3, 32, 2.75)),
        "small_crops": heavy_noise(splits[1], (SMALL, SMALL_SIDE, SMALL_SIDE, WIDE), 1.0, 6.0, ((0, 32),), (0, 3, 32, 2.75)),
        "small_count": with_ends(jax.random.randint(splits[2], (IMAGES,), 2, SLOTS + 1), jax.random.fold_in(splits[2], 1), 2, SLOTS).astype(jnp.int32),
        "w_reduce": scatter_about(splits[3], (WIDE, MID), WIDE ** -0.5, 0.125),
        "w_spatial": scatter_about(splits[4], (MID, 9, MID), (9 * MID) ** -0.5, 0.09375),
        "w_expand": scatter_about(splits[5], (MID, WIDE), MID ** -0.5, 0.25),
        "gain_mid": jnp.clip(jax.random.uniform(splits[6], (2, MID), jnp.float32, 0.5, 1.5), 0.5, 1.5),
        "bias_mid": scatter_about(splits[7], (2, MID), 0.5, 3.0, (), jnp.float32),
        "gain_wide": jnp.clip(jax.random.uniform(splits[8], (WIDE,), jnp.float32, 0.5, 1.5), 0.5, 1.5),
        "bias_wide": scatter_about(splits[9], (WIDE,), 0.5, 3.0, (), jnp.float32),
        "w_hidden": scatter_about(splits[10], (WIDE, HID), WIDE ** -0.5, 0.125),
        "gain_head": jnp.clip(jax.random.uniform(splits[11], (HID,), jnp.float32, 0.5, 1.5), 0.5, 1.5),
        "bias_head": scatter_about(splits[12], (HID,), 0.5, 3.0, (), jnp.float32),
        "w_project": scatter_about(splits[13], (HID, PROJ), HID ** -0.5, 0.125),
        "prototypes": scatter_about(splits[14], (PROJ, PROTO), 0.15, 0.8984375),
        "queue": scatter_about(splits[15], (VIEWS, QUEUE, PROJ), 1.0, 6.0, ((1, 32),)),
    }


EPS_NORM = 1e-05
EPS_UNIT = 1e-06
EPS_CODE = 0.05
SOFTMAX_HEAT = 0.1
HIGHEST_PRECISION = lax.Precision.HIGHEST

@jax.custom_vjp
def low(v):
    return lax.optimization_barrier(v.astype(jnp.bfloat16)).astype(jnp.float32)

@jax.custom_vjp
def low_back(v):
    return v

def low_keep(v):
    return (low(v), None)

def low_pass(kept, grad):
    return (grad,)

def back_keep(v):
    return (v, None)

def back_low(kept, grad):
    return (low(grad),)
low.defvjp(low_keep, low_pass)
low_back.defvjp(back_keep, back_low)

def product(left, right):
    return jnp.dot(left, right, precision=HIGHEST_PRECISION)

def normalize(value_entries, weight, count, gain, bias):
    mean = lax.optimization_barrier(jnp.sum(value_entries * weight[:, None], axis=0)) / count
    centered = value_entries - mean
    spread = lax.optimization_barrier(jnp.sum(weight[:, None] * centered * centered, axis=0)) / count
    return centered * lax.rsqrt(spread + EPS_NORM) * gain + bias

def spatial(field, weight, crops, side):
    channels = field.shape[1]
    padded = jnp.pad(field.reshape(crops, side, side, channels), ((0, 0), (1, 1), (1, 1), (0, 0)))
    total = jnp.zeros((crops * side * side, weight.shape[2]), jnp.float32)
    for tap in range(9):
        row = tap // 3
        column = tap % 3
        window = padded[:, row:row + side, column:column + side, :].reshape(crops * side * side, channels)
        total = total + product(window, weight[:, tap, :])
    return total

def scores_of(inputs, params, pixel_weight, crop_weight, pixel_count, crop_count):
    w_reduce, w_spatial, w_expand, gain_mid, bias_mid, gain_wide, bias_wide, w_hidden, gain_head, bias_head, w_project, prototypes = params
    big_pixels = BIG * BIG_SIDE * BIG_SIDE
    first = low_back(product(inputs, w_reduce))
    mid_one = low(jax.nn.silu(normalize(first, pixel_weight, pixel_count, gain_mid[0], bias_mid[0])))
    second = jnp.concatenate([spatial(mid_one[:big_pixels], w_spatial, BIG, BIG_SIDE), spatial(mid_one[big_pixels:], w_spatial, SMALL, SMALL_SIDE)])
    second = low_back(second)
    mid_two = low(jax.nn.silu(normalize(second, pixel_weight, pixel_count, gain_mid[1], bias_mid[1])))
    third = low_back(product(mid_two, w_expand))
    output = jax.nn.silu(normalize(third, pixel_weight, pixel_count, gain_wide, bias_wide) + inputs)
    pooled = jnp.concatenate([lax.optimization_barrier(jnp.mean(output[:big_pixels].reshape(BIG, BIG_SIDE * BIG_SIDE, WIDE), axis=1)), lax.optimization_barrier(jnp.mean(output[big_pixels:].reshape(SMALL, SMALL_SIDE * SMALL_SIDE, WIDE), axis=1))])
    pooled = low(pooled)
    hidden = low_back(product(pooled, w_hidden))
    active = low(jax.nn.silu(normalize(hidden, crop_weight, crop_count, gain_head, bias_head)))
    embedded = low_back(product(active, w_project))
    unit = low(embedded * lax.rsqrt(lax.optimization_barrier(jnp.sum(embedded * embedded, axis=1, keepdims=True)) + EPS_UNIT))
    return low_back(product(unit, prototypes))

def balanced_assignment(batch_score_rows, queue_score_rows):
    batch_exp = jnp.exp(batch_score_rows / EPS_CODE)
    queue_exp = jnp.exp(queue_score_rows / EPS_CODE)
    for step in range(ITERS):
        totals = lax.optimization_barrier(jnp.sum(batch_exp, axis=1, keepdims=True)) + lax.optimization_barrier(jnp.sum(queue_exp, axis=1, keepdims=True))
        batch_exp = batch_exp / totals
        queue_exp = queue_exp / totals
        batch_exp = batch_exp / lax.optimization_barrier(jnp.sum(batch_exp, axis=2, keepdims=True))
        queue_exp = queue_exp / lax.optimization_barrier(jnp.sum(queue_exp, axis=2, keepdims=True))
    return batch_exp

def loss_from(prototype_scores, code_targets, slot_mask, small_count):
    log_probability = jax.nn.log_softmax(prototype_scores / SOFTMAX_HEAT, axis=1)
    big_logp = log_probability[:BIG].reshape(IMAGES, VIEWS, PROTO)
    small_logp = log_probability[BIG:].reshape(IMAGES, SLOTS, PROTO)
    total = lax.optimization_barrier(jnp.sum(big_logp, axis=1)) + lax.optimization_barrier(jnp.sum(small_logp * slot_mask[:, :, None], axis=1))
    per_view = lax.optimization_barrier(jnp.sum(code_targets * (total[:, None, :] - big_logp), axis=2))
    share = 1.0 / (VIEWS * (VIEWS - 1.0 + small_count.astype(jnp.float32)))
    return -jnp.sum(lax.optimization_barrier(jnp.sum(per_view, axis=1)) * share) / IMAGES

def reference(big_crops, small_crops, small_count, w_reduce, w_spatial, w_expand, gain_mid, bias_mid, gain_wide, bias_wide, w_hidden, gain_head, bias_head, w_project, prototypes, queue):
    slot_mask = (jnp.arange(SLOTS)[None, :] < small_count[:, None]).astype(jnp.float32)
    flags = slot_mask.reshape(-1)
    crop_weight = jnp.concatenate([jnp.ones((BIG,), jnp.float32), flags])
    pixel_weight = jnp.concatenate([jnp.ones((BIG * BIG_SIDE * BIG_SIDE,), jnp.float32), jnp.repeat(flags, SMALL_SIDE * SMALL_SIDE)])
    count_sum = jnp.sum(small_count).astype(jnp.float32)
    pixel_count = BIG * BIG_SIDE * BIG_SIDE + SMALL_SIDE * SMALL_SIDE * count_sum
    crop_count = BIG + count_sum
    inputs = jnp.concatenate([big_crops.reshape(-1, WIDE), small_crops.reshape(-1, WIDE)]).astype(jnp.float32)
    params = tuple((p.astype(jnp.float32) for p in (w_reduce, w_spatial, w_expand, gain_mid, bias_mid, gain_wide, bias_wide, w_hidden, gain_head, bias_head, w_project, prototypes)))
    queue_float = queue.astype(jnp.float32)

    def forward_all(flat_inputs, weights):
        crop_scores = scores_of(flat_inputs, weights, pixel_weight, crop_weight, pixel_count, crop_count)
        queue_unit = low(queue_float * lax.rsqrt(lax.optimization_barrier(jnp.sum(queue_float * queue_float, axis=2, keepdims=True)) + EPS_UNIT))
        queue_score_rows = jnp.einsum('vqp,pk->vqk', queue_unit, weights[11], precision=HIGHEST_PRECISION)
        return (crop_scores, queue_score_rows)
    (score_value, queue_score_rows), pull = jax.vjp(forward_all, inputs, params)
    batch_score_rows = jnp.transpose(score_value[:BIG].reshape(IMAGES, VIEWS, PROTO), (1, 0, 2))
    code_targets = jnp.transpose(balanced_assignment(batch_score_rows, queue_score_rows), (1, 0, 2))

    def score_loss(value_entries):
        return loss_from(value_entries, code_targets, slot_mask, small_count)
    loss, loss_pull = jax.vjp(score_loss, score_value)
    grad_scores = loss_pull(jnp.ones((), jnp.float32))[0]
    grad_inputs, grads = pull((grad_scores, jnp.zeros_like(queue_score_rows)))
    big_pixels = BIG * BIG_SIDE * BIG_SIDE
    grad_big = grad_inputs[:big_pixels].reshape(big_crops.shape).astype(jnp.bfloat16)
    grad_small = grad_inputs[big_pixels:].reshape(small_crops.shape).astype(jnp.bfloat16)
    return (loss, grad_big, grad_small, grads[0], grads[1], grads[2], grads[3], grads[4], grads[5], grads[6], grads[7], grads[8], grads[9], grads[10], grads[11])
```

```python
import math

import jax
import jax.numpy as jnp
from jax import lax
from jax.experimental import pallas as pl
from jax.experimental.pallas import tpu as pltpu
from jax.sharding import PartitionSpec as P

ITERS = 3

EPS_NORM = 1e-05
EPS_UNIT = 1e-06
EPS_CODE = 0.05
SOFTMAX_HEAT = 0.1
LANES = 128
PLANE = 8
CHUNK = 512
TILE = 256
ROWS = 32
VMEM_LIMIT = 60 << 20
FLOAT = jnp.float32
HALF = jnp.bfloat16


def product(left, right):
    return jnp.dot(left, right, preferred_element_type=FLOAT)


def product_inner(left, right):
    return lax.dot_general(left, right, (((0,), (0,)), ((), ())), preferred_element_type=FLOAT)


def product_outer(left, right):
    return lax.dot_general(left, right, (((1,), (1,)), ((), ())), preferred_element_type=FLOAT)


def sigmoid(value):
    return 0.5 * jnp.tanh(0.5 * value) + 0.5


def silu(value):
    return value * sigmoid(value)


def slope(value):
    gate = sigmoid(value)
    return gate * (1.0 + value * (1.0 - gate))


def column_sum(value):
    return jnp.sum(value, axis=0, keepdims=True)


def shape(dims, dtype=FLOAT):
    return jax.ShapeDtypeStruct(dims, dtype)


def far_shape(dims, dtype=FLOAT):
    return pltpu.HBM(dims, dtype)


def far(array):
    return pltpu.with_memory_space_constraint(array, pltpu.HBM)


def whole(dims):
    return pl.BlockSpec(dims, lambda *_: (0,) * len(dims))


def call(
    kernel,
    out_shape,
    args,
    grid=None,
    in_specs=None,
    out_specs=None,
    flops=0,
    after=(),
    scalars=(),
    streamed=(),
    aliases=None,
    spill=0,
):
    flat = out_shape if isinstance(out_shape, (list, tuple)) else [out_shape]
    size = sum(a.size * a.dtype.itemsize for a in args)
    size += sum(math.prod(a.shape) * jnp.dtype(a.dtype).itemsize for a in flat)
    args = [far(a) if k in streamed else a for k, a in enumerate(args)]
    here = pl.BlockSpec(memory_space=pltpu.VMEM)
    limit = spill
    if grid is None:
        in_specs = [here] * len(args)
        out_specs = jax.tree.map(lambda _: here, out_shape)
        limit = max(limit, size + size // 4 + (2 << 20))
    else:
        limit = 20 << 20
    first, last = len(scalars), len(scalars) + len(args)

    def run(*refs):
        kernel(*refs[:last], *refs[last + len(after) :])

    specs = dict(out_specs=out_specs)
    if grid is not None:
        specs["grid"] = grid
    return pl.pallas_call(
        run,
        out_shape=out_shape,
        in_specs=[pl.BlockSpec(memory_space=pltpu.SMEM)] * first
        + list(in_specs)
        + [pl.BlockSpec(memory_space=pl.ANY)] * len(after),
        input_output_aliases={first + k: v for k, v in (aliases or {}).items()},
        compiler_params=pltpu.CompilerParams(vmem_limit_bytes=min(limit, VMEM_LIMIT)),
        cost_estimate=pl.CostEstimate(flops=flops, bytes_accessed=size, transcendentals=0),
        **specs,
    )(*scalars, *args, *after)


def copy_kernel(source, out):
    out[...] = source[...]


def tie(value, after):
    return call(copy_kernel, shape(value.shape, value.dtype), [value], after=after)


def rounds(devices):
    bits = [1 << k for k in range(devices.bit_length() - 1)]
    return [bits[:1]] + [bits[k : k + 2] for k in range(1, len(bits), 2)]


def peers(value, bits, devices):
    masks = [0]
    for bit in bits:
        masks = masks + [mask | bit for mask in masks]
    return [value] + [
        lax.ppermute(value, "dp", [(i, i ^ mask) for i in range(devices)]) for mask in masks[1:]
    ]


def tree(values):
    while len(values) > 1:
        values = [values[k] + values[k + 1] for k in range(0, len(values), 2)]
    return values[0]


def exchange(value, devices, merge, works=()):
    first, *others = rounds(devices)
    parts = peers(value, first, devices)
    for k, bits in enumerate(others):
        value = merge(parts)
        parts = peers(value, bits, devices)
        if k < len(works):
            parts[0] = tie(value, works[k](value))
    return parts


def sum_parts(value, devices, works=()):
    return exchange(value, devices, tree, works)


def merged(parts):
    channels = (parts[0].shape[1] - LANES) // 2
    counts = [part[:, 2 * channels : 2 * channels + 1] for part in parts]
    means = [part[:, :channels] for part in parts]
    spreads = [part[:, channels : 2 * channels] for part in parts]
    total = tree(counts)
    mean = tree([c * m for c, m in zip(counts, means)]) / total
    spread = tree([s + c * jnp.square(m - mean) for s, c, m in zip(spreads, counts, means)])
    return total, mean, spread


def merge_kernel(*refs):
    *parts, out = refs
    channels = (out.shape[1] - LANES) // 2
    total, mean, spread = merged([part[...] for part in parts])
    out[:, :channels] = mean
    out[:, channels : 2 * channels] = spread
    out[:, 2 * channels :] = jnp.broadcast_to(total, (1, LANES))


def merge_norms(parts):
    return call(merge_kernel, shape(parts[0].shape), parts)


def settle_kernel(*refs):
    *parts, gain, bias, scale, offset, mean_out, root_out, count = refs
    total, mean, spread = merged([part[...] for part in parts])
    root = lax.rsqrt(spread / total + EPS_NORM)
    factor = gain[...] * root
    scale[...] = factor
    offset[...] = bias[...] - mean * factor
    mean_out[...] = mean
    root_out[...] = root
    count[...] = jnp.broadcast_to(total, (1, LANES))


def settle_norm(packed, gain, bias, devices):
    channels = gain.shape[0]
    parts = exchange(packed, devices, merge_norms)
    row = shape((1, channels))
    return call(
        settle_kernel,
        [row, row, row, row, shape((1, LANES))],
        [*parts, gain[None], bias[None]],
    )


def settle_back_kernel(*refs):
    *parts, gain, mean, root, count, first, second, third, gain_sum, bias_sum, extra = refs
    channels = gain.shape[1]
    packed = tree([part[...] for part in parts])
    total = count[:, :1]
    low, high = packed[:, :channels], packed[:, channels : 2 * channels]
    factor = gain[...] * root[...]
    pull = root[...] * high / total
    first[...] = factor
    second[...] = factor * (mean[...] * pull - low / total)
    third[...] = -factor * pull
    gain_sum[...] = high
    bias_sum[...] = low
    extra[...] = packed[:, 2 * channels :]


def settle_back(packed, gain, mean, root, count, devices, works=()):
    parts = sum_parts(packed, devices, works)
    row = shape((1, gain.shape[0]))
    return call(
        settle_back_kernel,
        [row, row, row, row, row, shape((1, LANES))],
        [*parts, gain[None], mean, root, count],
    )


def pick(bits, place):
    return (bits[0] >> place) & 1


def send_kernel(bits, value, send):
    other = 1 - pick(bits, 0)

    def step(t, _):
        for k in range(send.shape[1]):
            send[t, k] = value[t, 2 * k + other]
        return _

    lax.fori_loop(0, value.shape[0], step, 0)


def send_rows(value, me, after):
    taps, devices, rows, width = value.shape
    out = shape((taps, devices // 2, rows, width))
    return call(send_kernel, out, [value], scalars=[me], after=after)


def first_kernel(bits, keep, got, keep_one, send_one, keep_two, send_two):
    taps, blocks, _, width = got.shape
    uncut = keep.shape[1] // blocks
    half = pick(bits, 0) * (uncut - 1)
    left, right = slice(0, width // 2), slice(width // 2, width)
    one, two = pick(bits, 1), pick(bits, 2)

    def step(t, _):
        for k in range(blocks // 2):
            for out, there in ((keep_one, 2 * k + one), (send_one, 2 * k + 1 - one)):
                out[t, k] = keep[t, uncut * there + half, :, left] + got[t, there, :, left]
            low = 4 * (k // 2) + k % 2
            for out, there in ((keep_two, low + 2 * two), (send_two, low + 2 * (1 - two))):
                out[t, k] = keep[t, uncut * there + half, :, right] + got[t, there, :, right]
        return _

    lax.fori_loop(0, taps, step, 0)


def second_kernel(bits, keep_one, got_one, keep_two, got_two, *outs):
    def step(t, _):
        for keep, got, place, out_keep, out_send in (
            (keep_one, got_one, 2, outs[0], outs[1]),
            (keep_two, got_two, 1, outs[2], outs[3]),
        ):
            half = pick(bits, place)
            for k in range(out_keep.shape[1]):
                out_keep[t, k] = keep[t, 2 * k + half] + got[t, 2 * k + half]
                out_send[t, k] = keep[t, 2 * k + 1 - half] + got[t, 2 * k + 1 - half]
        return _

    lax.fori_loop(0, keep_one.shape[0], step, 0)


def third_kernel(bits, keep_one, got_one, keep_two, got_two, out_keep, out_send):
    half = pick(bits, 3)
    width = keep_one.shape[3]

    def step(t, _):
        for k in range(out_keep.shape[1]):
            for out, there in ((out_keep, 2 * k + half), (out_send, 2 * k + 1 - half)):
                out[t, k, :, :width] = keep_one[t, there] + got_one[t, there]
                out[t, k, :, width:] = keep_two[t, there] + got_two[t, there]
        return _

    lax.fori_loop(0, keep_one.shape[0], step, 0)


def later_kernel(place, bits, keep, got, out_keep, out_send):
    half = pick(bits, place)

    def step(t, _):
        for k in range(out_keep.shape[1]):
            for out, there in ((out_keep, 2 * k + half), (out_send, 2 * k + 1 - half)):
                out[t, k] = keep[t, there] + got[t, there]
        return _

    lax.fori_loop(0, keep.shape[0], step, 0)


def last_kernel(keep, got, out):
    out[...] = keep[...] + got[...]


class Scatter:
    def __init__(self, keep, send, devices, me):
        self.devices, self.me = devices, me
        self.bits = devices.bit_length() - 1
        self.held = [keep]
        self.got = [self.cross(send, 0)]
        self.stage = 0

    def cross(self, value, place):
        return lax.ppermute(
            value, "dp", [(i, i ^ (1 << place)) for i in range(self.devices)]
        )

    def go(self, after=()):
        taps, blocks, rows, width = self.got[0].shape
        if self.stage == 0:
            out = shape((taps, blocks // 2, rows, width // 2))
            kernel, places = first_kernel, (1, 2)
        elif self.stage == 1:
            out = shape((taps, blocks // 2, rows, width))
            kernel, places = second_kernel, (2, 1)
        elif self.stage == 2:
            out = shape((taps, blocks // 2, rows, 2 * width))
            kernel, places = third_kernel, (3,)
        else:
            place = self.stage + 1
            out = shape((taps, blocks // 2, rows, width))
            kernel, places = (lambda *refs: later_kernel(place, *refs)), (place,)
        args = [a for pair in zip(self.held, self.got) for a in pair]
        made = call(kernel, [out] * (2 * len(places)), args, after=after, scalars=[self.me])
        self.held = list(made[::2])
        self.got = [self.cross(send, place) for send, place in zip(made[1::2], places)]
        self.stage += 1
        return self.held[0]

    def complete(self):
        return self.got[0].shape[1] == 1

    def end(self):
        while not self.complete():
            self.go()
        taps, _, rows, width = self.held[0].shape
        done = call(last_kernel, shape(self.held[0].shape), [self.held[0], self.got[0]])
        return done.reshape(taps, rows, width)


def weight_grad_kernel(rows, bits, left_big, right_big, left_small, right_small, keep, send):
    value = product_inner(left_big[...], right_big[...])
    value = value + product_inner(left_small[...], right_small[...])
    half = pick(bits, 0)
    for k in range(value.shape[0] // (2 * rows)):
        even = value[2 * k * rows : (2 * k + 1) * rows]
        odd = value[(2 * k + 1) * rows : (2 * k + 2) * rows]
        keep[0, k] = jnp.where(half == 0, even, odd)
        send[0, k] = jnp.where(half == 0, odd, even)


def weight_grad(left, right, devices, me, along, after=(), streamed=()):
    height, width = left[0].shape[1], right[0].shape[1]
    rows = height // devices
    out = shape((1, devices // 2, rows, width))

    def spec(pair, k, moves):
        dims = (pair[k].shape[0], CHUNK if moves else pair[k].shape[1])
        return pl.BlockSpec(dims, lambda j: (0, j if moves else 0))

    if along == 0:
        steps = height // CHUNK
        block = pl.BlockSpec((1, devices // 2 // steps, rows, width), lambda j: (0, j, 0, 0))
    else:
        steps = width // CHUNK
        block = pl.BlockSpec((1, devices // 2, rows, CHUNK), lambda j: (0, 0, 0, j))
    return call(
        lambda *refs: weight_grad_kernel(rows, *refs),
        [out, out],
        [left[0], right[0], left[1], right[1]],
        grid=(steps,),
        in_specs=[
            spec(left, 0, along == 0),
            spec(right, 0, along == 1),
            spec(left, 1, along == 0),
            spec(right, 1, along == 1),
        ],
        out_specs=[block, block],
        flops=2 * (left[0].shape[0] + left[1].shape[0]) * height * width,
        after=after,
        streamed=streamed,
        scalars=[me],
    )


class Rows:
    def __init__(self, big_side, big_crops, small_side, small_crops):
        self.steps = big_side, small_side
        self.rows = big_side * big_crops, small_side * small_crops
        self.crops = big_crops, small_crops

    def specs(self, channels):
        first = self.steps[0]
        return [
            pl.BlockSpec((self.rows[0], channels), lambda i: (jnp.minimum(i, first - 1), 0)),
            pl.BlockSpec((self.rows[1], channels), lambda i: (jnp.maximum(i - first, 0), 0)),
        ]

    def shapes(self, channels, dtype, place=shape):
        return [place((s * r, channels), dtype) for s, r in zip(self.steps, self.rows)]

    def run(self, body, args, row_outs, whole_outs, flops, after=(), streamed=(), aliases=None):
        pairs = [a for a in args if isinstance(a, tuple)]
        rest = [a for a in args if not isinstance(a, tuple)]
        in_specs, flat = [], []
        for pair in pairs:
            in_specs += self.specs(pair[0].shape[1])
            flat += list(pair)
        in_specs += [whole(a.shape) for a in rest]
        out_shapes, out_specs = [], []
        for channels, dtype, *place in row_outs:
            out_shapes += self.shapes(channels, dtype, *place)
            out_specs += self.specs(channels)
        out_shapes += [shape(dims) for dims in whole_outs]
        out_specs += [whole(dims) for dims in whole_outs]
        n_in, n_rest, n_out = len(pairs), len(rest), len(row_outs)

        def kernel(*refs):
            i = pl.program_id(0)
            given, fixed = refs[: 2 * n_in], refs[2 * n_in : 2 * n_in + n_rest]
            made = refs[2 * n_in + n_rest :]
            for kind in range(2):
                here = i < self.steps[0] if kind == 0 else i >= self.steps[0]

                @pl.when(here)
                def _(kind=kind):
                    body(
                        i,
                        kind,
                        given[kind : 2 * n_in : 2],
                        fixed,
                        made[kind : 2 * n_out : 2],
                        made[2 * n_out :],
                    )

        made = call(
            kernel,
            out_shapes,
            flat + rest,
            grid=(sum(self.steps),),
            in_specs=in_specs,
            out_specs=out_specs,
            flops=flops,
            after=after,
            streamed=[2 * k + j for k in streamed for j in range(2)],
            aliases={2 * k + j: 2 * v + j for k, v in (aliases or {}).items() for j in range(2)},
        )
        return [tuple(made[2 * k : 2 * k + 2]) for k in range(n_out)] + list(made[2 * n_out :])

    def total(self):
        return sum(s * r for s, r in zip(self.steps, self.rows))


def add_norm(i, kind, packed, value, weight, start):
    channels = (packed.shape[1] - LANES) // 2
    width = value.shape[1]
    here = slice(start, start + width)
    there = slice(channels + start, channels + start + width)
    if kind == 0:
        count = jnp.full((1, 1), value.shape[0], FLOAT)
        mean = column_sum(value) * (1.0 / value.shape[0])
        spread = column_sum(jnp.square(value - mean))
    else:
        count = column_sum(weight)
        mean = column_sum(value * weight) / count
        spread = column_sum(jnp.square(value - mean) * weight)

    def begin():
        packed[:, here] = mean
        packed[:, there] = spread

    def go_on():
        before = packed[:, 2 * channels : 2 * channels + 1]
        part = count / (before + count)
        old = packed[:, here]
        delta = mean - old
        packed[:, here] = old + delta * part
        packed[:, there] = packed[:, there] + spread + jnp.square(delta) * (before * part)

    if kind == 0:
        pl.when(i == 0)(begin)
        pl.when(i > 0)(go_on)
    else:
        go_on()
    return count


def add_count(i, kind, packed, count):
    channels = (packed.shape[1] - LANES) // 2
    lanes = slice(2 * channels, 2 * channels + LANES)
    wide_count = jnp.broadcast_to(count, (1, LANES))

    def begin():
        packed[:, lanes] = wide_count

    def go_on():
        packed[:, lanes] = packed[:, lanes] + wide_count

    if kind == 0:
        pl.when(i == 0)(begin)
        pl.when(i > 0)(go_on)
    else:
        go_on()


def add_sums(i, kind, packed, low, high, start):
    channels = (packed.shape[1] - LANES) // 2
    width = low.shape[1]
    here = slice(start, start + width)
    there = slice(channels + start, channels + start + width)

    def begin():
        packed[:, here] = low
        packed[:, there] = high
        if start == 0:
            packed[:, 2 * channels :] = jnp.zeros((1, LANES), FLOAT)

    def go_on():
        packed[:, here] = packed[:, here] + low
        packed[:, there] = packed[:, there] + high

    if kind == 0:
        pl.when(i == 0)(begin)
        pl.when(i > 0)(go_on)
    else:
        go_on()


def reduce_stage(rows, inputs, weight, live):
    mid = weight.shape[1]

    def body(i, kind, given, fixed, made, totals):
        value = product(given[0][...], fixed[0][...])
        made[0][...] = value
        count = add_norm(i, kind, totals[0], value, fixed[1][...], 0)
        add_count(i, kind, totals[0], count)

    return rows.run(
        body,
        [inputs, weight, live],
        [(mid, FLOAT)],
        [(1, 2 * mid + LANES)],
        2 * rows.total() * weight.size,
        streamed=[0],
    )


def norm_kernel(crops, big, small, live, packed):
    channels = big.shape[1]
    weights = [None] + [live[low : low + ROWS, :] for low in range(0, crops, ROWS)]
    big_steps, small_steps = big.shape[0] // ROWS, small.shape[0] // crops

    def gather(value_of):
        def fold(value):
            return jnp.sum(value.reshape(-1, 8, channels), axis=0)

        def step(p, total):
            return total + fold(value_of(big[pl.ds(p * ROWS, ROWS), :]))

        total = lax.fori_loop(0, big_steps, step, jnp.zeros((8, channels), FLOAT), unroll=7)
        for k, weight in enumerate(weights[1:]):

            def step(p, part):
                return part + value_of(small[pl.ds(p * crops + k * ROWS, ROWS), :])

            part = lax.fori_loop(
                0, small_steps, step, jnp.zeros((ROWS, channels), FLOAT), unroll=True
            )
            total = total + fold(part * weight)
        return column_sum(total)

    count = big.shape[0] + small_steps * column_sum(live[:crops, :])
    mean = gather(lambda value: value) / count
    packed[:, :channels] = mean
    packed[:, channels : 2 * channels] = gather(lambda value: jnp.square(value - mean))
    packed[:, 2 * channels :] = jnp.broadcast_to(count, (1, LANES))


def norm_stage(rows, value, live):
    return call(
        lambda *refs: norm_kernel(rows.crops[1], *refs),
        shape((1, 2 * value[0].shape[1] + LANES)),
        [*value, live],
    )


def expand_stage(rows, second, scale, offset, weight, live):
    mid, wide = weight.shape

    def body(i, kind, given, fixed, made, totals):
        scale, offset, weight, live = fixed
        active = silu(given[0][...] * scale[...] + offset[...]).astype(HALF)
        made[1][...] = active
        for start in range(0, wide, CHUNK):
            columns = slice(start, start + CHUNK)
            value = product(active, weight[:, columns])
            made[0][:, columns] = value.astype(HALF)
            count = add_norm(i, kind, totals[0], value, live[...], start)
        add_count(i, kind, totals[0], count)

    return rows.run(
        body,
        [second, scale, offset, weight, live],
        [(wide, HALF, far_shape), (mid, HALF)],
        [(1, 2 * wide + LANES)],
        2 * rows.total() * weight.size,
    )


def pool_stage(rows, third, inputs, scale, offset):
    wide = scale.shape[1]

    def body(i, kind, given, fixed, made, totals):
        scale, offset = fixed
        steps, crops = rows.steps[kind], rows.crops[kind]
        step = i if kind == 0 else i - rows.steps[0]
        out = totals[kind]

        @pl.when(step == 0)
        def _():
            out[...] = jnp.zeros(out.shape, FLOAT)

        for start in range(0, wide, TILE):
            columns = slice(start, start + TILE)
            factor, shift = scale[:, columns], offset[:, columns]
            for low in range(0, crops, ROWS):
                total = out[low : low + ROWS, columns]
                for place in range(steps):
                    here = slice(place * crops + low, place * crops + low + ROWS)
                    residual = given[0][here, columns].astype(FLOAT) * factor + shift
                    residual = residual + given[1][here, columns].astype(FLOAT)
                    half = 0.5 * residual
                    total = total + (half * jnp.tanh(half) + half)
                out[low : low + ROWS, columns] = total

        @pl.when(step == steps - 1)
        def _():
            out[...] = out[...] * (1.0 / (steps * steps))

    return rows.run(
        body,
        [third, inputs, scale, offset],
        [],
        [(crops, wide) for crops in rows.crops],
        12 * rows.total() * wide,
        streamed=[0, 1],
    )


def residual_back_stage(rows, third, inputs, grads, scale, offset, mean, root, live, after):
    wide = scale.shape[1]

    def body(i, kind, given, fixed, made, totals):
        scale, offset, mean, root, live = fixed[2:]
        grads, crops = fixed[kind], rows.crops[kind]
        for start in range(0, wide, TILE):
            columns = slice(start, start + TILE)
            factor, shift, center = scale[:, columns], offset[:, columns], mean[:, columns]
            lows, highs = 0.0, 0.0
            for low in range(0, crops, ROWS):
                spread = grads[low : low + ROWS, columns]
                total, product_total = 0.0, 0.0
                for place in range(rows.steps[kind]):
                    here = slice(place * crops + low, place * crops + low + ROWS)
                    value = given[0][here, columns].astype(FLOAT)
                    residual = value * factor + shift + given[1][here, columns].astype(FLOAT)
                    grad = slope(residual) * spread
                    made[0][here, columns] = grad.astype(HALF)
                    total = total + grad
                    product_total = product_total + grad * (value - center)
                if kind == 1:
                    weight = live[low : low + ROWS, :]
                    total, product_total = total * weight, product_total * weight
                lows, highs = lows + column_sum(total), highs + column_sum(product_total)
            add_sums(i, kind, totals[0], lows, highs * root[:, columns], start)

    return rows.run(
        body,
        [third, inputs, *grads, scale, offset, mean, root, live],
        [(wide, HALF, far_shape)],
        [(1, 2 * wide + LANES)],
        16 * rows.total() * wide,
        after,
        streamed=[0, 1],
    )


def expand_back_stage(rows, grad, third, second, back, weight, norm, live, after):
    mid, wide = weight.shape

    def body(i, kind, given, fixed, made, totals):
        first, second, third, weight, scale, offset, mean, root, live = fixed
        total = jnp.zeros((rows.rows[kind], mid), FLOAT)
        for start in range(0, wide, CHUNK):
            columns = slice(start, start + CHUNK)
            value = (
                given[0][:, columns].astype(FLOAT) * first[:, columns]
                + given[1][:, columns].astype(FLOAT) * third[:, columns]
                + second[:, columns]
            )
            if kind == 1:
                value = value * live[...]
            value = value.astype(HALF)
            made[0][:, columns] = value
            total = total + product_outer(value, weight[:, columns])
        before = given[2][...]
        total = total * slope(before * scale[...] + offset[...])
        made[1][...] = total
        if kind == 1:
            total = total * live[...]
        high = column_sum(total * (before - mean[...])) * root[...]
        add_sums(i, kind, totals[0], column_sum(total), high, 0)

    return rows.run(
        body,
        [grad, third, second, *back, weight, *norm, live],
        [(wide, HALF, far_shape), (mid, FLOAT)],
        [(1, 2 * mid + LANES)],
        2 * rows.total() * weight.size,
        after,
        streamed=[0, 1],
    )


def slope_stage(rows, grad, value, norm, live):
    mid = grad[0].shape[1]

    def body(i, kind, given, fixed, made, totals):
        scale, offset, mean, root, live = fixed
        before = given[1][...]
        total = given[0][...] * slope(before * scale[...] + offset[...])
        made[0][...] = total
        if kind == 1:
            total = total * live[...]
        high = column_sum(total * (before - mean[...])) * root[...]
        add_sums(i, kind, totals[0], column_sum(total), high, 0)

    return rows.run(
        body,
        [grad, value, *norm, live],
        [(mid, FLOAT)],
        [(1, 2 * mid + LANES)],
        16 * rows.total() * mid,
    )


def norm_back_stage(rows, grad, value, back, live, after):
    mid = grad[0].shape[1]

    def body(i, kind, given, fixed, made, totals):
        first, second, third, live = fixed
        total = given[0][...] * first[...] + given[1][...] * third[...] + second[...]
        if kind == 1:
            total = total * live[...]
        made[0][...] = total.astype(HALF)

    return rows.run(
        body, [grad, value, *back, live], [(mid, HALF)], [], 6 * rows.total() * mid, after
    )[0]


def input_grad_stage(rows, grad, first, weight, after):
    wide, mid = weight.shape

    def body(i, kind, given, fixed, made, totals):
        first = given[1][...]
        for start in range(0, wide, CHUNK):
            columns = slice(start, start + CHUNK)
            value = product_outer(first, fixed[0][columns, :])
            made[0][:, columns] = (value + given[0][:, columns].astype(FLOAT)).astype(HALF)

    return rows.run(
        body,
        [grad, first, weight],
        [(wide, HALF, far_shape)],
        [],
        2 * rows.total() * weight.size,
        after,
        streamed=[0],
    )[0]


def hidden_kernel(big, small, weight, live, out, packed):
    j = pl.program_id(0)
    channels = (packed.shape[1] - LANES) // 2
    pooled = jnp.concatenate([big[...].astype(HALF), small[...].astype(HALF)])
    value = product(pooled, weight[...])
    out[...] = value
    count = column_sum(live[...])
    mean = column_sum(value * live[...]) / count
    spread = column_sum(jnp.square(value - mean) * live[...])
    packed[:, pl.ds(pl.multiple_of(j * CHUNK, CHUNK), CHUNK)] = mean
    packed[:, pl.ds(pl.multiple_of(channels + j * CHUNK, CHUNK), CHUNK)] = spread
    packed[:, 2 * channels :] = jnp.broadcast_to(count, (1, LANES))


def hidden_stage(big, small, weight, live):
    crops = live.shape[0]
    wide, channels = weight.shape
    return call(
        hidden_kernel,
        [shape((crops, channels)), shape((1, 2 * channels + LANES))],
        [big, small, weight, live],
        grid=(channels // CHUNK,),
        in_specs=[
            whole(big.shape),
            whole(small.shape),
            pl.BlockSpec((wide, CHUNK), lambda j: (0, j)),
            whole(live.shape),
        ],
        out_specs=[
            pl.BlockSpec((crops, CHUNK), lambda j: (0, j)),
            whole((1, 2 * channels + LANES)),
        ],
        flops=2 * crops * weight.size,
        streamed=[2],
    )


def lanes_of(dims):
    return lax.broadcasted_iota(jnp.int32, dims, 1)


def sums_by_view(batch, stored, views):
    row = lax.broadcasted_iota(jnp.int32, batch.shape, 0) % views
    size = stored.shape[0] // views
    return jnp.concatenate(
        [
            column_sum(jnp.where(row == v, batch, 0.0))
            + column_sum(stored[v * size : (v + 1) * size])
            for v in range(views)
        ],
        axis=1,
    )


def queue_kernel(proto, views, queue, prototypes, stored):
    rows = queue.shape[0] // views
    value = queue[...].astype(FLOAT)
    unit = value * lax.rsqrt(jnp.sum(value * value, axis=1, keepdims=True) + EPS_UNIT)
    scores = product_outer(unit.astype(HALF), prototypes[...])
    value = jnp.where(lanes_of(scores.shape) < proto, jnp.exp(scores / EPS_CODE), 0.0)
    size = stored.shape[0] // views
    stored[...] = jnp.zeros(stored.shape, FLOAT)
    for v in range(views):
        stored[v * size : v * size + rows, :] = value[v * rows : (v + 1) * rows]


def score_kernel(
    proto, views, big_rows, hidden, scale, offset, project, prototypes, stored,
    active_out, embedded_out, unit_out, scores_out, batch_out, sums,
):
    active = silu(hidden[...] * scale[...] + offset[...]).astype(HALF)
    active_out[...] = active
    embedded = product(active, project[...])
    embedded_out[...] = embedded
    root = lax.rsqrt(jnp.sum(embedded * embedded, axis=1, keepdims=True) + EPS_UNIT)
    unit = (embedded * root).astype(HALF)
    unit_out[...] = unit
    scores = product_outer(unit, prototypes[...])
    scores_out[...] = scores
    batch = scores[:big_rows]
    batch = jnp.where(lanes_of(batch.shape) < proto, jnp.exp(batch / EPS_CODE), 0.0)
    batch_out[...] = batch
    sums[...] = sums_by_view(batch, stored[...], views)


def balanced(proto, views, parts, batch, stored):
    totals = tree([part[...] for part in parts])
    width = batch.shape[1]
    totals = [totals[:, v * width : (v + 1) * width] for v in range(views)]
    totals = [jnp.where(lanes_of(t.shape) < proto, t, 1.0) for t in totals]
    row = lax.broadcasted_iota(jnp.int32, batch.shape, 0) % views
    own = jnp.zeros(batch.shape, FLOAT)
    for v in range(views):
        own = jnp.where(row == v, totals[v], own)
    batch = batch / own
    batch = batch / jnp.sum(batch, axis=1, keepdims=True)
    if stored is None:
        return batch, None
    size = stored.shape[0] // views
    stored = jnp.concatenate(
        [stored[v * size : (v + 1) * size] / totals[v] for v in range(views)]
    )
    sums = jnp.sum(stored, axis=1, keepdims=True)
    return batch, jnp.where(sums > 0.0, stored / jnp.where(sums > 0.0, sums, 1.0), 0.0)


def balance_kernel(proto, views, *refs):
    *parts, batch, stored, batch_out, stored_out, sums = refs
    batch, stored = balanced(proto, views, parts, batch[...], stored[...])
    batch_out[...] = batch
    stored_out[...] = stored
    sums[...] = sums_by_view(batch, stored, views)


def loss_kernel(proto, views, *refs):
    (
        *parts, batch, scores, share, live, embedded, hidden, scale, offset, mean, root, project, prototypes,
        grad_scores_out, grad_embedded_out, grad_out, packed,
    ) = refs
    codes, _ = balanced(proto, views, parts, batch[...], None)
    big = codes.shape[0]
    images = big // views
    slots = (scores.shape[0] - big) // images
    row = lax.broadcasted_iota(jnp.int32, codes.shape, 0) % views
    others = jnp.zeros(codes.shape, FLOAT)
    for turn in range(1, views):
        ahead = jnp.concatenate([codes[turn:], codes[:turn]])
        behind = jnp.concatenate([codes[turn - views :], codes[: turn - views]])
        others = others + jnp.where(row + turn < views, ahead, behind)
    both = codes + others
    targets = jnp.concatenate(
        [others]
        + [
            jnp.broadcast_to(both[k * views : k * views + 1], (slots, both.shape[1]))
            for k in range(images)
        ]
    )
    lanes = lanes_of(scores.shape)
    logits = jnp.where(lanes < proto, scores[...] / SOFTMAX_HEAT, -1e30)
    top = jnp.max(logits, axis=1, keepdims=True)
    powers = jnp.where(lanes < proto, jnp.exp(logits - top), 0.0)
    sums = jnp.sum(powers, axis=1, keepdims=True)
    logs = jnp.where(lanes < proto, logits - top - jnp.log(sums), 0.0)
    loss = -column_sum(jnp.sum(targets * logs, axis=1, keepdims=True) * share[...])
    mass = jnp.sum(targets, axis=1, keepdims=True)
    grad = (share[...] / SOFTMAX_HEAT) * (powers * (mass / sums) - targets)
    grad = grad.astype(HALF)
    grad_scores_out[...] = grad
    grad = product(grad, prototypes[...])
    value = embedded[...]
    scaled = lax.rsqrt(jnp.sum(value * value, axis=1, keepdims=True) + EPS_UNIT)
    unit = value * scaled
    grad = scaled * (grad - unit * jnp.sum(unit * grad, axis=1, keepdims=True))
    grad = grad.astype(HALF)
    grad_embedded_out[...] = grad
    channels = scale.shape[1]
    for start in range(0, channels, CHUNK):
        columns = slice(start, start + CHUNK)
        before = hidden[:, columns]
        part = product_outer(grad, project[columns, :])
        part = part * slope(before * scale[:, columns] + offset[:, columns])
        grad_out[:, columns] = part
        part = part * live[...]
        packed[:, columns] = column_sum(part)
        packed[:, channels + start : channels + start + CHUNK] = (
            column_sum(part * (before - mean[:, columns])) * root[:, columns]
        )
    packed[:, 2 * channels :] = jnp.broadcast_to(loss, (1, LANES))


def pooled_back_kernel(areas, big_rows, grad, hidden, live, first, second, third, weight, grad_out, big, small):
    value = grad[...] * first[...] + hidden[...] * third[...] + second[...]
    value = value * live[...]
    grad_out[...] = value
    part = product_outer(value.astype(HALF), weight[...])
    big[...] = part[:big_rows] / areas[0]
    small[...] = part[big_rows:] / areas[1]


def turn_kernel(blocks, big, small, out):
    value = jnp.concatenate([big[...], small[...]]).T
    rows = value.shape[0] // blocks
    planes = out.shape[0]
    for k in range(planes):
        parts = [value[j * rows : (j + 1) * rows] for j in range(k, blocks, planes)]
        out[k] = jnp.concatenate(parts).T


def hidden_grad_kernel(left, right, out):
    out[...] = product_inner(left[...].astype(HALF), right[...].astype(HALF))


def hidden_grad_stage(left, right, after):
    crops, height = left.shape
    width = right.shape[1]
    return call(
        hidden_grad_kernel,
        shape((height, width)),
        [left, right],
        grid=(width // CHUNK,),
        in_specs=[whole(left.shape), pl.BlockSpec((crops, CHUNK), lambda j: (0, j))],
        out_specs=pl.BlockSpec((height, CHUNK), lambda j: (0, j)),
        flops=2 * crops * height * width,
        streamed=[0, 1],
        after=after,
    )


def head_grad_kernel(devices, bits, active, grad_embedded, unit, grad_scores, keep, send):
    half = pick(bits, 0)
    project = product_inner(active[...], grad_embedded[...])
    proto = product_inner(unit[...], grad_scores[...])
    rows, lines = project.shape[0] // devices, proto.shape[0] // devices

    def store(k, here, columns, even, odd):
        keep[0, k, here, columns] = jnp.where(half == 0, even, odd)
        send[0, k, here, columns] = jnp.where(half == 0, odd, even)

    for k in range(devices // 2):
        pair = project[2 * k * rows : 2 * (k + 1) * rows]
        for part in range(2):
            start = part * rows // 2
            store(
                k,
                slice(0, rows // 2),
                slice(part * LANES, (part + 1) * LANES),
                pair[start : start + rows // 2],
                pair[rows + start : rows + start + rows // 2],
            )
        pair = proto[2 * k * lines : 2 * (k + 1) * lines]
        for part in range(proto.shape[1] // TILE):
            piece = pair[:, part * TILE : (part + 1) * TILE]
            start = rows // 2 + part * lines
            store(k, slice(start, start + lines), slice(0, TILE), piece[:lines], piece[lines:])


def head_grad_stage(active, grad_embedded, unit, grad_scores, devices, me, after):
    rows = active.shape[1] * grad_embedded.shape[1] + unit.shape[1] * grad_scores.shape[1]
    out = shape((1, devices // 2, rows // (devices * TILE), TILE))
    return call(
        lambda *refs: head_grad_kernel(devices, *refs),
        [out, out],
        [active, grad_embedded, unit, grad_scores],
        scalars=[me],
        after=after,
    )


def conv(field, weight):
    return lax.conv_general_dilated(
        field,
        weight,
        (1, 1),
        ((1, 1), (1, 1)),
        dimension_numbers=("HWNC", "HWIO", "HWNC"),
        preferred_element_type=FLOAT,
    )


def conv_back(field, weight):
    return lax.conv_general_dilated(
        field,
        lax.rev(weight, (0, 1)),
        (1, 1),
        ((1, 1), (1, 1)),
        dimension_numbers=("HWNC", "HWOI", "HWNC"),
        preferred_element_type=FLOAT,
    )


def conv_filter(field, grad):
    return lax.conv_general_dilated(
        field,
        grad,
        (1, 1),
        ((1, 1), (1, 1)),
        dimension_numbers=("HWCN", "HWIO", "HWNC"),
        preferred_element_type=FLOAT,
    )


def local(
    big_crops,
    small_crops,
    small_count,
    w_reduce,
    w_spatial,
    w_expand,
    gain_mid,
    bias_mid,
    gain_wide,
    bias_wide,
    w_hidden,
    gain_head,
    bias_head,
    w_project,
    prototypes,
    queue,
):
    devices = lax.axis_size("dp")
    image_rows = small_count.shape[0]
    images = image_rows * devices
    big_rows, big_side = big_crops.shape[:2]
    small_rows, small_side = small_crops.shape[:2]
    views = big_rows // image_rows
    slots = small_rows // image_rows
    wide = big_crops.shape[3]
    mid = w_reduce.shape[1]
    hid = w_hidden.shape[1]
    proj, proto = prototypes.shape
    proto_wide = -(-proto // CHUNK) * CHUNK
    crops = big_rows + small_rows
    areas = (big_side * big_side, small_side * small_side)
    rows = Rows(big_side, big_rows, small_side, small_rows)
    sides = ((big_side, big_side, big_rows), (small_side, small_side, small_rows))
    planes = [[k * PLANE + j for j in range(PLANE)] for k in range(devices // PLANE)]
    stacks = [[k * PLANE + j for k in range(devices // PLANE)] for j in range(PLANE)]
    me = lax.axis_index("dp").astype(jnp.int32).reshape(1)

    slot_mask = (jnp.arange(slots)[None, :] < small_count[:, None]).astype(FLOAT)
    slot_flags = slot_mask.reshape(-1)
    live = jnp.tile(slot_flags, small_side)[:, None]
    crop_live = jnp.concatenate([jnp.ones((big_rows,), FLOAT), slot_flags])[:, None]
    share = 1.0 / (images * views * (views - 1.0 + small_count.astype(FLOAT)))
    share = jnp.concatenate(
        [jnp.repeat(share, views), jnp.repeat(share, slots) * slot_flags]
    )[:, None]

    def fields(pair):
        return [a.reshape(*s, a.shape[-1]) for a, s in zip(pair, sides)]

    def flat(pair):
        return tuple(a.reshape(-1, a.shape[-1]) for a in pair)

    inputs = flat((jnp.transpose(big_crops, (1, 2, 0, 3)), jnp.transpose(small_crops, (1, 2, 0, 3))))
    taps = jnp.transpose(w_spatial, (1, 0, 2))
    filters = taps.reshape(3, 3, mid, mid)
    lines = jnp.pad(jnp.transpose(prototypes), ((0, proto_wide - proto), (0, 0)))

    first, packed = reduce_stage(rows, inputs, w_reduce, live)
    scale_one, offset_one, mean_one, root_one, pixel_count = settle_norm(
        packed, gain_mid[0], bias_mid[0], devices
    )
    mid_one = fields([silu(a * scale_one + offset_one).astype(HALF) for a in first])
    second = flat([conv(a, filters) for a in mid_one])
    packed = norm_stage(rows, second, live)
    scale_two, offset_two, mean_two, root_two, _ = settle_norm(
        packed, gain_mid[1], bias_mid[1], devices
    )
    third, mid_two, packed = expand_stage(rows, second, scale_two, offset_two, w_expand, live)
    scale_three, offset_three, mean_three, root_three, _ = settle_norm(
        packed, gain_wide, bias_wide, devices
    )
    pooled_big, pooled_small = pool_stage(rows, third, inputs, scale_three, offset_three)

    hidden, packed = hidden_stage(pooled_big, pooled_small, w_hidden, crop_live)
    scale_head, offset_head, mean_head, root_head, crop_count = settle_norm(
        packed, gain_head, bias_head, devices
    )
    stored_rows = views * (-(-queue.shape[1] // 8) * 8)
    stored = call(
        lambda *refs: queue_kernel(proto, views, *refs),
        shape((stored_rows, proto_wide)),
        [queue.reshape(-1, proj), lines],
    )
    active, embedded, unit, scores, batch, sums = call(
        lambda *refs: score_kernel(proto, views, big_rows, *refs),
        [
            shape((crops, hid), HALF),
            shape((crops, proj)),
            shape((crops, proj), HALF),
            shape((crops, proto_wide)),
            shape((big_rows, proto_wide)),
            shape((1, views * proto_wide)),
        ],
        [hidden, scale_head, offset_head, w_project, lines, stored],
    )
    for step in range(ITERS - 1):
        batch, stored, sums = call(
            lambda *refs: balance_kernel(proto, views, *refs),
            [shape(batch.shape), shape(stored.shape), shape(sums.shape)],
            [*sum_parts(sums, devices), batch, stored],
            )

    loss_outs = [
        shape((crops, proto_wide), HALF),
        shape((crops, proj), HALF),
        shape((crops, hid)),
        shape((1, 2 * hid + LANES)),
    ]
    parts = sum_parts(sums, devices)
    loss_args = [
        batch,
        scores,
        share,
        crop_live,
        embedded,
        hidden,
        scale_head,
        offset_head,
        mean_head,
        root_head,
        w_project,
        lines,
    ]
    grad_scores, grad_embedded, grad_active, packed = call(
        lambda *refs: loss_kernel(proto, views, *refs),
        loss_outs,
        [*parts, *loss_args],
        grid=(1,),
        in_specs=[whole(a.shape) for a in (*parts, *loss_args)],
        out_specs=[whole(a.shape) for a in loss_outs],
        streamed=range(len(parts), len(parts) + len(loss_args)),
    )
    made = {}

    def head_work(mark):
        made["head"] = head_grad_stage(
            active, grad_embedded, unit, grad_scores, devices, me, [mark]
        )
        return [made["head"][0]]

    *back, gain_head_grad, bias_head_grad, loss = settle_back(
        packed, gain_head, mean_head, root_head, crop_count, devices, [head_work]
    )
    head_sum = Scatter(*made["head"], devices, me)
    grad_hidden, *grad_pooled = call(
        lambda *refs: pooled_back_kernel(areas, big_rows, *refs),
        [shape((crops, hid)), shape((big_rows, wide)), shape((small_rows, wide))],
        [grad_active, hidden, crop_live, *back, w_hidden],
        grid=(wide // CHUNK,),
        in_specs=[
            whole((crops, hid)),
            whole((crops, hid)),
            whole((crops, 1)),
            whole((1, hid)),
            whole((1, hid)),
            whole((1, hid)),
            pl.BlockSpec((CHUNK, hid), lambda j: (j, 0)),
        ],
        out_specs=[
            whole((crops, hid)),
            pl.BlockSpec((big_rows, CHUNK), lambda j: (0, j)),
            pl.BlockSpec((small_rows, CHUNK), lambda j: (0, j)),
        ],
        flops=2 * crops * w_hidden.size,
        streamed=[6],
    )
    plane_grad = lax.all_gather(grad_hidden, "dp", axis_index_groups=planes, tiled=True)

    grad_residual, packed = residual_back_stage(
        rows,
        third,
        inputs,
        grad_pooled,
        scale_three,
        offset_three,
        mean_three,
        root_three,
        live,
        [head_sum.go()],
    )
    *back, gain_three, bias_three, _ = settle_back(
        packed, gain_wide, mean_three, root_three, pixel_count, devices
    )
    turned = call(
        lambda *refs: turn_kernel(devices, *refs),
        shape((PLANE, crops, wide // PLANE)),
        [pooled_big, pooled_small],
        after=[back[0]],
    )
    plane_pooled = lax.all_to_all(
        turned, "dp", 0, 0, axis_index_groups=planes, tiled=True
    ).reshape(PLANE * crops, wide // PLANE)
    grad_third, grad_two, packed = expand_back_stage(
        rows,
        grad_residual,
        third,
        second,
        back,
        w_expand,
        [scale_two, offset_two, mean_two, root_two],
        live,
        [turned],
    )
    packed = tie(packed, [plane_pooled])

    def expand_work(mark):
        made["expand"] = weight_grad(mid_two, grad_third, devices, me, 1, [mark], [1, 3])
        return [made["expand"][0]]

    def hidden_work(mark):
        made["hidden"] = hidden_grad_stage(plane_pooled, plane_grad, [mark])
        return [made["hidden"]]

    *back, gain_two, bias_two, _ = settle_back(
        packed,
        gain_mid[1],
        mean_two,
        root_two,
        pixel_count,
        devices,
        [expand_work, hidden_work],
    )
    expand_sum = Scatter(*made["expand"], devices, me)
    hidden_grad = lax.psum_scatter(
        made["hidden"], "dp", scatter_dimension=0, axis_index_groups=stacks, tiled=True
    )
    grad_second = norm_back_stage(
        rows, grad_two, second, back, live, [expand_sum.go([back[0]]), head_sum.go([back[0]])]
    )
    grad_mid_one = flat([conv_back(a, filters) for a in fields(grad_second)])
    grad_one, packed = slope_stage(
        rows, grad_mid_one, first, [scale_one, offset_one, mean_one, root_one], live
    )

    def big_work(mark):
        grad = tie(grad_second[0], [mark])
        made["big"] = conv_filter(mid_one[0], fields((grad, grad_second[1]))[0])
        return [made["big"]]

    def small_work(mark):
        grad = tie(grad_second[1], [mark])
        part = made["big"] + conv_filter(mid_one[1], fields((grad_second[0], grad))[1])
        made["spatial"] = part.reshape(9, devices, mid // devices, mid)
        return [made["spatial"]]

    *back, gain_one, bias_one, _ = settle_back(
        packed,
        gain_mid[0],
        mean_one,
        root_one,
        pixel_count,
        devices,
        [big_work, small_work],
    )
    spatial_send = send_rows(made["spatial"], me, [back[0]])
    spatial_sum = Scatter(made["spatial"], spatial_send, devices, me)
    mark = expand_sum.go([back[0]])
    grad_first = norm_back_stage(rows, grad_one, first, back, live, [mark])
    reduce_keep, reduce_send = weight_grad(
        inputs, grad_first, devices, me, 0, [spatial_send], [0, 2]
    )
    reduce_sum = Scatter(reduce_keep, reduce_send, devices, me)
    mark = spatial_sum.go([reduce_keep])
    mark = reduce_sum.go([mark])
    grad_inputs = input_grad_stage(rows, grad_residual, grad_first, w_reduce, [mark])
    grad_big, grad_small = fields(grad_inputs)
    mark = grad_inputs[0]
    order = (expand_sum, spatial_sum, reduce_sum, head_sum, spatial_sum, reduce_sum, expand_sum)
    for part in order + (spatial_sum, reduce_sum, head_sum) * 2:
        if not part.complete():
            mark = part.go([mark])
    head_grad = head_sum.end()[0]
    ends = w_project.shape[0] // (2 * devices)
    project_grad = jnp.concatenate([head_grad[:ends, :LANES], head_grad[:ends, LANES:]])
    proto_grad = head_grad[ends:].reshape(-1, proj // devices, TILE)
    proto_grad = jnp.transpose(proto_grad, (1, 0, 2)).reshape(proj // devices, -1)[:, :proto]
    expand_grad = expand_sum.end()[0]
    spatial_grad = spatial_sum.end()
    reduce_grad = reduce_sum.end()[0]
    return (
        loss[0, 0],
        jnp.transpose(grad_big, (2, 0, 1, 3)),
        jnp.transpose(grad_small, (2, 0, 1, 3)),
        reduce_grad,
        jnp.transpose(spatial_grad, (1, 0, 2)),
        expand_grad,
        jnp.concatenate([gain_one, gain_two]),
        jnp.concatenate([bias_one, bias_two]),
        gain_three[0],
        bias_three[0],
        hidden_grad,
        gain_head_grad[0],
        bias_head_grad[0],
        project_grad,
        proto_grad,
    )


def solution(mesh):
    placed = (
        P("dp", None, None, None),
        P("dp", None, None, None),
        P("dp"),
        P(),
        P(),
        P(),
        P(),
        P(),
        P(),
        P(),
        P(),
        P(),
        P(),
        P(),
        P(),
        P(None, "dp", None),
    )
    return jax.shard_map(
        local,
        mesh=mesh,
        in_specs=placed,
        out_specs=(
            P(),
            P("dp", None, None, None),
            P("dp", None, None, None),
            P("dp", None),
            P("dp", None, None),
            P("dp", None),
            P(),
            P(),
            P(),
            P(),
            P("dp", None),
            P(),
            P(),
            P("dp", None),
            P("dp", None),
        ),
        check_vma=False,
    )
```

```python
import math

import jax
import jax.numpy as jnp
from jax import lax
from jax.experimental import pallas as pl
from jax.experimental.pallas import tpu as pltpu
from jax.sharding import PartitionSpec as P

ITERS = 3

EPS_NORM = 1e-05
EPS_UNIT = 1e-06
EPS_CODE = 0.05
SOFTMAX_HEAT = 0.1
LANES = 128
PLANE = 8
CHUNK = 512
TILE = 256
ROWS = 32
VMEM_LIMIT = 60 << 20
GRID_LIMIT = 16 << 20
SLOTS = 3
FLOAT = jnp.float32
HALF = jnp.bfloat16


def product(left, right):
    return jnp.dot(left, right, preferred_element_type=FLOAT)


def product_inner(left, right):
    return lax.dot_general(left, right, (((0,), (0,)), ((), ())), preferred_element_type=FLOAT)


def product_outer(left, right):
    return lax.dot_general(left, right, (((1,), (1,)), ((), ())), preferred_element_type=FLOAT)


def sigmoid(value):
    return 0.5 * jnp.tanh(0.5 * value) + 0.5


def silu(value):
    return value * sigmoid(value)


def slope(value):
    gate = sigmoid(value)
    return gate * (1.0 + value * (1.0 - gate))


def column_sum(value):
    return jnp.sum(value, axis=0, keepdims=True)


def shape(dims, dtype=FLOAT):
    return jax.ShapeDtypeStruct(dims, dtype)


def far_shape(dims, dtype=FLOAT):
    return pltpu.HBM(dims, dtype)


def far(array):
    return pltpu.with_memory_space_constraint(array, pltpu.HBM)


def whole(dims):
    return pl.BlockSpec(dims, lambda *_: (0,) * len(dims))


class Far:
    def __init__(self, array):
        self.array = array


def call(
    kernel,
    out_shape,
    args,
    grid=None,
    in_specs=None,
    out_specs=None,
    flops=0,
    after=(),
    scalars=(),
    streamed=(),
    scratch=(),
):
    flat = out_shape if isinstance(out_shape, (list, tuple)) else [out_shape]
    size = sum(a.size * a.dtype.itemsize for a in args)
    size += sum(math.prod(a.shape) * jnp.dtype(a.dtype).itemsize for a in flat)
    args = [far(a) if k in streamed else a for k, a in enumerate(args)]
    here = pl.BlockSpec(memory_space=pltpu.VMEM)
    limit = 0
    if grid is None:
        in_specs = [here] * len(args)
        out_specs = jax.tree.map(lambda _: here, out_shape)
        limit = max(limit, size + size // 4 + (2 << 20))
    else:
        limit = GRID_LIMIT + sum(
            math.prod(a.shape) * jnp.dtype(a.dtype).itemsize for a in scratch[:-1]
        )
    limit += sum(a.size * a.dtype.itemsize for a in after if not isinstance(a, Far))
    first, last = len(scalars), len(scalars) + len(args)

    def run(*refs):
        kernel(*refs[:last], *refs[last + len(after) :])

    specs = dict(out_specs=out_specs)
    if grid is not None:
        specs["grid"] = grid
    return pl.pallas_call(
        run,
        out_shape=out_shape,
        in_specs=[pl.BlockSpec(memory_space=pltpu.SMEM)] * first
        + list(in_specs)
        + [pl.BlockSpec(memory_space=pl.ANY if isinstance(a, Far) else pltpu.VMEM) for a in after],
        scratch_shapes=list(scratch),
        compiler_params=pltpu.CompilerParams(vmem_limit_bytes=min(limit, VMEM_LIMIT)),
        cost_estimate=pl.CostEstimate(flops=flops, bytes_accessed=size, transcendentals=0),
        **specs,
    )(*scalars, *args, *(a.array if isinstance(a, Far) else a for a in after))


def copy_kernel(source, out):
    out[...] = source[...]


def tie(value, after):
    return call(copy_kernel, shape(value.shape, value.dtype), [value], after=after)


def rounds(devices):
    bits = [1 << k for k in range(devices.bit_length() - 1)]
    return [bits[:1]] + [bits[k : k + 2] for k in range(1, len(bits), 2)]


def peers(value, bits, devices):
    masks = [0]
    for bit in bits:
        masks = masks + [mask | bit for mask in masks]
    return [value] + [
        lax.ppermute(value, "dp", [(i, i ^ mask) for i in range(devices)]) for mask in masks[1:]
    ]


def tree(values):
    while len(values) > 1:
        values = [values[k] + values[k + 1] for k in range(0, len(values), 2)]
    return values[0]


def exchange(value, devices, merge, works=()):
    first, *others = rounds(devices)
    parts = peers(value, first, devices)
    for k, bits in enumerate(others):
        value = merge(parts)
        parts = peers(value, bits, devices)
        if k < len(works):
            parts[0] = tie(value, works[k](value))
    return parts


def sum_parts(value, devices, works=()):
    return exchange(value, devices, tree, works)


def merged(parts):
    channels = (parts[0].shape[1] - LANES) // 2
    counts = [part[:, 2 * channels : 2 * channels + 1] for part in parts]
    means = [part[:, :channels] for part in parts]
    spreads = [part[:, channels : 2 * channels] for part in parts]
    total = tree(counts)
    mean = tree([c * m for c, m in zip(counts, means)]) / total
    spread = tree([s + c * jnp.square(m - mean) for s, c, m in zip(spreads, counts, means)])
    return total, mean, spread


def merge_kernel(*refs):
    *parts, out = refs
    channels = (out.shape[1] - LANES) // 2
    total, mean, spread = merged([part[...] for part in parts])
    out[:, :channels] = mean
    out[:, channels : 2 * channels] = spread
    out[:, 2 * channels :] = jnp.broadcast_to(total, (1, LANES))


def merge_norms(parts):
    return call(merge_kernel, shape(parts[0].shape), parts)


def settle_kernel(*refs):
    *parts, gain, bias, scale, offset, mean_out, root_out, count = refs
    total, mean, spread = merged([part[...] for part in parts])
    root = lax.rsqrt(spread / total + EPS_NORM)
    factor = gain[...] * root
    scale[...] = factor
    offset[...] = bias[...] - mean * factor
    mean_out[...] = mean
    root_out[...] = root
    count[...] = jnp.broadcast_to(total, (1, LANES))


def settle_norm(packed, gain, bias, devices):
    channels = gain.shape[0]
    parts = exchange(packed, devices, merge_norms)
    row = shape((1, channels))
    return call(
        settle_kernel,
        [row, row, row, row, shape((1, LANES))],
        [*parts, gain[None], bias[None]],
    )


def settle_back_kernel(*refs):
    *parts, gain, mean, root, count, first, second, third, gain_sum, bias_sum, extra = refs
    channels = gain.shape[1]
    packed = tree([part[...] for part in parts])
    total = count[:, :1]
    low, high = packed[:, :channels], packed[:, channels : 2 * channels]
    factor = gain[...] * root[...]
    pull = root[...] * high / total
    first[...] = factor
    second[...] = factor * (mean[...] * pull - low / total)
    third[...] = -factor * pull
    gain_sum[...] = high
    bias_sum[...] = low
    extra[...] = packed[:, 2 * channels :]


def settle_back(packed, gain, mean, root, count, devices, works=()):
    parts = sum_parts(packed, devices, works)
    row = shape((1, gain.shape[0]))
    return call(
        settle_back_kernel,
        [row, row, row, row, row, shape((1, LANES))],
        [*parts, gain[None], mean, root, count],
    )


def pick(bits, place):
    return (bits[0] >> place) & 1


def send_kernel(bits, value, send):
    other = 1 - pick(bits, 0)

    def step(t, _):
        for k in range(send.shape[1]):
            send[t, k] = value[t, 2 * k + other]
        return _

    lax.fori_loop(0, value.shape[0], step, 0)


def send_rows(value, me, after):
    taps, devices, rows, width = value.shape
    out = shape((taps, devices // 2, rows, width))
    return call(send_kernel, out, [value], scalars=[me], after=after)


def first_kernel(bits, keep, got, keep_one, send_one, keep_two, send_two):
    taps, blocks, _, width = got.shape
    uncut = keep.shape[1] // blocks
    half = pick(bits, 0) * (uncut - 1)
    left, right = slice(0, width // 2), slice(width // 2, width)
    one, two = pick(bits, 1), pick(bits, 2)

    def step(t, _):
        for k in range(blocks // 2):
            for out, there in ((keep_one, 2 * k + one), (send_one, 2 * k + 1 - one)):
                out[t, k] = keep[t, uncut * there + half, :, left] + got[t, there, :, left]
            low = 4 * (k // 2) + k % 2
            for out, there in ((keep_two, low + 2 * two), (send_two, low + 2 * (1 - two))):
                out[t, k] = keep[t, uncut * there + half, :, right] + got[t, there, :, right]
        return _

    lax.fori_loop(0, taps, step, 0)


def second_kernel(bits, keep_one, got_one, keep_two, got_two, *outs):
    def step(t, _):
        for keep, got, place, out_keep, out_send in (
            (keep_one, got_one, 2, outs[0], outs[1]),
            (keep_two, got_two, 1, outs[2], outs[3]),
        ):
            half = pick(bits, place)
            for k in range(out_keep.shape[1]):
                out_keep[t, k] = keep[t, 2 * k + half] + got[t, 2 * k + half]
                out_send[t, k] = keep[t, 2 * k + 1 - half] + got[t, 2 * k + 1 - half]
        return _

    lax.fori_loop(0, keep_one.shape[0], step, 0)


def third_kernel(bits, keep_one, got_one, keep_two, got_two, out_keep, out_send):
    half = pick(bits, 3)
    width = keep_one.shape[3]

    def step(t, _):
        for k in range(out_keep.shape[1]):
            for out, there in ((out_keep, 2 * k + half), (out_send, 2 * k + 1 - half)):
                out[t, k, :, :width] = keep_one[t, there] + got_one[t, there]
                out[t, k, :, width:] = keep_two[t, there] + got_two[t, there]
        return _

    lax.fori_loop(0, keep_one.shape[0], step, 0)


def later_kernel(place, bits, keep, got, out_keep, out_send):
    half = pick(bits, place)

    def step(t, _):
        for k in range(out_keep.shape[1]):
            for out, there in ((out_keep, 2 * k + half), (out_send, 2 * k + 1 - half)):
                out[t, k] = keep[t, there] + got[t, there]
        return _

    lax.fori_loop(0, keep.shape[0], step, 0)


def last_kernel(keep, got, out):
    out[...] = keep[...] + got[...]


class Scatter:
    def __init__(self, keep, send, devices, me):
        self.devices, self.me = devices, me
        self.bits = devices.bit_length() - 1
        self.held = [keep]
        self.got = [self.cross(send, 0)]
        self.stage = 0

    def cross(self, value, place):
        return lax.ppermute(
            value, "dp", [(i, i ^ (1 << place)) for i in range(self.devices)]
        )

    def go(self, after=()):
        taps, blocks, rows, width = self.got[0].shape
        if self.stage == 0:
            out = shape((taps, blocks // 2, rows, width // 2))
            kernel, places = first_kernel, (1, 2)
        elif self.stage == 1:
            out = shape((taps, blocks // 2, rows, width))
            kernel, places = second_kernel, (2, 1)
        elif self.stage == 2:
            out = shape((taps, blocks // 2, rows, 2 * width))
            kernel, places = third_kernel, (3,)
        else:
            place = self.stage + 1
            out = shape((taps, blocks // 2, rows, width))
            kernel, places = (lambda *refs: later_kernel(place, *refs)), (place,)
        args = [a for pair in zip(self.held, self.got) for a in pair]
        made = call(kernel, [out] * (2 * len(places)), args, after=after, scalars=[self.me])
        self.held = list(made[::2])
        self.got = [self.cross(send, place) for send, place in zip(made[1::2], places)]
        self.stage += 1
        return self.held[0]

    def complete(self):
        return self.got[0].shape[1] == 1

    def end(self):
        while not self.complete():
            self.go()
        taps, _, rows, width = self.held[0].shape
        done = call(last_kernel, shape(self.held[0].shape), [self.held[0], self.got[0]])
        return done.reshape(taps, rows, width)


def weight_grad_kernel(rows, bits, left_big, right_big, left_small, right_small, keep, send):
    value = product_inner(left_big[...], right_big[...])
    value = value + product_inner(left_small[...], right_small[...])
    half = pick(bits, 0)
    for k in range(value.shape[0] // (2 * rows)):
        even = value[2 * k * rows : (2 * k + 1) * rows]
        odd = value[(2 * k + 1) * rows : (2 * k + 2) * rows]
        keep[0, k] = jnp.where(half == 0, even, odd)
        send[0, k] = jnp.where(half == 0, odd, even)


def weight_grad(left, right, devices, me, along, after=(), streamed=()):
    height, width = left[0].shape[1], right[0].shape[1]
    rows = height // devices
    out = shape((1, devices // 2, rows, width))

    def spec(pair, k, moves):
        dims = (pair[k].shape[0], CHUNK if moves else pair[k].shape[1])
        return pl.BlockSpec(dims, lambda j: (0, j if moves else 0))

    if along == 0:
        steps = height // CHUNK
        block = pl.BlockSpec((1, devices // 2 // steps, rows, width), lambda j: (0, j, 0, 0))
    else:
        steps = width // CHUNK
        block = pl.BlockSpec((1, devices // 2, rows, CHUNK), lambda j: (0, 0, 0, j))
    return call(
        lambda *refs: weight_grad_kernel(rows, *refs),
        [out, out],
        [left[0], right[0], left[1], right[1]],
        grid=(steps,),
        in_specs=[
            spec(left, 0, along == 0),
            spec(right, 0, along == 1),
            spec(left, 1, along == 0),
            spec(right, 1, along == 1),
        ],
        out_specs=[block, block],
        flops=2 * (left[0].shape[0] + left[1].shape[0]) * height * width,
        after=after,
        streamed=streamed,
        scalars=[me],
    )


class Rows:
    def __init__(self, big_side, big_crops, small_side, small_crops):
        self.steps = big_side, small_side
        self.rows = big_side * big_crops, small_side * small_crops
        self.crops = big_crops, small_crops

    def specs(self, channels):
        first = self.steps[0]
        return [
            pl.BlockSpec((self.rows[0], channels), lambda i: (jnp.minimum(i, first - 1), 0)),
            pl.BlockSpec((self.rows[1], channels), lambda i: (jnp.maximum(i - first, 0), 0)),
        ]

    def shapes(self, channels, dtype, place=shape):
        return [place((s * r, channels), dtype) for s, r in zip(self.steps, self.rows)]

    def run(self, body, args, row_outs, whole_outs, flops, after=(), streamed=()):
        pairs = [a for a in args if isinstance(a, tuple)]
        rest = [a for a in args if not isinstance(a, tuple)]
        in_specs, flat = [], []
        scratch = []
        for k, pair in enumerate(pairs):
            flat += list(pair)
            if k in streamed:
                in_specs += [pl.BlockSpec(memory_space=pl.ANY)] * 2
                scratch += [
                    pltpu.VMEM((SLOTS, rows, pair[0].shape[1]), pair[0].dtype)
                    for rows in self.rows
                ]
            else:
                in_specs += self.specs(pair[0].shape[1])
        if streamed:
            scratch.append(pltpu.SemaphoreType.DMA((2 * len(streamed), SLOTS)))
        in_specs += [whole(a.shape) for a in rest]
        out_shapes, out_specs = [], []
        for channels, dtype, *place in row_outs:
            out_shapes += self.shapes(channels, dtype, *place)
            out_specs += self.specs(channels)
        out_shapes += [shape(dims) for dims in whole_outs]
        out_specs += [whole(dims) for dims in whole_outs]
        n_in, n_rest, n_out = len(pairs), len(rest), len(row_outs)

        def kernel(*refs):
            i = pl.program_id(0)
            refs, held = refs[: len(refs) - len(scratch)], refs[len(refs) - len(scratch) :]
            given, fixed = refs[: 2 * n_in], refs[2 * n_in : 2 * n_in + n_rest]
            made = refs[2 * n_in + n_rest :]

            def fetch(kind, step, slot):
                start = step * self.rows[kind]
                if not isinstance(step, int):
                    start = pl.multiple_of(start, self.rows[kind])
                return [
                    pltpu.make_async_copy(
                        given[2 * k + kind].at[pl.ds(start, self.rows[kind]), :],
                        held[2 * n + kind].at[slot],
                        held[-1].at[2 * n + kind, slot],
                    )
                    for n, k in enumerate(streamed)
                ]

            def start_big(step):
                for copy in fetch(0, step, lax.rem(step, SLOTS)):
                    copy.start()

            if streamed:

                @pl.when(i == 0)
                def _():
                    for step in range(SLOTS - 1):
                        for copy in fetch(0, step, step):
                            copy.start()

                pl.when(i + SLOTS - 1 < self.steps[0])(lambda: start_big(i + SLOTS - 1))
                for step in range(self.steps[1]):

                    @pl.when(i == self.steps[0] - self.steps[1] + step)
                    def _(step=step):
                        for copy in fetch(1, step, step):
                            copy.start()

            for kind in range(2):
                here = i < self.steps[0] if kind == 0 else i >= self.steps[0]

                @pl.when(here)
                def _(kind=kind):
                    blocks = list(given[kind : 2 * n_in : 2])
                    if streamed:
                        step = i if kind == 0 else i - self.steps[0]
                        slot = lax.rem(step, SLOTS)
                        for copy in fetch(kind, step, slot):
                            copy.wait()
                        for n, k in enumerate(streamed):
                            blocks[k] = held[2 * n + kind].at[slot]
                    body(i, kind, blocks, fixed, made[kind : 2 * n_out : 2], made[2 * n_out :])

        made = call(
            kernel,
            out_shapes,
            flat + rest,
            grid=(sum(self.steps),),
            in_specs=in_specs,
            out_specs=out_specs,
            flops=flops,
            after=after,
            streamed=[2 * k + j for k in streamed for j in range(2)],
            scratch=scratch,
        )
        return [tuple(made[2 * k : 2 * k + 2]) for k in range(n_out)] + list(made[2 * n_out :])

    def total(self):
        return sum(s * r for s, r in zip(self.steps, self.rows))


def add_norm(i, kind, packed, value, weight, start):
    channels = (packed.shape[1] - LANES) // 2
    width = value.shape[1]
    here = slice(start, start + width)
    there = slice(channels + start, channels + start + width)
    rows = value.shape[0]
    count = jnp.full((1, 1), rows, FLOAT) if kind == 0 else column_sum(weight)
    pivot = column_sum(value[:ROWS]) * (1.0 / ROWS)
    means, spreads = [], []
    for left in range(0, width, TILE):
        center = pivot[:, left : left + TILE]
        total, squares = 0.0, 0.0
        for low in range(0, rows, ROWS):
            apart = value[low : low + ROWS, left : left + TILE] - center
            weighted = apart if kind == 0 else apart * weight[low : low + ROWS]
            total = total + weighted
            squares = squares + weighted * apart
        total = column_sum(total) / count
        means.append(center + total)
        spreads.append(column_sum(squares) - count * jnp.square(total))
    mean, spread = jnp.concatenate(means, axis=1), jnp.concatenate(spreads, axis=1)

    before = packed[:, 2 * channels : 2 * channels + 1]
    part = count / (before + count)
    old = packed[:, here]
    delta = mean - old
    new_mean = old + delta * part
    new_spread = packed[:, there] + spread + jnp.square(delta) * (before * part)
    if kind == 0:
        new_mean = jnp.where(i == 0, mean, new_mean)
        new_spread = jnp.where(i == 0, spread, new_spread)
    packed[:, here] = new_mean
    packed[:, there] = new_spread
    return count


def add_count(i, kind, packed, count):
    channels = (packed.shape[1] - LANES) // 2
    lanes = slice(2 * channels, 2 * channels + LANES)
    wide_count = jnp.broadcast_to(count, (1, LANES))

    total = packed[:, lanes] + wide_count
    packed[:, lanes] = jnp.where(i == 0, wide_count, total) if kind == 0 else total


def add_sums(i, kind, packed, low, high, start):
    channels = (packed.shape[1] - LANES) // 2
    width = low.shape[1]
    here = slice(start, start + width)
    there = slice(channels + start, channels + start + width)

    new_low, new_high = packed[:, here] + low, packed[:, there] + high
    if kind == 0:
        new_low = jnp.where(i == 0, low, new_low)
        new_high = jnp.where(i == 0, high, new_high)
    packed[:, here] = new_low
    packed[:, there] = new_high
    if start == 0:
        packed[:, 2 * channels :] = jnp.zeros((1, LANES), FLOAT)


def reduce_stage(rows, inputs, weight, live):
    mid = weight.shape[1]

    def body(i, kind, given, fixed, made, totals):
        value = product(given[0][...], fixed[0][...])
        made[0][...] = value
        count = add_norm(i, kind, totals[0], value, fixed[1][...], 0)
        add_count(i, kind, totals[0], count)

    return rows.run(
        body,
        [inputs, weight, live],
        [(mid, FLOAT)],
        [(1, 2 * mid + LANES)],
        2 * rows.total() * weight.size,
        streamed=[0],
    )


def norm_kernel(crops, big, small, live, packed):
    channels = big.shape[1]
    weights = [None] + [live[low : low + ROWS, :] for low in range(0, crops, ROWS)]
    big_steps, small_steps = big.shape[0] // ROWS, small.shape[0] // crops

    def gather(value_of):
        def fold(value):
            return jnp.sum(value.reshape(-1, 8, channels), axis=0)

        def step(p, total):
            return total + fold(value_of(big[pl.ds(p * ROWS, ROWS), :]))

        total = lax.fori_loop(0, big_steps, step, jnp.zeros((8, channels), FLOAT), unroll=7)
        for k, weight in enumerate(weights[1:]):

            def step(p, part):
                return part + value_of(small[pl.ds(p * crops + k * ROWS, ROWS), :])

            part = lax.fori_loop(
                0, small_steps, step, jnp.zeros((ROWS, channels), FLOAT), unroll=True
            )
            total = total + fold(part * weight)
        return column_sum(total)

    count = big.shape[0] + small_steps * column_sum(live[:crops, :])
    mean = gather(lambda value: value) / count
    packed[:, :channels] = mean
    packed[:, channels : 2 * channels] = gather(lambda value: jnp.square(value - mean))
    packed[:, 2 * channels :] = jnp.broadcast_to(count, (1, LANES))


def norm_stage(rows, value, live):
    return call(
        lambda *refs: norm_kernel(rows.crops[1], *refs),
        shape((1, 2 * value[0].shape[1] + LANES)),
        [*value, live],
    )


def expand_stage(rows, second, scale, offset, weight, live):
    mid, wide = weight.shape

    def body(i, kind, given, fixed, made, totals):
        scale, offset, weight, live = fixed
        active = silu(given[0][...] * scale[...] + offset[...]).astype(HALF)
        made[1][...] = active
        for start in range(0, wide, CHUNK):
            columns = slice(start, start + CHUNK)
            value = product(active, weight[:, columns])
            made[0][:, columns] = value.astype(HALF)
            count = add_norm(i, kind, totals[0], value, live[...], start)
        add_count(i, kind, totals[0], count)

    return rows.run(
        body,
        [second, scale, offset, weight, live],
        [(wide, HALF, far_shape), (mid, HALF)],
        [(1, 2 * wide + LANES)],
        2 * rows.total() * weight.size,
    )


def pool_stage(rows, third, inputs, scale, offset):
    wide = scale.shape[1]

    def body(i, kind, given, fixed, made, totals):
        scale, offset = fixed
        steps, crops = rows.steps[kind], rows.crops[kind]
        step = i if kind == 0 else i - rows.steps[0]
        out = totals[kind]

        @pl.when(step == 0)
        def _():
            out[...] = jnp.zeros(out.shape, FLOAT)

        for start in range(0, wide, TILE):
            columns = slice(start, start + TILE)
            factor, shift = scale[:, columns], offset[:, columns]
            for low in range(0, crops, ROWS):
                total = out[low : low + ROWS, columns]
                for place in range(steps):
                    here = slice(place * crops + low, place * crops + low + ROWS)
                    residual = given[0][here, columns].astype(FLOAT) * factor + shift
                    residual = residual + given[1][here, columns].astype(FLOAT)
                    half = 0.5 * residual
                    total = total + (half * jnp.tanh(half) + half)
                out[low : low + ROWS, columns] = total

        @pl.when(step == steps - 1)
        def _():
            out[...] = out[...] * (1.0 / (steps * steps))

    return rows.run(
        body,
        [third, inputs, scale, offset],
        [],
        [(crops, wide) for crops in rows.crops],
        12 * rows.total() * wide,
        streamed=[0, 1],
    )


def residual_back_stage(rows, third, inputs, grads, scale, offset, mean, root, live, after):
    wide = scale.shape[1]

    def body(i, kind, given, fixed, made, totals):
        scale, offset, mean, root, live = fixed[2:]
        grads, crops = fixed[kind], rows.crops[kind]
        for start in range(0, wide, TILE):
            columns = slice(start, start + TILE)
            factor, shift, center = scale[:, columns], offset[:, columns], mean[:, columns]
            lows, highs = 0.0, 0.0
            for low in range(0, crops, ROWS):
                spread = grads[low : low + ROWS, columns]
                total, product_total = 0.0, 0.0
                for place in range(rows.steps[kind]):
                    here = slice(place * crops + low, place * crops + low + ROWS)
                    value = given[0][here, columns].astype(FLOAT)
                    residual = value * factor + shift + given[1][here, columns].astype(FLOAT)
                    grad = slope(residual) * spread
                    made[0][here, columns] = grad.astype(HALF)
                    total = total + grad
                    product_total = product_total + grad * (value - center)
                if kind == 1:
                    weight = live[low : low + ROWS, :]
                    total, product_total = total * weight, product_total * weight
                lows, highs = lows + column_sum(total), highs + column_sum(product_total)
            add_sums(i, kind, totals[0], lows, highs * root[:, columns], start)

    return rows.run(
        body,
        [third, inputs, *grads, scale, offset, mean, root, live],
        [(wide, HALF, far_shape)],
        [(1, 2 * wide + LANES)],
        16 * rows.total() * wide,
        after,
        streamed=[0, 1],
    )


def expand_back_stage(rows, grad, third, second, back, weight, norm, live, after):
    mid, wide = weight.shape

    def body(i, kind, given, fixed, made, totals):
        first, second, third, weight, scale, offset, mean, root, live = fixed
        total = jnp.zeros((rows.rows[kind], mid), FLOAT)
        for start in range(0, wide, CHUNK):
            columns = slice(start, start + CHUNK)
            value = (
                given[0][:, columns].astype(FLOAT) * first[:, columns]
                + given[1][:, columns].astype(FLOAT) * third[:, columns]
                + second[:, columns]
            )
            if kind == 1:
                value = value * live[...]
            value = value.astype(HALF)
            made[0][:, columns] = value
            total = total + product_outer(value, weight[:, columns])
        before = given[2][...]
        total = total * slope(before * scale[...] + offset[...])
        made[1][...] = total
        if kind == 1:
            total = total * live[...]
        high = column_sum(total * (before - mean[...])) * root[...]
        add_sums(i, kind, totals[0], column_sum(total), high, 0)

    return rows.run(
        body,
        [grad, third, second, *back, weight, *norm, live],
        [(wide, HALF, far_shape), (mid, FLOAT)],
        [(1, 2 * mid + LANES)],
        2 * rows.total() * weight.size,
        after,
        streamed=[0, 1],
    )


def slope_stage(rows, grad, value, norm, live, after):
    mid = grad[0].shape[1]

    def body(i, kind, given, fixed, made, totals):
        scale, offset, mean, root, live = fixed
        before = given[1][...]
        total = given[0][...] * slope(before * scale[...] + offset[...])
        made[0][...] = total
        if kind == 1:
            total = total * live[...]
        high = column_sum(total * (before - mean[...])) * root[...]
        add_sums(i, kind, totals[0], column_sum(total), high, 0)

    return rows.run(
        body,
        [grad, value, *norm, live],
        [(mid, FLOAT)],
        [(1, 2 * mid + LANES)],
        16 * rows.total() * mid,
        after,
    )


def norm_back_stage(rows, grad, value, back, live, after):
    mid = grad[0].shape[1]

    def body(i, kind, given, fixed, made, totals):
        first, second, third, live = fixed
        total = given[0][...] * first[...] + given[1][...] * third[...] + second[...]
        if kind == 1:
            total = total * live[...]
        made[0][...] = total.astype(HALF)

    return rows.run(
        body, [grad, value, *back, live], [(mid, HALF)], [], 6 * rows.total() * mid, after
    )[0]


def input_grad_stage(rows, grad, first, weight, after):
    wide, mid = weight.shape

    def body(i, kind, given, fixed, made, totals):
        first = given[1][...]
        for start in range(0, wide, CHUNK):
            columns = slice(start, start + CHUNK)
            value = product_outer(first, fixed[0][columns, :])
            made[0][:, columns] = (value + given[0][:, columns].astype(FLOAT)).astype(HALF)

    return rows.run(
        body,
        [grad, first, weight],
        [(wide, HALF, far_shape)],
        [],
        2 * rows.total() * weight.size,
        after,
        streamed=[0],
    )[0]


def hidden_kernel(big, small, weight, live, out, packed):
    j = pl.program_id(0)
    channels = (packed.shape[1] - LANES) // 2
    pooled = jnp.concatenate([big[...].astype(HALF), small[...].astype(HALF)])
    value = product(pooled, weight[...])
    out[...] = value
    count = column_sum(live[...])
    mean = column_sum(value * live[...]) / count
    spread = column_sum(jnp.square(value - mean) * live[...])
    packed[:, pl.ds(pl.multiple_of(j * CHUNK, CHUNK), CHUNK)] = mean
    packed[:, pl.ds(pl.multiple_of(channels + j * CHUNK, CHUNK), CHUNK)] = spread
    packed[:, 2 * channels :] = jnp.broadcast_to(count, (1, LANES))


def hidden_stage(big, small, weight, live):
    crops = live.shape[0]
    wide, channels = weight.shape
    return call(
        hidden_kernel,
        [shape((crops, channels)), shape((1, 2 * channels + LANES))],
        [big, small, weight, live],
        grid=(channels // CHUNK,),
        in_specs=[
            whole(big.shape),
            whole(small.shape),
            pl.BlockSpec((wide, CHUNK), lambda j: (0, j)),
            whole(live.shape),
        ],
        out_specs=[
            pl.BlockSpec((crops, CHUNK), lambda j: (0, j)),
            whole((1, 2 * channels + LANES)),
        ],
        flops=2 * crops * weight.size,
        streamed=[2],
    )


def lanes_of(dims):
    return lax.broadcasted_iota(jnp.int32, dims, 1)


def sums_by_view(batch, stored, views):
    row = lax.broadcasted_iota(jnp.int32, batch.shape, 0) % views
    size = stored.shape[0] // views
    return jnp.concatenate(
        [
            column_sum(jnp.where(row == v, batch, 0.0))
            + column_sum(stored[v * size : (v + 1) * size])
            for v in range(views)
        ],
        axis=1,
    )


def queue_kernel(proto, views, queue, prototypes, stored):
    rows = queue.shape[0] // views
    value = queue[...].astype(FLOAT)
    unit = value * lax.rsqrt(jnp.sum(value * value, axis=1, keepdims=True) + EPS_UNIT)
    scores = product_outer(unit.astype(HALF), prototypes[...])
    value = jnp.where(lanes_of(scores.shape) < proto, jnp.exp(scores / EPS_CODE), 0.0)
    size = stored.shape[0] // views
    stored[...] = jnp.zeros(stored.shape, FLOAT)
    for v in range(views):
        stored[v * size : v * size + rows, :] = value[v * rows : (v + 1) * rows]


def score_kernel(
    proto, views, big_rows, hidden, scale, offset, project, prototypes, stored,
    active_out, embedded_out, unit_out, scores_out, batch_out, sums,
):
    active = silu(hidden[...] * scale[...] + offset[...]).astype(HALF)
    active_out[...] = active
    embedded = product(active, project[...])
    embedded_out[...] = embedded
    root = lax.rsqrt(jnp.sum(embedded * embedded, axis=1, keepdims=True) + EPS_UNIT)
    unit = (embedded * root).astype(HALF)
    unit_out[...] = unit
    scores = product_outer(unit, prototypes[...])
    scores_out[...] = scores
    batch = scores[:big_rows]
    batch = jnp.where(lanes_of(batch.shape) < proto, jnp.exp(batch / EPS_CODE), 0.0)
    batch_out[...] = batch
    sums[...] = sums_by_view(batch, stored[...], views)


def balanced(proto, views, parts, batch, stored):
    totals = tree([part[...] for part in parts])
    width = batch.shape[1]
    totals = [totals[:, v * width : (v + 1) * width] for v in range(views)]
    totals = [jnp.where(lanes_of(t.shape) < proto, t, 1.0) for t in totals]
    row = lax.broadcasted_iota(jnp.int32, batch.shape, 0) % views
    own = jnp.zeros(batch.shape, FLOAT)
    for v in range(views):
        own = jnp.where(row == v, totals[v], own)
    batch = batch / own
    batch = batch / jnp.sum(batch, axis=1, keepdims=True)
    if stored is None:
        return batch, None
    size = stored.shape[0] // views
    stored = jnp.concatenate(
        [stored[v * size : (v + 1) * size] / totals[v] for v in range(views)]
    )
    sums = jnp.sum(stored, axis=1, keepdims=True)
    return batch, jnp.where(sums > 0.0, stored / jnp.where(sums > 0.0, sums, 1.0), 0.0)


def balance_kernel(proto, views, *refs):
    *parts, batch, stored, batch_out, stored_out, sums = refs
    batch, stored = balanced(proto, views, parts, batch[...], stored[...])
    batch_out[...] = batch
    stored_out[...] = stored
    sums[...] = sums_by_view(batch, stored, views)


def loss_kernel(proto, views, *refs):
    (
        *parts, batch, scores, share, live, embedded, hidden, scale, offset, mean, root, project, prototypes,
        grad_scores_out, grad_embedded_out, grad_out, packed,
    ) = refs
    codes, _ = balanced(proto, views, parts, batch[...], None)
    big = codes.shape[0]
    images = big // views
    slots = (scores.shape[0] - big) // images
    row = lax.broadcasted_iota(jnp.int32, codes.shape, 0) % views
    others = jnp.zeros(codes.shape, FLOAT)
    for turn in range(1, views):
        ahead = jnp.concatenate([codes[turn:], codes[:turn]])
        behind = jnp.concatenate([codes[turn - views :], codes[: turn - views]])
        others = others + jnp.where(row + turn < views, ahead, behind)
    both = codes + others
    targets = jnp.concatenate(
        [others]
        + [
            jnp.broadcast_to(both[k * views : k * views + 1], (slots, both.shape[1]))
            for k in range(images)
        ]
    )
    lanes = lanes_of(scores.shape)
    logits = jnp.where(lanes < proto, scores[...] / SOFTMAX_HEAT, -1e30)
    top = jnp.max(logits, axis=1, keepdims=True)
    powers = jnp.where(lanes < proto, jnp.exp(logits - top), 0.0)
    sums = jnp.sum(powers, axis=1, keepdims=True)
    logs = jnp.where(lanes < proto, logits - top - jnp.log(sums), 0.0)
    loss = -column_sum(jnp.sum(targets * logs, axis=1, keepdims=True) * share[...])
    mass = jnp.sum(targets, axis=1, keepdims=True)
    grad = (share[...] / SOFTMAX_HEAT) * (powers * (mass / sums) - targets)
    grad = grad.astype(HALF)
    grad_scores_out[...] = grad
    grad = product(grad, prototypes[...])
    value = embedded[...]
    scaled = lax.rsqrt(jnp.sum(value * value, axis=1, keepdims=True) + EPS_UNIT)
    unit = value * scaled
    grad = scaled * (grad - unit * jnp.sum(unit * grad, axis=1, keepdims=True))
    grad = grad.astype(HALF)
    grad_embedded_out[...] = grad
    channels = scale.shape[1]
    for start in range(0, channels, CHUNK):
        columns = slice(start, start + CHUNK)
        before = hidden[:, columns]
        part = product_outer(grad, project[columns, :])
        part = part * slope(before * scale[:, columns] + offset[:, columns])
        grad_out[:, columns] = part
        part = part * live[...]
        packed[:, columns] = column_sum(part)
        packed[:, channels + start : channels + start + CHUNK] = (
            column_sum(part * (before - mean[:, columns])) * root[:, columns]
        )
    packed[:, 2 * channels :] = jnp.broadcast_to(loss, (1, LANES))


def pooled_back_kernel(areas, big_rows, grad, hidden, live, first, second, third, weight, grad_out, big, small):
    value = grad[...] * first[...] + hidden[...] * third[...] + second[...]
    value = value * live[...]
    grad_out[...] = value
    part = product_outer(value.astype(HALF), weight[...])
    big[...] = part[:big_rows] / areas[0]
    small[...] = part[big_rows:] / areas[1]


def turn_kernel(blocks, big, small, out):
    value = jnp.concatenate([big[...], small[...]]).T
    rows = value.shape[0] // blocks
    planes = out.shape[0]
    for k in range(planes):
        parts = [value[j * rows : (j + 1) * rows] for j in range(k, blocks, planes)]
        out[k] = jnp.concatenate(parts).T


def hidden_grad_kernel(left, right, out):
    out[...] = product_inner(left[...].astype(HALF), right[...].astype(HALF))


def hidden_grad_stage(left, right, after):
    crops, height = left.shape
    width = right.shape[1]
    return call(
        hidden_grad_kernel,
        shape((height, width)),
        [left, right],
        grid=(width // CHUNK,),
        in_specs=[whole(left.shape), pl.BlockSpec((crops, CHUNK), lambda j: (0, j))],
        out_specs=pl.BlockSpec((height, CHUNK), lambda j: (0, j)),
        flops=2 * crops * height * width,
        streamed=[0, 1],
        after=after,
    )


def head_grad_kernel(devices, bits, active, grad_embedded, unit, grad_scores, keep, send):
    half = pick(bits, 0)
    project = product_inner(active[...], grad_embedded[...])
    proto = product_inner(unit[...], grad_scores[...])
    rows, lines = project.shape[0] // devices, proto.shape[0] // devices

    def store(k, here, columns, even, odd):
        keep[0, k, here, columns] = jnp.where(half == 0, even, odd)
        send[0, k, here, columns] = jnp.where(half == 0, odd, even)

    for k in range(devices // 2):
        pair = project[2 * k * rows : 2 * (k + 1) * rows]
        for part in range(2):
            start = part * rows // 2
            store(
                k,
                slice(0, rows // 2),
                slice(part * LANES, (part + 1) * LANES),
                pair[start : start + rows // 2],
                pair[rows + start : rows + start + rows // 2],
            )
        pair = proto[2 * k * lines : 2 * (k + 1) * lines]
        for part in range(proto.shape[1] // TILE):
            piece = pair[:, part * TILE : (part + 1) * TILE]
            start = rows // 2 + part * lines
            store(k, slice(start, start + lines), slice(0, TILE), piece[:lines], piece[lines:])


def head_grad_stage(active, grad_embedded, unit, grad_scores, devices, me, after):
    rows = active.shape[1] * grad_embedded.shape[1] + unit.shape[1] * grad_scores.shape[1]
    out = shape((1, devices // 2, rows // (devices * TILE), TILE))
    return call(
        lambda *refs: head_grad_kernel(devices, *refs),
        [out, out],
        [active, grad_embedded, unit, grad_scores],
        scalars=[me],
        after=after,
    )


def conv(field, weight):
    return lax.conv_general_dilated(
        field,
        weight,
        (1, 1),
        ((1, 1), (1, 1)),
        dimension_numbers=("HWNC", "HWIO", "HWNC"),
        preferred_element_type=FLOAT,
    )


def conv_back(field, weight):
    return lax.conv_general_dilated(
        field,
        lax.rev(weight, (0, 1)),
        (1, 1),
        ((1, 1), (1, 1)),
        dimension_numbers=("HWNC", "HWOI", "HWNC"),
        preferred_element_type=FLOAT,
    )


def conv_filter(field, grad):
    return lax.conv_general_dilated(
        field,
        grad,
        (1, 1),
        ((1, 1), (1, 1)),
        dimension_numbers=("HWCN", "HWIO", "HWNC"),
        preferred_element_type=FLOAT,
    )


def local(
    big_crops,
    small_crops,
    small_count,
    w_reduce,
    w_spatial,
    w_expand,
    gain_mid,
    bias_mid,
    gain_wide,
    bias_wide,
    w_hidden,
    gain_head,
    bias_head,
    w_project,
    prototypes,
    queue,
):
    devices = lax.axis_size("dp")
    image_rows = small_count.shape[0]
    images = image_rows * devices
    big_rows, big_side = big_crops.shape[:2]
    small_rows, small_side = small_crops.shape[:2]
    views = big_rows // image_rows
    slots = small_rows // image_rows
    wide = big_crops.shape[3]
    mid = w_reduce.shape[1]
    hid = w_hidden.shape[1]
    proj, proto = prototypes.shape
    proto_wide = -(-proto // CHUNK) * CHUNK
    crops = big_rows + small_rows
    areas = (big_side * big_side, small_side * small_side)
    rows = Rows(big_side, big_rows, small_side, small_rows)
    sides = ((big_side, big_side, big_rows), (small_side, small_side, small_rows))
    planes = [[k * PLANE + j for j in range(PLANE)] for k in range(devices // PLANE)]
    stacks = [[k * PLANE + j for k in range(devices // PLANE)] for j in range(PLANE)]
    me = lax.axis_index("dp").astype(jnp.int32).reshape(1)

    slot_mask = (jnp.arange(slots)[None, :] < small_count[:, None]).astype(FLOAT)
    slot_flags = slot_mask.reshape(-1)
    live = jnp.tile(slot_flags, small_side)[:, None]
    crop_live = jnp.concatenate([jnp.ones((big_rows,), FLOAT), slot_flags])[:, None]
    share = 1.0 / (images * views * (views - 1.0 + small_count.astype(FLOAT)))
    share = jnp.concatenate(
        [jnp.repeat(share, views), jnp.repeat(share, slots) * slot_flags]
    )[:, None]

    def fields(pair):
        return [a.reshape(*s, a.shape[-1]) for a, s in zip(pair, sides)]

    def flat(pair):
        return tuple(a.reshape(-1, a.shape[-1]) for a in pair)

    inputs = flat((jnp.transpose(big_crops, (1, 2, 0, 3)), jnp.transpose(small_crops, (1, 2, 0, 3))))
    taps = jnp.transpose(w_spatial, (1, 0, 2))
    filters = taps.reshape(3, 3, mid, mid)
    lines = jnp.pad(jnp.transpose(prototypes), ((0, proto_wide - proto), (0, 0)))

    first, packed = reduce_stage(rows, inputs, w_reduce, live)
    scale_one, offset_one, mean_one, root_one, pixel_count = settle_norm(
        packed, gain_mid[0], bias_mid[0], devices
    )
    mid_one = fields([silu(a * scale_one + offset_one).astype(HALF) for a in first])
    second = flat([conv(a, filters) for a in mid_one])
    packed = norm_stage(rows, second, live)
    scale_two, offset_two, mean_two, root_two, _ = settle_norm(
        packed, gain_mid[1], bias_mid[1], devices
    )
    third, mid_two, packed = expand_stage(rows, second, scale_two, offset_two, w_expand, live)
    scale_three, offset_three, mean_three, root_three, _ = settle_norm(
        packed, gain_wide, bias_wide, devices
    )
    pooled_big, pooled_small = pool_stage(rows, third, inputs, scale_three, offset_three)

    hidden, packed = hidden_stage(pooled_big, pooled_small, w_hidden, crop_live)
    scale_head, offset_head, mean_head, root_head, crop_count = settle_norm(
        packed, gain_head, bias_head, devices
    )
    stored_rows = views * (-(-queue.shape[1] // 8) * 8)
    stored = call(
        lambda *refs: queue_kernel(proto, views, *refs),
        shape((stored_rows, proto_wide)),
        [queue.reshape(-1, proj), lines],
    )
    active, embedded, unit, scores, batch, sums = call(
        lambda *refs: score_kernel(proto, views, big_rows, *refs),
        [
            shape((crops, hid), HALF),
            shape((crops, proj)),
            shape((crops, proj), HALF),
            shape((crops, proto_wide)),
            shape((big_rows, proto_wide)),
            shape((1, views * proto_wide)),
        ],
        [hidden, scale_head, offset_head, w_project, lines, stored],
    )
    for step in range(ITERS - 1):
        batch, stored, sums = call(
            lambda *refs: balance_kernel(proto, views, *refs),
            [shape(batch.shape), shape(stored.shape), shape(sums.shape)],
            [*sum_parts(sums, devices), batch, stored],
            )

    loss_outs = [
        shape((crops, proto_wide), HALF),
        shape((crops, proj), HALF),
        shape((crops, hid)),
        shape((1, 2 * hid + LANES)),
    ]
    parts = sum_parts(sums, devices)
    loss_args = [
        batch,
        scores,
        share,
        crop_live,
        embedded,
        hidden,
        scale_head,
        offset_head,
        mean_head,
        root_head,
        w_project,
        lines,
    ]
    grad_scores, grad_embedded, grad_active, packed = call(
        lambda *refs: loss_kernel(proto, views, *refs),
        loss_outs,
        [*parts, *loss_args],
        grid=(1,),
        in_specs=[whole(a.shape) for a in (*parts, *loss_args)],
        out_specs=[whole(a.shape) for a in loss_outs],
        streamed=range(len(parts), len(parts) + len(loss_args)),
    )
    made = {}

    def head_work(mark):
        made["head"] = head_grad_stage(
            active, grad_embedded, unit, grad_scores, devices, me, [mark]
        )
        return [made["head"][0]]

    *back, gain_head_grad, bias_head_grad, loss = settle_back(
        packed, gain_head, mean_head, root_head, crop_count, devices, [head_work]
    )
    head_sum = Scatter(*made["head"], devices, me)
    grad_hidden, *grad_pooled = call(
        lambda *refs: pooled_back_kernel(areas, big_rows, *refs),
        [shape((crops, hid)), shape((big_rows, wide)), shape((small_rows, wide))],
        [grad_active, hidden, crop_live, *back, w_hidden],
        grid=(wide // CHUNK,),
        in_specs=[
            whole((crops, hid)),
            whole((crops, hid)),
            whole((crops, 1)),
            whole((1, hid)),
            whole((1, hid)),
            whole((1, hid)),
            pl.BlockSpec((CHUNK, hid), lambda j: (j, 0)),
        ],
        out_specs=[
            whole((crops, hid)),
            pl.BlockSpec((big_rows, CHUNK), lambda j: (0, j)),
            pl.BlockSpec((small_rows, CHUNK), lambda j: (0, j)),
        ],
        flops=2 * crops * w_hidden.size,
        streamed=[6],
    )
    plane_grad = lax.all_gather(grad_hidden, "dp", axis_index_groups=planes, tiled=True)

    grad_residual, packed = residual_back_stage(
        rows,
        third,
        inputs,
        grad_pooled,
        scale_three,
        offset_three,
        mean_three,
        root_three,
        live,
        [head_sum.go()],
    )
    packed = tie(packed, head_sum.got)
    *back, gain_three, bias_three, _ = settle_back(
        packed, gain_wide, mean_three, root_three, pixel_count, devices
    )
    turned = call(
        lambda *refs: turn_kernel(devices, *refs),
        shape((PLANE, crops, wide // PLANE)),
        [pooled_big, pooled_small],
        after=[back[0]],
    )
    plane_pooled = lax.all_to_all(
        turned, "dp", 0, 0, axis_index_groups=planes, tiled=True
    ).reshape(PLANE * crops, wide // PLANE)
    grad_third, grad_two, packed = expand_back_stage(
        rows,
        grad_residual,
        third,
        second,
        back,
        w_expand,
        [scale_two, offset_two, mean_two, root_two],
        live,
        [turned, head_sum.go([turned])],
    )
    packed = tie(packed, [Far(plane_pooled), *head_sum.got])

    def expand_work(mark):
        made["expand"] = weight_grad(mid_two, grad_third, devices, me, 1, [mark], [1, 3])
        return [made["expand"][0]]

    def hidden_work(mark):
        made["hidden"] = hidden_grad_stage(plane_pooled, plane_grad, [mark])
        return [made["hidden"]]

    *back, gain_two, bias_two, _ = settle_back(
        packed,
        gain_mid[1],
        mean_two,
        root_two,
        pixel_count,
        devices,
        [expand_work, hidden_work],
    )
    expand_sum = Scatter(*made["expand"], devices, me)
    hidden_grad = lax.psum_scatter(
        made["hidden"], "dp", scatter_dimension=0, axis_index_groups=stacks, tiled=True
    )
    grad_second = norm_back_stage(
        rows, grad_two, second, back, live, [expand_sum.go([back[0]]), head_sum.go([back[0]])]
    )
    grad_mid_one = flat([conv_back(a, filters) for a in fields(grad_second)])
    grad_one, packed = slope_stage(
        rows,
        grad_mid_one,
        first,
        [scale_one, offset_one, mean_one, root_one],
        live,
        [*expand_sum.got, *head_sum.got],
    )

    def big_work(mark):
        grad = tie(grad_second[0], [mark])
        made["big"] = conv_filter(mid_one[0], fields((grad, grad_second[1]))[0])
        return [made["big"]]

    def small_work(mark):
        grad = tie(grad_second[1], [mark])
        part = made["big"] + conv_filter(mid_one[1], fields((grad_second[0], grad))[1])
        made["spatial"] = part.reshape(9, devices, mid // devices, mid)
        made["send"] = send_rows(made["spatial"], me, [])
        return [Far(made["send"])]

    *back, gain_one, bias_one, _ = settle_back(
        packed,
        gain_mid[0],
        mean_one,
        root_one,
        pixel_count,
        devices,
        [big_work, small_work],
    )
    spatial_sum = Scatter(made["spatial"], made["send"], devices, me)
    mark = expand_sum.go([head_sum.go([back[0]])])
    grad_first = norm_back_stage(rows, grad_one, first, back, live, [mark])
    reduce_keep, reduce_send = weight_grad(inputs, grad_first, devices, me, 0, (), [0, 2])
    mark = spatial_sum.go([reduce_keep, *expand_sum.got, *head_sum.got])
    reduce_sum = Scatter(reduce_keep, tie(reduce_send, [mark]), devices, me)
    mark = expand_sum.go([mark])
    grad_inputs = input_grad_stage(rows, grad_residual, grad_first, w_reduce, [mark])
    grad_big, grad_small = fields(grad_inputs)
    mark = expand_sum.go([Far(grad_inputs[0])])
    for part in (spatial_sum, reduce_sum) * 4:
        if not part.complete():
            mark = part.go([mark])
    head_grad = head_sum.end()[0]
    ends = w_project.shape[0] // (2 * devices)
    project_grad = jnp.concatenate([head_grad[:ends, :LANES], head_grad[:ends, LANES:]])
    proto_grad = head_grad[ends:].reshape(-1, proj // devices, TILE)
    proto_grad = jnp.transpose(proto_grad, (1, 0, 2)).reshape(proj // devices, -1)[:, :proto]
    expand_grad = expand_sum.end()[0]
    spatial_grad = spatial_sum.end()
    reduce_grad = reduce_sum.end()[0]
    return (
        loss[0, 0],
        jnp.transpose(grad_big, (2, 0, 1, 3)),
        jnp.transpose(grad_small, (2, 0, 1, 3)),
        reduce_grad,
        jnp.transpose(spatial_grad, (1, 0, 2)),
        expand_grad,
        jnp.concatenate([gain_one, gain_two]),
        jnp.concatenate([bias_one, bias_two]),
        gain_three[0],
        bias_three[0],
        hidden_grad,
        gain_head_grad[0],
        bias_head_grad[0],
        project_grad,
        proto_grad,
    )


def solution(mesh):
    placed = (
        P("dp", None, None, None),
        P("dp", None, None, None),
        P("dp"),
        P(),
        P(),
        P(),
        P(),
        P(),
        P(),
        P(),
        P(),
        P(),
        P(),
        P(),
        P(),
        P(None, "dp", None),
    )
    return jax.shard_map(
        local,
        mesh=mesh,
        in_specs=placed,
        out_specs=(
            P(),
            P("dp", None, None, None),
            P("dp", None, None, None),
            P("dp", None),
            P("dp", None, None),
            P("dp", None),
            P(),
            P(),
            P(),
            P(),
            P("dp", None),
            P(),
            P(),
            P("dp", None),
            P("dp", None),
        ),
        check_vma=False,
    )
```

```python
import math

import jax
import jax.numpy as jnp
from jax import lax
from jax.experimental import pallas as pl
from jax.experimental.pallas import tpu as pltpu
from jax.sharding import PartitionSpec as P

ITERS = 3

EPS_NORM = 1e-05
EPS_UNIT = 1e-06
EPS_CODE = 0.05
SOFTMAX_HEAT = 0.1
LANES = 128
PLANE = 8
CHUNK = 512
TILE = 256
ROWS = 32
VMEM_LIMIT = 60 << 20
GRID_LIMIT = 16 << 20
SLOTS = 3
FLOAT = jnp.float32
HALF = jnp.bfloat16


def product(left, right):
    return jnp.dot(left, right, preferred_element_type=FLOAT)


def product_inner(left, right):
    return lax.dot_general(left, right, (((0,), (0,)), ((), ())), preferred_element_type=FLOAT)


def product_outer(left, right):
    return lax.dot_general(left, right, (((1,), (1,)), ((), ())), preferred_element_type=FLOAT)


def sigmoid(value):
    return 0.5 * jnp.tanh(0.5 * value) + 0.5


def silu(value):
    return value * sigmoid(value)


def slope(value):
    gate = sigmoid(value)
    return gate * (1.0 + value * (1.0 - gate))


def column_sum(value):
    return jnp.sum(value, axis=0, keepdims=True)


def shape(dims, dtype=FLOAT):
    return jax.ShapeDtypeStruct(dims, dtype)


def far_shape(dims, dtype=FLOAT):
    return pltpu.HBM(dims, dtype)


def far(array):
    return pltpu.with_memory_space_constraint(array, pltpu.HBM)


def whole(dims):
    return pl.BlockSpec(dims, lambda *_: (0,) * len(dims))


class Far:
    def __init__(self, array):
        self.array = array


def call(
    kernel,
    out_shape,
    args,
    grid=None,
    in_specs=None,
    out_specs=None,
    flops=0,
    after=(),
    scalars=(),
    streamed=(),
    scratch=(),
):
    flat = out_shape if isinstance(out_shape, (list, tuple)) else [out_shape]
    size = sum(a.size * a.dtype.itemsize for a in args)
    size += sum(math.prod(a.shape) * jnp.dtype(a.dtype).itemsize for a in flat)
    args = [far(a) if k in streamed else a for k, a in enumerate(args)]
    here = pl.BlockSpec(memory_space=pltpu.VMEM)
    limit = 0
    if grid is None:
        in_specs = [here] * len(args)
        out_specs = jax.tree.map(lambda _: here, out_shape)
        limit = max(limit, size + size // 4 + (2 << 20))
    else:
        limit = GRID_LIMIT + sum(
            math.prod(a.shape) * jnp.dtype(a.dtype).itemsize for a in scratch[:-1]
        )
    limit += sum(a.size * a.dtype.itemsize for a in after if not isinstance(a, Far))
    first, last = len(scalars), len(scalars) + len(args)

    def run(*refs):
        kernel(*refs[:last], *refs[last + len(after) :])

    specs = dict(out_specs=out_specs)
    if grid is not None:
        specs["grid"] = grid
    return pl.pallas_call(
        run,
        out_shape=out_shape,
        in_specs=[pl.BlockSpec(memory_space=pltpu.SMEM)] * first
        + list(in_specs)
        + [pl.BlockSpec(memory_space=pl.ANY if isinstance(a, Far) else pltpu.VMEM) for a in after],
        scratch_shapes=list(scratch),
        compiler_params=pltpu.CompilerParams(vmem_limit_bytes=min(limit, VMEM_LIMIT)),
        cost_estimate=pl.CostEstimate(flops=flops, bytes_accessed=size, transcendentals=0),
        **specs,
    )(*scalars, *args, *(a.array if isinstance(a, Far) else a for a in after))


def copy_kernel(source, out):
    out[...] = source[...]


def tie(value, after):
    return call(copy_kernel, shape(value.shape, value.dtype), [value], after=after)


def rounds(devices):
    bits = [1 << k for k in range(devices.bit_length() - 1)]
    return [bits[:1]] + [bits[k : k + 2] for k in range(1, len(bits), 2)]


def peers(value, bits, devices):
    masks = [0]
    for bit in bits:
        masks = masks + [mask | bit for mask in masks]
    return [value] + [
        lax.ppermute(value, "dp", [(i, i ^ mask) for i in range(devices)]) for mask in masks[1:]
    ]


def tree(values):
    while len(values) > 1:
        values = [values[k] + values[k + 1] for k in range(0, len(values), 2)]
    return values[0]


def exchange(value, devices, merge, works=()):
    first, *others = rounds(devices)
    parts = peers(value, first, devices)
    for k, bits in enumerate(others):
        value = merge(parts)
        parts = peers(value, bits, devices)
        if k < len(works):
            parts[0] = tie(value, works[k](value))
    return parts


def sum_parts(value, devices, works=()):
    return exchange(value, devices, tree, works)


def merged(parts):
    channels = (parts[0].shape[1] - LANES) // 2
    counts = [part[:, 2 * channels : 2 * channels + 1] for part in parts]
    means = [part[:, :channels] for part in parts]
    spreads = [part[:, channels : 2 * channels] for part in parts]
    total = tree(counts)
    mean = tree([c * m for c, m in zip(counts, means)]) / total
    spread = tree([s + c * jnp.square(m - mean) for s, c, m in zip(spreads, counts, means)])
    return total, mean, spread


def merge_kernel(*refs):
    *parts, out = refs
    channels = (out.shape[1] - LANES) // 2
    total, mean, spread = merged([part[...] for part in parts])
    out[:, :channels] = mean
    out[:, channels : 2 * channels] = spread
    out[:, 2 * channels :] = jnp.broadcast_to(total, (1, LANES))


def merge_norms(parts):
    return call(merge_kernel, shape(parts[0].shape), parts)


def settle_kernel(*refs):
    *parts, gain, bias, scale, offset, mean_out, root_out, count = refs
    total, mean, spread = merged([part[...] for part in parts])
    root = lax.rsqrt(spread / total + EPS_NORM)
    factor = gain[...] * root
    scale[...] = factor
    offset[...] = bias[...] - mean * factor
    mean_out[...] = mean
    root_out[...] = root
    count[...] = jnp.broadcast_to(total, (1, LANES))


def settle_norm(packed, gain, bias, devices):
    channels = gain.shape[0]
    parts = exchange(packed, devices, merge_norms)
    row = shape((1, channels))
    return call(
        settle_kernel,
        [row, row, row, row, shape((1, LANES))],
        [*parts, gain[None], bias[None]],
    )


def settle_back_kernel(*refs):
    *parts, gain, mean, root, count, first, second, third, gain_sum, bias_sum, extra = refs
    channels = gain.shape[1]
    packed = tree([part[...] for part in parts])
    total = count[:, :1]
    low, high = packed[:, :channels], packed[:, channels : 2 * channels]
    factor = gain[...] * root[...]
    pull = root[...] * high / total
    first[...] = factor
    second[...] = factor * (mean[...] * pull - low / total)
    third[...] = -factor * pull
    gain_sum[...] = high
    bias_sum[...] = low
    extra[...] = packed[:, 2 * channels :]


def settle_back(packed, gain, mean, root, count, devices, works=()):
    parts = sum_parts(packed, devices, works)
    row = shape((1, gain.shape[0]))
    return call(
        settle_back_kernel,
        [row, row, row, row, row, shape((1, LANES))],
        [*parts, gain[None], mean, root, count],
    )


def pick(bits, place):
    return (bits[0] >> place) & 1


def send_kernel(bits, value, send):
    other = 1 - pick(bits, 0)

    def step(t, _):
        for k in range(send.shape[1]):
            send[t, k] = value[t, 2 * k + other]
        return _

    lax.fori_loop(0, value.shape[0], step, 0)


def send_rows(value, me, after):
    taps, devices, rows, width = value.shape
    out = shape((taps, devices // 2, rows, width))
    return call(send_kernel, out, [value], scalars=[me], after=after)


def first_kernel(bits, keep, got, keep_one, send_one, keep_two, send_two):
    taps, blocks, _, width = got.shape
    uncut = keep.shape[1] // blocks
    half = pick(bits, 0) * (uncut - 1)
    left, right = slice(0, width // 2), slice(width // 2, width)
    one, two = pick(bits, 1), pick(bits, 2)

    def step(t, _):
        for k in range(blocks // 2):
            for out, there in ((keep_one, 2 * k + one), (send_one, 2 * k + 1 - one)):
                out[t, k] = keep[t, uncut * there + half, :, left] + got[t, there, :, left]
            low = 4 * (k // 2) + k % 2
            for out, there in ((keep_two, low + 2 * two), (send_two, low + 2 * (1 - two))):
                out[t, k] = keep[t, uncut * there + half, :, right] + got[t, there, :, right]
        return _

    lax.fori_loop(0, taps, step, 0)


def second_kernel(bits, keep_one, got_one, keep_two, got_two, *outs):
    def step(t, _):
        for keep, got, place, out_keep, out_send in (
            (keep_one, got_one, 2, outs[0], outs[1]),
            (keep_two, got_two, 1, outs[2], outs[3]),
        ):
            half = pick(bits, place)
            for k in range(out_keep.shape[1]):
                out_keep[t, k] = keep[t, 2 * k + half] + got[t, 2 * k + half]
                out_send[t, k] = keep[t, 2 * k + 1 - half] + got[t, 2 * k + 1 - half]
        return _

    lax.fori_loop(0, keep_one.shape[0], step, 0)


def third_kernel(bits, keep_one, got_one, keep_two, got_two, out_keep, out_send):
    half = pick(bits, 3)
    width = keep_one.shape[3]

    def step(t, _):
        for k in range(out_keep.shape[1]):
            for out, there in ((out_keep, 2 * k + half), (out_send, 2 * k + 1 - half)):
                out[t, k, :, :width] = keep_one[t, there] + got_one[t, there]
                out[t, k, :, width:] = keep_two[t, there] + got_two[t, there]
        return _

    lax.fori_loop(0, keep_one.shape[0], step, 0)


def later_kernel(place, bits, keep, got, out_keep, out_send):
    half = pick(bits, place)

    def step(t, _):
        for k in range(out_keep.shape[1]):
            for out, there in ((out_keep, 2 * k + half), (out_send, 2 * k + 1 - half)):
                out[t, k] = keep[t, there] + got[t, there]
        return _

    lax.fori_loop(0, keep.shape[0], step, 0)


def last_kernel(keep, got, out):
    out[...] = keep[...] + got[...]


class Scatter:
    def __init__(self, keep, send, devices, me):
        self.devices, self.me = devices, me
        self.bits = devices.bit_length() - 1
        self.held = [keep]
        self.got = [self.cross(send, 0)]
        self.stage = 0

    def cross(self, value, place):
        return lax.ppermute(
            value, "dp", [(i, i ^ (1 << place)) for i in range(self.devices)]
        )

    def go(self, after=()):
        taps, blocks, rows, width = self.got[0].shape
        if self.stage == 0:
            out = shape((taps, blocks // 2, rows, width // 2))
            kernel, places = first_kernel, (1, 2)
        elif self.stage == 1:
            out = shape((taps, blocks // 2, rows, width))
            kernel, places = second_kernel, (2, 1)
        elif self.stage == 2:
            out = shape((taps, blocks // 2, rows, 2 * width))
            kernel, places = third_kernel, (3,)
        else:
            place = self.stage + 1
            out = shape((taps, blocks // 2, rows, width))
            kernel, places = (lambda *refs: later_kernel(place, *refs)), (place,)
        args = [a for pair in zip(self.held, self.got) for a in pair]
        made = call(kernel, [out] * (2 * len(places)), args, after=after, scalars=[self.me])
        self.held = list(made[::2])
        self.got = [self.cross(send, place) for send, place in zip(made[1::2], places)]
        self.stage += 1
        return self.held[0]

    def complete(self):
        return self.got[0].shape[1] == 1

    def end(self):
        while not self.complete():
            self.go()
        taps, _, rows, width = self.held[0].shape
        done = call(last_kernel, shape(self.held[0].shape), [self.held[0], self.got[0]])
        return done.reshape(taps, rows, width)


def weight_grad_kernel(rows, bits, left_big, right_big, left_small, right_small, keep, send):
    value = product_inner(left_big[...], right_big[...])
    value = value + product_inner(left_small[...], right_small[...])
    half = pick(bits, 0)
    for k in range(value.shape[0] // (2 * rows)):
        even = value[2 * k * rows : (2 * k + 1) * rows]
        odd = value[(2 * k + 1) * rows : (2 * k + 2) * rows]
        keep[0, k] = jnp.where(half == 0, even, odd)
        send[0, k] = jnp.where(half == 0, odd, even)


def weight_grad(left, right, devices, me, along, after=(), streamed=()):
    height, width = left[0].shape[1], right[0].shape[1]
    rows = height // devices
    out = shape((1, devices // 2, rows, width))

    def spec(pair, k, moves):
        dims = (pair[k].shape[0], CHUNK if moves else pair[k].shape[1])
        return pl.BlockSpec(dims, lambda j: (0, j if moves else 0))

    if along == 0:
        steps = height // CHUNK
        block = pl.BlockSpec((1, devices // 2 // steps, rows, width), lambda j: (0, j, 0, 0))
    else:
        steps = width // CHUNK
        block = pl.BlockSpec((1, devices // 2, rows, CHUNK), lambda j: (0, 0, 0, j))
    return call(
        lambda *refs: weight_grad_kernel(rows, *refs),
        [out, out],
        [left[0], right[0], left[1], right[1]],
        grid=(steps,),
        in_specs=[
            spec(left, 0, along == 0),
            spec(right, 0, along == 1),
            spec(left, 1, along == 0),
            spec(right, 1, along == 1),
        ],
        out_specs=[block, block],
        flops=2 * (left[0].shape[0] + left[1].shape[0]) * height * width,
        after=after,
        streamed=streamed,
        scalars=[me],
    )


class Rows:
    def __init__(self, big_side, big_crops, small_side, small_crops):
        self.steps = big_side, small_side
        self.rows = big_side * big_crops, small_side * small_crops
        self.crops = big_crops, small_crops

    def specs(self, channels):
        first = self.steps[0]
        return [
            pl.BlockSpec((self.rows[0], channels), lambda i: (jnp.minimum(i, first - 1), 0)),
            pl.BlockSpec((self.rows[1], channels), lambda i: (jnp.maximum(i - first, 0), 0)),
        ]

    def shapes(self, channels, dtype, place=shape):
        return [place((s * r, channels), dtype) for s, r in zip(self.steps, self.rows)]

    def run(self, body, args, row_outs, whole_outs, flops, after=(), streamed=()):
        pairs = [a for a in args if isinstance(a, tuple)]
        rest = [a for a in args if not isinstance(a, tuple)]
        in_specs, flat = [], []
        scratch = []
        for k, pair in enumerate(pairs):
            flat += list(pair)
            if k in streamed:
                in_specs += [pl.BlockSpec(memory_space=pl.ANY)] * 2
                scratch += [
                    pltpu.VMEM((SLOTS, rows, pair[0].shape[1]), pair[0].dtype)
                    for rows in self.rows
                ]
            else:
                in_specs += self.specs(pair[0].shape[1])
        if streamed:
            scratch.append(pltpu.SemaphoreType.DMA((2 * len(streamed), SLOTS)))
        in_specs += [whole(a.shape) for a in rest]
        out_shapes, out_specs = [], []
        for channels, dtype, *place in row_outs:
            out_shapes += self.shapes(channels, dtype, *place)
            out_specs += self.specs(channels)
        out_shapes += [shape(dims) for dims in whole_outs]
        out_specs += [whole(dims) for dims in whole_outs]
        n_in, n_rest, n_out = len(pairs), len(rest), len(row_outs)

        def kernel(*refs):
            i = pl.program_id(0)
            refs, held = refs[: len(refs) - len(scratch)], refs[len(refs) - len(scratch) :]
            given, fixed = refs[: 2 * n_in], refs[2 * n_in : 2 * n_in + n_rest]
            made = refs[2 * n_in + n_rest :]

            def fetch(kind, step, slot):
                start = step * self.rows[kind]
                if not isinstance(step, int):
                    start = pl.multiple_of(start, self.rows[kind])
                return [
                    pltpu.make_async_copy(
                        given[2 * k + kind].at[pl.ds(start, self.rows[kind]), :],
                        held[2 * n + kind].at[slot],
                        held[-1].at[2 * n + kind, slot],
                    )
                    for n, k in enumerate(streamed)
                ]

            def start_big(step):
                for copy in fetch(0, step, lax.rem(step, SLOTS)):
                    copy.start()

            if streamed:

                @pl.when(i == 0)
                def _():
                    for step in range(SLOTS - 1):
                        for copy in fetch(0, step, step):
                            copy.start()

                pl.when(i + SLOTS - 1 < self.steps[0])(lambda: start_big(i + SLOTS - 1))
                for step in range(self.steps[1]):

                    @pl.when(i == self.steps[0] - self.steps[1] + step)
                    def _(step=step):
                        for copy in fetch(1, step, step):
                            copy.start()

            for kind in range(2):
                here = i < self.steps[0] if kind == 0 else i >= self.steps[0]

                @pl.when(here)
                def _(kind=kind):
                    blocks = list(given[kind : 2 * n_in : 2])
                    if streamed:
                        step = i if kind == 0 else i - self.steps[0]
                        slot = lax.rem(step, SLOTS)
                        for copy in fetch(kind, step, slot):
                            copy.wait()
                        for n, k in enumerate(streamed):
                            blocks[k] = held[2 * n + kind].at[slot]
                    body(i, kind, blocks, fixed, made[kind : 2 * n_out : 2], made[2 * n_out :])

        made = call(
            kernel,
            out_shapes,
            flat + rest,
            grid=(sum(self.steps),),
            in_specs=in_specs,
            out_specs=out_specs,
            flops=flops,
            after=after,
            streamed=[2 * k + j for k in streamed for j in range(2)],
            scratch=scratch,
        )
        return [tuple(made[2 * k : 2 * k + 2]) for k in range(n_out)] + list(made[2 * n_out :])

    def total(self):
        return sum(s * r for s, r in zip(self.steps, self.rows))


def add_norm(i, kind, packed, value, weight, start):
    channels = (packed.shape[1] - LANES) // 2
    width = value.shape[1]
    here = slice(start, start + width)
    there = slice(channels + start, channels + start + width)
    rows = value.shape[0]
    count = jnp.full((1, 1), rows, FLOAT) if kind == 0 else column_sum(weight)
    pivot = column_sum(value[:ROWS]) * (1.0 / ROWS)
    means, spreads = [], []
    for left in range(0, width, TILE):
        center = pivot[:, left : left + TILE]
        total, squares = 0.0, 0.0
        for low in range(0, rows, ROWS):
            apart = value[low : low + ROWS, left : left + TILE] - center
            weighted = apart if kind == 0 else apart * weight[low : low + ROWS]
            total = total + weighted
            squares = squares + weighted * apart
        total = column_sum(total) / count
        means.append(center + total)
        spreads.append(column_sum(squares) - count * jnp.square(total))
    mean, spread = jnp.concatenate(means, axis=1), jnp.concatenate(spreads, axis=1)

    before = packed[:, 2 * channels : 2 * channels + 1]
    part = count / (before + count)
    old = packed[:, here]
    delta = mean - old
    new_mean = old + delta * part
    new_spread = packed[:, there] + spread + jnp.square(delta) * (before * part)
    if kind == 0:
        new_mean = jnp.where(i == 0, mean, new_mean)
        new_spread = jnp.where(i == 0, spread, new_spread)
    packed[:, here] = new_mean
    packed[:, there] = new_spread
    return count


def add_count(i, kind, packed, count):
    channels = (packed.shape[1] - LANES) // 2
    lanes = slice(2 * channels, 2 * channels + LANES)
    wide_count = jnp.broadcast_to(count, (1, LANES))

    total = packed[:, lanes] + wide_count
    packed[:, lanes] = jnp.where(i == 0, wide_count, total) if kind == 0 else total


def add_sums(i, kind, packed, low, high, start):
    channels = (packed.shape[1] - LANES) // 2
    width = low.shape[1]
    here = slice(start, start + width)
    there = slice(channels + start, channels + start + width)

    new_low, new_high = packed[:, here] + low, packed[:, there] + high
    if kind == 0:
        new_low = jnp.where(i == 0, low, new_low)
        new_high = jnp.where(i == 0, high, new_high)
    packed[:, here] = new_low
    packed[:, there] = new_high
    if start == 0:
        packed[:, 2 * channels :] = jnp.zeros((1, LANES), FLOAT)


def reduce_stage(rows, inputs, weight, live):
    mid = weight.shape[1]

    def body(i, kind, given, fixed, made, totals):
        value = product(given[0][...], fixed[0][...])
        made[0][...] = value
        count = add_norm(i, kind, totals[0], value, fixed[1][...], 0)
        add_count(i, kind, totals[0], count)

    return rows.run(
        body,
        [inputs, weight, live],
        [(mid, FLOAT)],
        [(1, 2 * mid + LANES)],
        2 * rows.total() * weight.size,
        streamed=[0],
    )


def norm_kernel(crops, big, small, live, packed):
    channels = big.shape[1]
    weights = [None] + [live[low : low + ROWS, :] for low in range(0, crops, ROWS)]
    big_steps, small_steps = big.shape[0] // ROWS, small.shape[0] // crops

    def gather(value_of):
        def fold(value):
            return jnp.sum(value.reshape(-1, 8, channels), axis=0)

        def step(p, total):
            return total + fold(value_of(big[pl.ds(p * ROWS, ROWS), :]))

        total = lax.fori_loop(0, big_steps, step, jnp.zeros((8, channels), FLOAT), unroll=7)
        for k, weight in enumerate(weights[1:]):

            def step(p, part):
                return part + value_of(small[pl.ds(p * crops + k * ROWS, ROWS), :])

            part = lax.fori_loop(
                0, small_steps, step, jnp.zeros((ROWS, channels), FLOAT), unroll=True
            )
            total = total + fold(part * weight)
        return column_sum(total)

    count = big.shape[0] + small_steps * column_sum(live[:crops, :])
    mean = gather(lambda value: value) / count
    packed[:, :channels] = mean
    packed[:, channels : 2 * channels] = gather(lambda value: jnp.square(value - mean))
    packed[:, 2 * channels :] = jnp.broadcast_to(count, (1, LANES))


def norm_stage(rows, value, live):
    return call(
        lambda *refs: norm_kernel(rows.crops[1], *refs),
        shape((1, 2 * value[0].shape[1] + LANES)),
        [*value, live],
    )


def expand_stage(rows, second, scale, offset, weight, live):
    mid, wide = weight.shape

    def body(i, kind, given, fixed, made, totals):
        scale, offset, weight, live = fixed
        active = silu(given[0][...] * scale[...] + offset[...]).astype(HALF)
        made[1][...] = active
        for start in range(0, wide, CHUNK):
            columns = slice(start, start + CHUNK)
            value = product(active, weight[:, columns])
            made[0][:, columns] = value.astype(HALF)
            count = add_norm(i, kind, totals[0], value, live[...], start)
        add_count(i, kind, totals[0], count)

    return rows.run(
        body,
        [second, scale, offset, weight, live],
        [(wide, HALF, far_shape), (mid, HALF)],
        [(1, 2 * wide + LANES)],
        2 * rows.total() * weight.size,
    )


def pool_stage(rows, third, inputs, scale, offset):
    wide = scale.shape[1]

    def body(i, kind, given, fixed, made, totals):
        scale, offset = fixed
        steps, crops = rows.steps[kind], rows.crops[kind]
        step = i if kind == 0 else i - rows.steps[0]
        out = totals[kind]

        @pl.when(step == 0)
        def _():
            out[...] = jnp.zeros(out.shape, FLOAT)

        for start in range(0, wide, TILE):
            columns = slice(start, start + TILE)
            factor, shift = scale[:, columns], offset[:, columns]
            for low in range(0, crops, ROWS):
                total = out[low : low + ROWS, columns]
                for place in range(steps):
                    here = slice(place * crops + low, place * crops + low + ROWS)
                    residual = given[0][here, columns].astype(FLOAT) * factor + shift
                    residual = residual + given[1][here, columns].astype(FLOAT)
                    half = 0.5 * residual
                    total = total + (half * jnp.tanh(half) + half)
                out[low : low + ROWS, columns] = total

        @pl.when(step == steps - 1)
        def _():
            out[...] = out[...] * (1.0 / (steps * steps))

    return rows.run(
        body,
        [third, inputs, scale, offset],
        [],
        [(crops, wide) for crops in rows.crops],
        12 * rows.total() * wide,
        streamed=[0, 1],
    )


def residual_back_stage(rows, third, inputs, grads, scale, offset, mean, root, live, after):
    wide = scale.shape[1]

    def body(i, kind, given, fixed, made, totals):
        scale, offset, mean, root, live = fixed[2:]
        grads, crops = fixed[kind], rows.crops[kind]
        for start in range(0, wide, TILE):
            columns = slice(start, start + TILE)
            factor, shift, center = scale[:, columns], offset[:, columns], mean[:, columns]
            lows, highs = 0.0, 0.0
            for low in range(0, crops, ROWS):
                spread = grads[low : low + ROWS, columns]
                total, product_total = 0.0, 0.0
                for place in range(rows.steps[kind]):
                    here = slice(place * crops + low, place * crops + low + ROWS)
                    value = given[0][here, columns].astype(FLOAT)
                    residual = value * factor + shift + given[1][here, columns].astype(FLOAT)
                    grad = slope(residual) * spread
                    made[0][here, columns] = grad.astype(HALF)
                    total = total + grad
                    product_total = product_total + grad * (value - center)
                if kind == 1:
                    weight = live[low : low + ROWS, :]
                    total, product_total = total * weight, product_total * weight
                lows, highs = lows + column_sum(total), highs + column_sum(product_total)
            add_sums(i, kind, totals[0], lows, highs * root[:, columns], start)

    return rows.run(
        body,
        [third, inputs, *grads, scale, offset, mean, root, live],
        [(wide, HALF, far_shape)],
        [(1, 2 * wide + LANES)],
        16 * rows.total() * wide,
        after,
        streamed=[0, 1],
    )


def expand_back_stage(rows, grad, third, second, back, weight, norm, live, after):
    mid, wide = weight.shape

    def body(i, kind, given, fixed, made, totals):
        first, second, third, weight, scale, offset, mean, root, live = fixed
        total = jnp.zeros((rows.rows[kind], mid), FLOAT)
        for start in range(0, wide, CHUNK):
            columns = slice(start, start + CHUNK)
            value = (
                given[0][:, columns].astype(FLOAT) * first[:, columns]
                + given[1][:, columns].astype(FLOAT) * third[:, columns]
                + second[:, columns]
            )
            if kind == 1:
                value = value * live[...]
            value = value.astype(HALF)
            made[0][:, columns] = value
            total = total + product_outer(value, weight[:, columns])
        before = given[2][...]
        total = total * slope(before * scale[...] + offset[...])
        made[1][...] = total
        if kind == 1:
            total = total * live[...]
        high = column_sum(total * (before - mean[...])) * root[...]
        add_sums(i, kind, totals[0], column_sum(total), high, 0)

    return rows.run(
        body,
        [grad, third, second, *back, weight, *norm, live],
        [(wide, HALF, far_shape), (mid, FLOAT)],
        [(1, 2 * mid + LANES)],
        2 * rows.total() * weight.size,
        after,
        streamed=[0, 1],
    )


def slope_stage(rows, grad, value, norm, live, after):
    mid = grad[0].shape[1]

    def body(i, kind, given, fixed, made, totals):
        scale, offset, mean, root, live = fixed
        before = given[1][...]
        total = given[0][...] * slope(before * scale[...] + offset[...])
        made[0][...] = total
        if kind == 1:
            total = total * live[...]
        high = column_sum(total * (before - mean[...])) * root[...]
        add_sums(i, kind, totals[0], column_sum(total), high, 0)

    return rows.run(
        body,
        [grad, value, *norm, live],
        [(mid, FLOAT)],
        [(1, 2 * mid + LANES)],
        16 * rows.total() * mid,
        after,
    )


def norm_back_stage(rows, grad, value, back, live, after):
    mid = grad[0].shape[1]

    def body(i, kind, given, fixed, made, totals):
        first, second, third, live = fixed
        total = given[0][...] * first[...] + given[1][...] * third[...] + second[...]
        if kind == 1:
            total = total * live[...]
        made[0][...] = total.astype(HALF)

    return rows.run(
        body, [grad, value, *back, live], [(mid, HALF)], [], 6 * rows.total() * mid, after
    )[0]


def input_grad_stage(rows, grad, first, weight, after):
    wide, mid = weight.shape

    def body(i, kind, given, fixed, made, totals):
        first = given[1][...]
        for start in range(0, wide, CHUNK):
            columns = slice(start, start + CHUNK)
            value = product_outer(first, fixed[0][columns, :])
            made[0][:, columns] = (value + given[0][:, columns].astype(FLOAT)).astype(HALF)

    return rows.run(
        body,
        [grad, first, weight],
        [(wide, HALF, far_shape)],
        [],
        2 * rows.total() * weight.size,
        after,
        streamed=[0],
    )[0]


def hidden_kernel(big, small, weight, live, out, packed):
    j = pl.program_id(0)
    channels = (packed.shape[1] - LANES) // 2
    pooled = jnp.concatenate([big[...].astype(HALF), small[...].astype(HALF)])
    value = product(pooled, weight[...])
    out[...] = value
    count = column_sum(live[...])
    mean = column_sum(value * live[...]) / count
    spread = column_sum(jnp.square(value - mean) * live[...])
    packed[:, pl.ds(pl.multiple_of(j * CHUNK, CHUNK), CHUNK)] = mean
    packed[:, pl.ds(pl.multiple_of(channels + j * CHUNK, CHUNK), CHUNK)] = spread
    packed[:, 2 * channels :] = jnp.broadcast_to(count, (1, LANES))


def hidden_stage(big, small, weight, live):
    crops = live.shape[0]
    wide, channels = weight.shape
    return call(
        hidden_kernel,
        [shape((crops, channels)), shape((1, 2 * channels + LANES))],
        [big, small, weight, live],
        grid=(channels // CHUNK,),
        in_specs=[
            whole(big.shape),
            whole(small.shape),
            pl.BlockSpec((wide, CHUNK), lambda j: (0, j)),
            whole(live.shape),
        ],
        out_specs=[
            pl.BlockSpec((crops, CHUNK), lambda j: (0, j)),
            whole((1, 2 * channels + LANES)),
        ],
        flops=2 * crops * weight.size,
        streamed=[2],
    )


def lanes_of(dims):
    return lax.broadcasted_iota(jnp.int32, dims, 1)


def sums_by_view(batch, stored, views):
    row = lax.broadcasted_iota(jnp.int32, batch.shape, 0) % views
    size = stored.shape[0] // views
    return jnp.concatenate(
        [
            column_sum(jnp.where(row == v, batch, 0.0))
            + column_sum(stored[v * size : (v + 1) * size])
            for v in range(views)
        ],
        axis=1,
    )


def queue_kernel(proto, views, queue, prototypes, stored):
    rows = queue.shape[0] // views
    value = queue[...].astype(FLOAT)
    unit = value * lax.rsqrt(jnp.sum(value * value, axis=1, keepdims=True) + EPS_UNIT)
    scores = product_outer(unit.astype(HALF), prototypes[...])
    value = jnp.where(lanes_of(scores.shape) < proto, jnp.exp(scores / EPS_CODE), 0.0)
    size = stored.shape[0] // views
    stored[...] = jnp.zeros(stored.shape, FLOAT)
    for v in range(views):
        stored[v * size : v * size + rows, :] = value[v * rows : (v + 1) * rows]


def score_kernel(
    proto, views, big_rows, hidden, scale, offset, project, prototypes, stored,
    active_out, embedded_out, unit_out, scores_out, batch_out, sums,
):
    active = silu(hidden[...] * scale[...] + offset[...]).astype(HALF)
    active_out[...] = active
    embedded = product(active, project[...])
    embedded_out[...] = embedded
    root = lax.rsqrt(jnp.sum(embedded * embedded, axis=1, keepdims=True) + EPS_UNIT)
    unit = (embedded * root).astype(HALF)
    unit_out[...] = unit
    scores = product_outer(unit, prototypes[...])
    scores_out[...] = scores
    batch = scores[:big_rows]
    batch = jnp.where(lanes_of(batch.shape) < proto, jnp.exp(batch / EPS_CODE), 0.0)
    batch_out[...] = batch
    sums[...] = sums_by_view(batch, stored[...], views)


def balanced(proto, views, parts, batch, stored):
    totals = tree([part[...] for part in parts])
    width = batch.shape[1]
    totals = [totals[:, v * width : (v + 1) * width] for v in range(views)]
    totals = [jnp.where(lanes_of(t.shape) < proto, t, 1.0) for t in totals]
    row = lax.broadcasted_iota(jnp.int32, batch.shape, 0) % views
    own = jnp.zeros(batch.shape, FLOAT)
    for v in range(views):
        own = jnp.where(row == v, totals[v], own)
    batch = batch / own
    batch = batch / jnp.sum(batch, axis=1, keepdims=True)
    if stored is None:
        return batch, None
    size = stored.shape[0] // views
    stored = jnp.concatenate(
        [stored[v * size : (v + 1) * size] / totals[v] for v in range(views)]
    )
    sums = jnp.sum(stored, axis=1, keepdims=True)
    return batch, jnp.where(sums > 0.0, stored / jnp.where(sums > 0.0, sums, 1.0), 0.0)


def balance_kernel(proto, views, *refs):
    *parts, batch, stored, batch_out, stored_out, sums = refs
    batch, stored = balanced(proto, views, parts, batch[...], stored[...])
    batch_out[...] = batch
    stored_out[...] = stored
    sums[...] = sums_by_view(batch, stored, views)


def loss_kernel(proto, views, *refs):
    (
        *parts, batch, scores, share, live, embedded, hidden, scale, offset, mean, root, project, prototypes,
        grad_scores_out, grad_embedded_out, grad_out, packed,
    ) = refs
    codes, _ = balanced(proto, views, parts, batch[...], None)
    big = codes.shape[0]
    images = big // views
    slots = (scores.shape[0] - big) // images
    row = lax.broadcasted_iota(jnp.int32, codes.shape, 0) % views
    others = jnp.zeros(codes.shape, FLOAT)
    for turn in range(1, views):
        ahead = jnp.concatenate([codes[turn:], codes[:turn]])
        behind = jnp.concatenate([codes[turn - views :], codes[: turn - views]])
        others = others + jnp.where(row + turn < views, ahead, behind)
    both = codes + others
    targets = jnp.concatenate(
        [others]
        + [
            jnp.broadcast_to(both[k * views : k * views + 1], (slots, both.shape[1]))
            for k in range(images)
        ]
    )
    lanes = lanes_of(scores.shape)
    logits = jnp.where(lanes < proto, scores[...] / SOFTMAX_HEAT, -1e30)
    top = jnp.max(logits, axis=1, keepdims=True)
    powers = jnp.where(lanes < proto, jnp.exp(logits - top), 0.0)
    sums = jnp.sum(powers, axis=1, keepdims=True)
    logs = jnp.where(lanes < proto, logits - top - jnp.log(sums), 0.0)
    loss = -column_sum(jnp.sum(targets * logs, axis=1, keepdims=True) * share[...])
    mass = jnp.sum(targets, axis=1, keepdims=True)
    grad = (share[...] / SOFTMAX_HEAT) * (powers * (mass / sums) - targets)
    grad = grad.astype(HALF)
    grad_scores_out[...] = grad
    grad = product(grad, prototypes[...])
    value = embedded[...]
    scaled = lax.rsqrt(jnp.sum(value * value, axis=1, keepdims=True) + EPS_UNIT)
    unit = value * scaled
    grad = scaled * (grad - unit * jnp.sum(unit * grad, axis=1, keepdims=True))
    grad = grad.astype(HALF)
    grad_embedded_out[...] = grad
    channels = scale.shape[1]
    for start in range(0, channels, CHUNK):
        columns = slice(start, start + CHUNK)
        before = hidden[:, columns]
        part = product_outer(grad, project[columns, :])
        part = part * slope(before * scale[:, columns] + offset[:, columns])
        grad_out[:, columns] = part
        part = part * live[...]
        packed[:, columns] = column_sum(part)
        packed[:, channels + start : channels + start + CHUNK] = (
            column_sum(part * (before - mean[:, columns])) * root[:, columns]
        )
    packed[:, 2 * channels :] = jnp.broadcast_to(loss, (1, LANES))


def pooled_back_kernel(areas, big_rows, grad, hidden, live, first, second, third, weight, grad_out, big, small):
    value = grad[...] * first[...] + hidden[...] * third[...] + second[...]
    value = value * live[...]
    grad_out[...] = value
    part = product_outer(value.astype(HALF), weight[...])
    big[...] = part[:big_rows] / areas[0]
    small[...] = part[big_rows:] / areas[1]


def hidden_grad_kernel(blocks, me, left, right, out, held, sem):
    place = lax.rem(me[0], PLANE)
    width = left.shape[1] // blocks
    per = LANES // width
    planes = blocks // PLANE

    @pl.when(pl.program_id(0) == 0)
    def _():
        copies = []
        for k in range(planes):
            start = pl.multiple_of((k * PLANE + place) // per * LANES, LANES)
            copies.append(
                pltpu.make_async_copy(
                    left.at[:, pl.ds(start, LANES)],
                    held.at[:, pl.ds(k * LANES, LANES)],
                    sem.at[k],
                )
            )
        for copy in copies:
            copy.start()
        for copy in copies:
            copy.wait()

    value = product_inner(held[...].astype(HALF), right[...].astype(HALF))
    part = lax.rem(place, per)
    for k in range(planes):
        chosen = value[k * LANES : k * LANES + width]
        for other in range(1, per):
            start = k * LANES + other * width
            chosen = jnp.where(part == other, value[start : start + width], chosen)
        out[k * width : (k + 1) * width, :] = chosen


def hidden_grad_stage(left, right, devices, me, after):
    crops, height = left.shape
    width = right.shape[1]
    planes = devices // PLANE
    return call(
        lambda *refs: hidden_grad_kernel(devices, *refs),
        shape((height // PLANE, width)),
        [left, right],
        grid=(width // CHUNK,),
        in_specs=[
            pl.BlockSpec(memory_space=pl.ANY),
            pl.BlockSpec((crops, CHUNK), lambda j: (0, j)),
        ],
        out_specs=pl.BlockSpec((height // PLANE, CHUNK), lambda j: (0, j)),
        flops=2 * crops * height // PLANE * width,
        streamed=[0, 1],
        after=after,
        scalars=[me],
        scratch=[
            pltpu.VMEM((crops, planes * LANES), FLOAT),
            pltpu.SemaphoreType.DMA((planes,)),
        ],
    )


def head_grad_kernel(devices, active, grad_embedded, unit, grad_scores, out):
    project = product_inner(active[...], grad_embedded[...])
    proto = product_inner(unit[...], grad_scores[...])
    rows, lines = project.shape[0] // devices, proto.shape[0] // devices
    for k in range(devices):
        place = k % PLANE * (devices // PLANE) + k // PLANE
        half = rows // 2
        for part in range(2):
            start = k * rows + part * half
            out[place, :half, part * LANES : (part + 1) * LANES] = project[start : start + half]
        for part in range(proto.shape[1] // TILE):
            start = half + part * lines
            out[place, start : start + lines, :] = proto[
                k * lines : (k + 1) * lines, part * TILE : (part + 1) * TILE
            ]


def head_grad_stage(active, grad_embedded, unit, grad_scores, devices, after):
    rows = active.shape[1] * grad_embedded.shape[1] + unit.shape[1] * grad_scores.shape[1]
    return call(
        lambda *refs: head_grad_kernel(devices, *refs),
        shape((devices, rows // (devices * TILE), TILE)),
        [active, grad_embedded, unit, grad_scores],
        after=after,
    )


def conv(field, weight):
    return lax.conv_general_dilated(
        field,
        weight,
        (1, 1),
        ((1, 1), (1, 1)),
        dimension_numbers=("HWNC", "HWIO", "HWNC"),
        preferred_element_type=FLOAT,
    )


def conv_back(field, weight):
    return lax.conv_general_dilated(
        field,
        lax.rev(weight, (0, 1)),
        (1, 1),
        ((1, 1), (1, 1)),
        dimension_numbers=("HWNC", "HWOI", "HWNC"),
        preferred_element_type=FLOAT,
    )


def conv_filter(field, grad):
    return lax.conv_general_dilated(
        field,
        grad,
        (1, 1),
        ((1, 1), (1, 1)),
        dimension_numbers=("HWCN", "HWIO", "HWNC"),
        preferred_element_type=FLOAT,
    )


def local(
    big_crops,
    small_crops,
    small_count,
    w_reduce,
    w_spatial,
    w_expand,
    gain_mid,
    bias_mid,
    gain_wide,
    bias_wide,
    w_hidden,
    gain_head,
    bias_head,
    w_project,
    prototypes,
    queue,
):
    devices = lax.axis_size("dp")
    image_rows = small_count.shape[0]
    images = image_rows * devices
    big_rows, big_side = big_crops.shape[:2]
    small_rows, small_side = small_crops.shape[:2]
    views = big_rows // image_rows
    slots = small_rows // image_rows
    wide = big_crops.shape[3]
    mid = w_reduce.shape[1]
    hid = w_hidden.shape[1]
    proj, proto = prototypes.shape
    proto_wide = -(-proto // CHUNK) * CHUNK
    crops = big_rows + small_rows
    areas = (big_side * big_side, small_side * small_side)
    rows = Rows(big_side, big_rows, small_side, small_rows)
    sides = ((big_side, big_side, big_rows), (small_side, small_side, small_rows))
    planes = [[k * PLANE + j for j in range(PLANE)] for k in range(devices // PLANE)]
    stacks = [[k * PLANE + j for k in range(devices // PLANE)] for j in range(PLANE)]
    me = lax.axis_index("dp").astype(jnp.int32).reshape(1)

    slot_mask = (jnp.arange(slots)[None, :] < small_count[:, None]).astype(FLOAT)
    slot_flags = slot_mask.reshape(-1)
    live = jnp.tile(slot_flags, small_side)[:, None]
    crop_live = jnp.concatenate([jnp.ones((big_rows,), FLOAT), slot_flags])[:, None]
    share = 1.0 / (images * views * (views - 1.0 + small_count.astype(FLOAT)))
    share = jnp.concatenate(
        [jnp.repeat(share, views), jnp.repeat(share, slots) * slot_flags]
    )[:, None]

    def fields(pair):
        return [a.reshape(*s, a.shape[-1]) for a, s in zip(pair, sides)]

    def flat(pair):
        return tuple(a.reshape(-1, a.shape[-1]) for a in pair)

    inputs = flat((jnp.transpose(big_crops, (1, 2, 0, 3)), jnp.transpose(small_crops, (1, 2, 0, 3))))
    taps = jnp.transpose(w_spatial, (1, 0, 2))
    filters = taps.reshape(3, 3, mid, mid)
    lines = jnp.pad(jnp.transpose(prototypes), ((0, proto_wide - proto), (0, 0)))

    first, packed = reduce_stage(rows, inputs, w_reduce, live)
    scale_one, offset_one, mean_one, root_one, pixel_count = settle_norm(
        packed, gain_mid[0], bias_mid[0], devices
    )
    mid_one = fields([silu(a * scale_one + offset_one).astype(HALF) for a in first])
    second = flat([conv(a, filters) for a in mid_one])
    packed = norm_stage(rows, second, live)
    scale_two, offset_two, mean_two, root_two, _ = settle_norm(
        packed, gain_mid[1], bias_mid[1], devices
    )
    third, mid_two, packed = expand_stage(rows, second, scale_two, offset_two, w_expand, live)
    scale_three, offset_three, mean_three, root_three, _ = settle_norm(
        packed, gain_wide, bias_wide, devices
    )
    pooled_big, pooled_small = pool_stage(rows, third, inputs, scale_three, offset_three)

    hidden, packed = hidden_stage(pooled_big, pooled_small, w_hidden, crop_live)
    scale_head, offset_head, mean_head, root_head, crop_count = settle_norm(
        packed, gain_head, bias_head, devices
    )
    plane_pooled = lax.all_gather(
        jnp.concatenate([pooled_big, pooled_small]), "dp", axis_index_groups=planes, tiled=True
    )
    stored_rows = views * (-(-queue.shape[1] // 8) * 8)
    stored = call(
        lambda *refs: queue_kernel(proto, views, *refs),
        shape((stored_rows, proto_wide)),
        [queue.reshape(-1, proj), lines],
    )
    active, embedded, unit, scores, batch, sums = call(
        lambda *refs: score_kernel(proto, views, big_rows, *refs),
        [
            shape((crops, hid), HALF),
            shape((crops, proj)),
            shape((crops, proj), HALF),
            shape((crops, proto_wide)),
            shape((big_rows, proto_wide)),
            shape((1, views * proto_wide)),
        ],
        [hidden, scale_head, offset_head, w_project, lines, stored],
    )
    for step in range(ITERS - 1):
        batch, stored, sums = call(
            lambda *refs: balance_kernel(proto, views, *refs),
            [shape(batch.shape), shape(stored.shape), shape(sums.shape)],
            [*sum_parts(sums, devices), batch, stored],
            )

    loss_outs = [
        shape((crops, proto_wide), HALF),
        shape((crops, proj), HALF),
        shape((crops, hid)),
        shape((1, 2 * hid + LANES)),
    ]
    parts = sum_parts(sums, devices)
    loss_args = [
        batch,
        scores,
        share,
        crop_live,
        embedded,
        hidden,
        scale_head,
        offset_head,
        mean_head,
        root_head,
        w_project,
        lines,
    ]
    grad_scores, grad_embedded, grad_active, packed = call(
        lambda *refs: loss_kernel(proto, views, *refs),
        loss_outs,
        [*parts, *loss_args],
        grid=(1,),
        in_specs=[whole(a.shape) for a in (*parts, *loss_args)],
        out_specs=[whole(a.shape) for a in loss_outs],
        streamed=range(len(parts), len(parts) + len(loss_args)),
    )
    made = {}

    def head_work(mark):
        made["head"] = head_grad_stage(
            active, grad_embedded, unit, grad_scores, devices, [mark]
        )
        return [Far(made["head"])]

    *back, gain_head_grad, bias_head_grad, loss = settle_back(
        packed, gain_head, mean_head, root_head, crop_count, devices, [head_work]
    )
    grad_hidden, *grad_pooled = call(
        lambda *refs: pooled_back_kernel(areas, big_rows, *refs),
        [shape((crops, hid)), shape((big_rows, wide)), shape((small_rows, wide))],
        [grad_active, hidden, crop_live, *back, w_hidden],
        grid=(wide // CHUNK,),
        in_specs=[
            whole((crops, hid)),
            whole((crops, hid)),
            whole((crops, 1)),
            whole((1, hid)),
            whole((1, hid)),
            whole((1, hid)),
            pl.BlockSpec((CHUNK, hid), lambda j: (j, 0)),
        ],
        out_specs=[
            whole((crops, hid)),
            pl.BlockSpec((big_rows, CHUNK), lambda j: (0, j)),
            pl.BlockSpec((small_rows, CHUNK), lambda j: (0, j)),
        ],
        flops=2 * crops * w_hidden.size,
        streamed=[6],
    )
    plane_grad = lax.all_gather(grad_hidden, "dp", axis_index_groups=planes, tiled=True)

    grad_residual, packed = residual_back_stage(
        rows,
        third,
        inputs,
        grad_pooled,
        scale_three,
        offset_three,
        mean_three,
        root_three,
        live,
        [],
    )
    *back, gain_three, bias_three, _ = settle_back(
        packed, gain_wide, mean_three, root_three, pixel_count, devices
    )
    grad_third, grad_two, packed = expand_back_stage(
        rows,
        grad_residual,
        third,
        second,
        back,
        w_expand,
        [scale_two, offset_two, mean_two, root_two],
        live,
        [],
    )

    def expand_work(mark):
        made["expand"] = weight_grad(mid_two, grad_third, devices, me, 1, [mark], [1, 3])
        return [made["expand"][0]]

    def hidden_work(mark):
        made["hidden"] = hidden_grad_stage(plane_pooled, plane_grad, devices, me, [mark])
        return [made["hidden"]]

    *back, gain_two, bias_two, _ = settle_back(
        packed,
        gain_mid[1],
        mean_two,
        root_two,
        pixel_count,
        devices,
        [expand_work, hidden_work],
    )
    expand_sum = Scatter(*made["expand"], devices, me)
    hidden_grad = lax.psum_scatter(
        made["hidden"], "dp", scatter_dimension=0, axis_index_groups=stacks, tiled=True
    )
    head_part = lax.psum_scatter(
        made["head"], "dp", scatter_dimension=0, axis_index_groups=planes, tiled=True
    )
    head_grad = lax.psum_scatter(
        head_part, "dp", scatter_dimension=0, axis_index_groups=stacks, tiled=True
    )
    grad_second = norm_back_stage(
        rows, grad_two, second, back, live, [expand_sum.go([back[0]])]
    )
    grad_mid_one = flat([conv_back(a, filters) for a in fields(grad_second)])
    grad_one, packed = slope_stage(
        rows,
        grad_mid_one,
        first,
        [scale_one, offset_one, mean_one, root_one],
        live,
        [*expand_sum.got, Far(head_part)],
    )

    def big_work(mark):
        grad = tie(grad_second[0], [mark])
        made["big"] = conv_filter(mid_one[0], fields((grad, grad_second[1]))[0])
        return [made["big"]]

    def small_work(mark):
        grad = tie(grad_second[1], [mark])
        part = made["big"] + conv_filter(mid_one[1], fields((grad_second[0], grad))[1])
        made["spatial"] = part.reshape(9, devices, mid // devices, mid)
        made["send"] = send_rows(made["spatial"], me, [])
        return [Far(made["send"])]

    *back, gain_one, bias_one, _ = settle_back(
        packed,
        gain_mid[0],
        mean_one,
        root_one,
        pixel_count,
        devices,
        [big_work, small_work],
    )
    spatial_sum = Scatter(made["spatial"], made["send"], devices, me)
    mark = expand_sum.go([back[0]])
    grad_first = norm_back_stage(rows, grad_one, first, back, live, [mark])
    reduce_keep, reduce_send = weight_grad(inputs, grad_first, devices, me, 0, (), [0, 2])
    mark = spatial_sum.go([reduce_keep, *expand_sum.got])
    reduce_sum = Scatter(reduce_keep, tie(reduce_send, [mark]), devices, me)
    mark = expand_sum.go([mark])
    grad_inputs = input_grad_stage(
        rows, grad_residual, grad_first, w_reduce, [mark]
    )
    head_grad = head_grad[0]
    grad_big, grad_small = fields(grad_inputs)
    mark = expand_sum.go([Far(grad_inputs[0])])
    for part in (spatial_sum, reduce_sum) * 4:
        if not part.complete():
            mark = part.go([mark])
    ends = w_project.shape[0] // (2 * devices)
    project_grad = jnp.concatenate([head_grad[:ends, :LANES], head_grad[:ends, LANES:]])
    proto_grad = head_grad[ends:].reshape(-1, proj // devices, TILE)
    proto_grad = jnp.transpose(proto_grad, (1, 0, 2)).reshape(proj // devices, -1)[:, :proto]
    expand_grad = expand_sum.end()[0]
    spatial_grad = spatial_sum.end()
    reduce_grad = reduce_sum.end()[0]
    return (
        loss[0, 0],
        jnp.transpose(grad_big, (2, 0, 1, 3)),
        jnp.transpose(grad_small, (2, 0, 1, 3)),
        reduce_grad,
        jnp.transpose(spatial_grad, (1, 0, 2)),
        expand_grad,
        jnp.concatenate([gain_one, gain_two]),
        jnp.concatenate([bias_one, bias_two]),
        gain_three[0],
        bias_three[0],
        hidden_grad,
        gain_head_grad[0],
        bias_head_grad[0],
        project_grad,
        proto_grad,
    )


def solution(mesh):
    placed = (
        P("dp", None, None, None),
        P("dp", None, None, None),
        P("dp"),
        P(),
        P(),
        P(),
        P(),
        P(),
        P(),
        P(),
        P(),
        P(),
        P(),
        P(),
        P(),
        P(None, "dp", None),
    )
    return jax.shard_map(
        local,
        mesh=mesh,
        in_specs=placed,
        out_specs=(
            P(),
            P("dp", None, None, None),
            P("dp", None, None, None),
            P("dp", None),
            P("dp", None, None),
            P("dp", None),
            P(),
            P(),
            P(),
            P(),
            P("dp", None),
            P(),
            P(),
            P("dp", None),
            P("dp", None),
        ),
        check_vma=False,
    )
```

```python
import math

import jax
import jax.numpy as jnp
from jax import lax
from jax.experimental import pallas as pl
from jax.experimental.pallas import tpu as pltpu
from jax.sharding import PartitionSpec as P

ITERS = 3

EPS_NORM = 1e-05
EPS_UNIT = 1e-06
EPS_CODE = 0.05
SOFTMAX_HEAT = 0.1
LANES = 128
PLANE = 8
CHUNK = 512
TILE = 256
ROWS = 32
VMEM_LIMIT = 60 << 20
GRID_LIMIT = 16 << 20
SLOTS = 3
FLOAT = jnp.float32
HALF = jnp.bfloat16


def product(left, right):
    return jnp.dot(left, right, preferred_element_type=FLOAT)


def product_inner(left, right):
    return lax.dot_general(left, right, (((0,), (0,)), ((), ())), preferred_element_type=FLOAT)


def product_outer(left, right):
    return lax.dot_general(left, right, (((1,), (1,)), ((), ())), preferred_element_type=FLOAT)


def sigmoid(value):
    return 0.5 * jnp.tanh(0.5 * value) + 0.5


def silu(value):
    return value * sigmoid(value)


def slope(value):
    gate = sigmoid(value)
    return gate * (1.0 + value * (1.0 - gate))


def column_sum(value):
    return jnp.sum(value, axis=0, keepdims=True)


def shape(dims, dtype=FLOAT):
    return jax.ShapeDtypeStruct(dims, dtype)


def far_shape(dims, dtype=FLOAT):
    return pltpu.HBM(dims, dtype)


def far(array):
    return pltpu.with_memory_space_constraint(array, pltpu.HBM)


def whole(dims):
    return pl.BlockSpec(dims, lambda *_: (0,) * len(dims))


class Far:
    def __init__(self, array):
        self.array = array


def call(
    kernel,
    out_shape,
    args,
    grid=None,
    in_specs=None,
    out_specs=None,
    flops=0,
    after=(),
    scalars=(),
    streamed=(),
    scratch=(),
):
    flat = out_shape if isinstance(out_shape, (list, tuple)) else [out_shape]
    size = sum(a.size * a.dtype.itemsize for a in args)
    size += sum(math.prod(a.shape) * jnp.dtype(a.dtype).itemsize for a in flat)
    args = [far(a) if k in streamed else a for k, a in enumerate(args)]
    here = pl.BlockSpec(memory_space=pltpu.VMEM)
    limit = 0
    if grid is None:
        in_specs = [here] * len(args)
        out_specs = jax.tree.map(lambda _: here, out_shape)
        limit = max(limit, size + size // 4 + (2 << 20))
    else:
        limit = GRID_LIMIT + sum(
            math.prod(a.shape) * jnp.dtype(a.dtype).itemsize for a in scratch[:-1]
        )
    limit += sum(a.size * a.dtype.itemsize for a in after if not isinstance(a, Far))
    first, last = len(scalars), len(scalars) + len(args)

    def run(*refs):
        kernel(*refs[:last], *refs[last + len(after) :])

    specs = dict(out_specs=out_specs)
    if grid is not None:
        specs["grid"] = grid
    return pl.pallas_call(
        run,
        out_shape=out_shape,
        in_specs=[pl.BlockSpec(memory_space=pltpu.SMEM)] * first
        + list(in_specs)
        + [pl.BlockSpec(memory_space=pl.ANY if isinstance(a, Far) else pltpu.VMEM) for a in after],
        scratch_shapes=list(scratch),
        compiler_params=pltpu.CompilerParams(vmem_limit_bytes=min(limit, VMEM_LIMIT)),
        cost_estimate=pl.CostEstimate(flops=1, bytes_accessed=1, transcendentals=0),
        **specs,
    )(*scalars, *args, *(a.array if isinstance(a, Far) else a for a in after))


def copy_kernel(source, out):
    out[...] = source[...]


def tie(value, after):
    return call(copy_kernel, shape(value.shape, value.dtype), [value], after=after)


def rounds(devices):
    bits = [1 << k for k in range(devices.bit_length() - 1)]
    return [bits[:1]] + [bits[k : k + 2] for k in range(1, len(bits), 2)]


def peers(value, bits, devices):
    masks = [0]
    for bit in bits:
        masks = masks + [mask | bit for mask in masks]
    return [value] + [
        lax.ppermute(value, "dp", [(i, i ^ mask) for i in range(devices)]) for mask in masks[1:]
    ]


def tree(values):
    while len(values) > 1:
        values = [values[k] + values[k + 1] for k in range(0, len(values), 2)]
    return values[0]


def exchange(value, devices, merge, works=()):
    first, *others = rounds(devices)
    parts = peers(value, first, devices)
    for k, bits in enumerate(others):
        value = merge(parts)
        parts = peers(value, bits, devices)
        if k < len(works):
            parts[0] = tie(value, works[k](value))
    return parts


def sum_parts(value, devices, works=()):
    return exchange(value, devices, tree, works)


def merged(parts):
    channels = (parts[0].shape[1] - LANES) // 2
    counts = [part[:, 2 * channels : 2 * channels + 1] for part in parts]
    means = [part[:, :channels] for part in parts]
    spreads = [part[:, channels : 2 * channels] for part in parts]
    total = tree(counts)
    mean = tree([c * m for c, m in zip(counts, means)]) / total
    spread = tree([s + c * jnp.square(m - mean) for s, c, m in zip(spreads, counts, means)])
    return total, mean, spread


def merge_kernel(*refs):
    *parts, out = refs
    channels = (out.shape[1] - LANES) // 2
    total, mean, spread = merged([part[...] for part in parts])
    out[:, :channels] = mean
    out[:, channels : 2 * channels] = spread
    out[:, 2 * channels :] = jnp.broadcast_to(total, (1, LANES))


def merge_norms(parts):
    return call(merge_kernel, shape(parts[0].shape), parts)


def settle_kernel(*refs):
    *parts, gain, bias, scale, offset, mean_out, root_out, count = refs
    total, mean, spread = merged([part[...] for part in parts])
    root = lax.rsqrt(spread / total + EPS_NORM)
    factor = gain[...] * root
    scale[...] = factor
    offset[...] = bias[...] - mean * factor
    mean_out[...] = mean
    root_out[...] = root
    count[...] = jnp.broadcast_to(total, (1, LANES))


def settle_norm(packed, gain, bias, devices):
    channels = gain.shape[0]
    parts = exchange(packed, devices, merge_norms)
    row = shape((1, channels))
    return call(
        settle_kernel,
        [row, row, row, row, shape((1, LANES))],
        [*parts, gain[None], bias[None]],
    )


def settle_back_kernel(*refs):
    *parts, gain, mean, root, count, first, second, third, gain_sum, bias_sum, extra = refs
    channels = gain.shape[1]
    packed = tree([part[...] for part in parts])
    total = count[:, :1]
    low, high = packed[:, :channels], packed[:, channels : 2 * channels]
    factor = gain[...] * root[...]
    pull = root[...] * high / total
    first[...] = factor
    second[...] = factor * (mean[...] * pull - low / total)
    third[...] = -factor * pull
    gain_sum[...] = high
    bias_sum[...] = low
    extra[...] = packed[:, 2 * channels :]


def settle_back(packed, gain, mean, root, count, devices, works=()):
    parts = sum_parts(packed, devices, works)
    row = shape((1, gain.shape[0]))
    return call(
        settle_back_kernel,
        [row, row, row, row, row, shape((1, LANES))],
        [*parts, gain[None], mean, root, count],
    )


def pick(bits, place):
    return (bits[0] >> place) & 1


def send_kernel(bits, value, send):
    other = 1 - pick(bits, 0)

    def step(t, _):
        for k in range(send.shape[1]):
            send[t, k] = value[t, 2 * k + other]
        return _

    lax.fori_loop(0, value.shape[0], step, 0)


def send_rows(value, me, after):
    taps, devices, rows, width = value.shape
    out = shape((taps, devices // 2, rows, width))
    return call(send_kernel, out, [value], scalars=[me], after=after)


def first_kernel(bits, keep, got, keep_one, send_one, keep_two, send_two):
    taps, blocks, _, width = got.shape
    uncut = keep.shape[1] // blocks
    half = pick(bits, 0) * (uncut - 1)
    left, right = slice(0, width // 2), slice(width // 2, width)
    one, two = pick(bits, 1), pick(bits, 2)

    def step(t, _):
        for k in range(blocks // 2):
            for out, there in ((keep_one, 2 * k + one), (send_one, 2 * k + 1 - one)):
                out[t, k] = keep[t, uncut * there + half, :, left] + got[t, there, :, left]
            low = 4 * (k // 2) + k % 2
            for out, there in ((keep_two, low + 2 * two), (send_two, low + 2 * (1 - two))):
                out[t, k] = keep[t, uncut * there + half, :, right] + got[t, there, :, right]
        return _

    lax.fori_loop(0, taps, step, 0)


def second_kernel(bits, keep_one, got_one, keep_two, got_two, *outs):
    def step(t, _):
        for keep, got, place, out_keep, out_send in (
            (keep_one, got_one, 2, outs[0], outs[1]),
            (keep_two, got_two, 1, outs[2], outs[3]),
        ):
            half = pick(bits, place)
            for k in range(out_keep.shape[1]):
                out_keep[t, k] = keep[t, 2 * k + half] + got[t, 2 * k + half]
                out_send[t, k] = keep[t, 2 * k + 1 - half] + got[t, 2 * k + 1 - half]
        return _

    lax.fori_loop(0, keep_one.shape[0], step, 0)


def third_kernel(bits, keep_one, got_one, keep_two, got_two, out_keep, out_send):
    half = pick(bits, 3)
    width = keep_one.shape[3]

    def step(t, _):
        for k in range(out_keep.shape[1]):
            for out, there in ((out_keep, 2 * k + half), (out_send, 2 * k + 1 - half)):
                out[t, k, :, :width] = keep_one[t, there] + got_one[t, there]
                out[t, k, :, width:] = keep_two[t, there] + got_two[t, there]
        return _

    lax.fori_loop(0, keep_one.shape[0], step, 0)


def later_kernel(place, bits, keep, got, out_keep, out_send):
    half = pick(bits, place)

    def step(t, _):
        for k in range(out_keep.shape[1]):
            for out, there in ((out_keep, 2 * k + half), (out_send, 2 * k + 1 - half)):
                out[t, k] = keep[t, there] + got[t, there]
        return _

    lax.fori_loop(0, keep.shape[0], step, 0)


def last_kernel(keep, got, out):
    out[...] = keep[...] + got[...]


class Scatter:
    def __init__(self, keep, send, devices, me):
        self.devices, self.me = devices, me
        self.bits = devices.bit_length() - 1
        self.held = [keep]
        self.got = [self.cross(send, 0)]
        self.stage = 0

    def cross(self, value, place):
        return lax.ppermute(
            value, "dp", [(i, i ^ (1 << place)) for i in range(self.devices)]
        )

    def go(self, after=()):
        taps, blocks, rows, width = self.got[0].shape
        if self.stage == 0:
            out = shape((taps, blocks // 2, rows, width // 2))
            kernel, places = first_kernel, (1, 2)
        elif self.stage == 1:
            out = shape((taps, blocks // 2, rows, width))
            kernel, places = second_kernel, (2, 1)
        elif self.stage == 2:
            out = shape((taps, blocks // 2, rows, 2 * width))
            kernel, places = third_kernel, (3,)
        else:
            place = self.stage + 1
            out = shape((taps, blocks // 2, rows, width))
            kernel, places = (lambda *refs: later_kernel(place, *refs)), (place,)
        args = [a for pair in zip(self.held, self.got) for a in pair]
        made = call(kernel, [out] * (2 * len(places)), args, after=after, scalars=[self.me])
        self.held = list(made[::2])
        self.got = [self.cross(send, place) for send, place in zip(made[1::2], places)]
        self.stage += 1
        return self.held[0]

    def complete(self):
        return self.got[0].shape[1] == 1

    def end(self):
        while not self.complete():
            self.go()
        taps, _, rows, width = self.held[0].shape
        done = call(last_kernel, shape(self.held[0].shape), [self.held[0], self.got[0]])
        return done.reshape(taps, rows, width)


def weight_grad_kernel(rows, bits, left_big, right_big, left_small, right_small, keep, send):
    value = product_inner(left_big[...], right_big[...])
    value = value + product_inner(left_small[...], right_small[...])
    half = pick(bits, 0)
    for k in range(value.shape[0] // (2 * rows)):
        even = value[2 * k * rows : (2 * k + 1) * rows]
        odd = value[(2 * k + 1) * rows : (2 * k + 2) * rows]
        keep[0, k] = jnp.where(half == 0, even, odd)
        send[0, k] = jnp.where(half == 0, odd, even)


def weight_grad(left, right, devices, me, along, after=(), streamed=()):
    height, width = left[0].shape[1], right[0].shape[1]
    rows = height // devices
    out = shape((1, devices // 2, rows, width))

    def spec(pair, k, moves):
        dims = (pair[k].shape[0], CHUNK if moves else pair[k].shape[1])
        return pl.BlockSpec(dims, lambda j: (0, j if moves else 0))

    if along == 0:
        steps = height // CHUNK
        block = pl.BlockSpec((1, devices // 2 // steps, rows, width), lambda j: (0, j, 0, 0))
    else:
        steps = width // CHUNK
        block = pl.BlockSpec((1, devices // 2, rows, CHUNK), lambda j: (0, 0, 0, j))
    return call(
        lambda *refs: weight_grad_kernel(rows, *refs),
        [out, out],
        [left[0], right[0], left[1], right[1]],
        grid=(steps,),
        in_specs=[
            spec(left, 0, along == 0),
            spec(right, 0, along == 1),
            spec(left, 1, along == 0),
            spec(right, 1, along == 1),
        ],
        out_specs=[block, block],
        flops=2 * (left[0].shape[0] + left[1].shape[0]) * height * width,
        after=after,
        streamed=streamed,
        scalars=[me],
    )


class Rows:
    def __init__(self, big_side, big_crops, small_side, small_crops):
        self.steps = big_side, small_side
        self.rows = big_side * big_crops, small_side * small_crops
        self.crops = big_crops, small_crops

    def specs(self, channels):
        first = self.steps[0]
        return [
            pl.BlockSpec((self.rows[0], channels), lambda i: (jnp.minimum(i, first - 1), 0)),
            pl.BlockSpec((self.rows[1], channels), lambda i: (jnp.maximum(i - first, 0), 0)),
        ]

    def shapes(self, channels, dtype, place=shape):
        return [place((s * r, channels), dtype) for s, r in zip(self.steps, self.rows)]

    def run(self, body, args, row_outs, whole_outs, flops, after=(), streamed=()):
        pairs = [a for a in args if isinstance(a, tuple)]
        rest = [a for a in args if not isinstance(a, tuple)]
        in_specs, flat = [], []
        scratch = []
        for k, pair in enumerate(pairs):
            flat += list(pair)
            if k in streamed:
                in_specs += [pl.BlockSpec(memory_space=pl.ANY)] * 2
                scratch += [
                    pltpu.VMEM((SLOTS, rows, pair[0].shape[1]), pair[0].dtype)
                    for rows in self.rows
                ]
            else:
                in_specs += self.specs(pair[0].shape[1])
        if streamed:
            scratch.append(pltpu.SemaphoreType.DMA((2 * len(streamed), SLOTS)))
        in_specs += [whole(a.shape) for a in rest]
        out_shapes, out_specs = [], []
        for channels, dtype, *place in row_outs:
            out_shapes += self.shapes(channels, dtype, *place)
            out_specs += self.specs(channels)
        out_shapes += [shape(dims) for dims in whole_outs]
        out_specs += [whole(dims) for dims in whole_outs]
        n_in, n_rest, n_out = len(pairs), len(rest), len(row_outs)

        def kernel(*refs):
            i = pl.program_id(0)
            refs, held = refs[: len(refs) - len(scratch)], refs[len(refs) - len(scratch) :]
            given, fixed = refs[: 2 * n_in], refs[2 * n_in : 2 * n_in + n_rest]
            made = refs[2 * n_in + n_rest :]

            def fetch(kind, step, slot):
                start = step * self.rows[kind]
                if not isinstance(step, int):
                    start = pl.multiple_of(start, self.rows[kind])
                return [
                    pltpu.make_async_copy(
                        given[2 * k + kind].at[pl.ds(start, self.rows[kind]), :],
                        held[2 * n + kind].at[slot],
                        held[-1].at[2 * n + kind, slot],
                    )
                    for n, k in enumerate(streamed)
                ]

            def start_big(step):
                for copy in fetch(0, step, lax.rem(step, SLOTS)):
                    copy.start()

            if streamed:

                @pl.when(i == 0)
                def _():
                    for step in range(SLOTS - 1):
                        for copy in fetch(0, step, step):
                            copy.start()

                pl.when(i + SLOTS - 1 < self.steps[0])(lambda: start_big(i + SLOTS - 1))
                for step in range(self.steps[1]):

                    @pl.when(i == self.steps[0] - self.steps[1] + step)
                    def _(step=step):
                        for copy in fetch(1, step, step):
                            copy.start()

            for kind in range(2):
                here = i < self.steps[0] if kind == 0 else i >= self.steps[0]

                @pl.when(here)
                def _(kind=kind):
                    blocks = list(given[kind : 2 * n_in : 2])
                    if streamed:
                        step = i if kind == 0 else i - self.steps[0]
                        slot = lax.rem(step, SLOTS)
                        for copy in fetch(kind, step, slot):
                            copy.wait()
                        for n, k in enumerate(streamed):
                            blocks[k] = held[2 * n + kind].at[slot]
                    body(i, kind, blocks, fixed, made[kind : 2 * n_out : 2], made[2 * n_out :])

        made = call(
            kernel,
            out_shapes,
            flat + rest,
            grid=(sum(self.steps),),
            in_specs=in_specs,
            out_specs=out_specs,
            flops=flops,
            after=after,
            streamed=[2 * k + j for k in streamed for j in range(2)],
            scratch=scratch,
        )
        return [tuple(made[2 * k : 2 * k + 2]) for k in range(n_out)] + list(made[2 * n_out :])

    def total(self):
        return sum(s * r for s, r in zip(self.steps, self.rows))


def add_norm(i, kind, packed, value, weight, start):
    channels = (packed.shape[1] - LANES) // 2
    width = value.shape[1]
    here = slice(start, start + width)
    there = slice(channels + start, channels + start + width)
    rows = value.shape[0]
    count = jnp.full((1, 1), rows, FLOAT) if kind == 0 else column_sum(weight)
    pivot = column_sum(value[:ROWS]) * (1.0 / ROWS)
    means, spreads = [], []
    for left in range(0, width, TILE):
        center = pivot[:, left : left + TILE]
        total, squares = 0.0, 0.0
        for low in range(0, rows, ROWS):
            apart = value[low : low + ROWS, left : left + TILE] - center
            weighted = apart if kind == 0 else apart * weight[low : low + ROWS]
            total = total + weighted
            squares = squares + weighted * apart
        total = column_sum(total) / count
        means.append(center + total)
        spreads.append(column_sum(squares) - count * jnp.square(total))
    mean, spread = jnp.concatenate(means, axis=1), jnp.concatenate(spreads, axis=1)

    before = packed[:, 2 * channels : 2 * channels + 1]
    part = count / (before + count)
    old = packed[:, here]
    delta = mean - old
    new_mean = old + delta * part
    new_spread = packed[:, there] + spread + jnp.square(delta) * (before * part)
    if kind == 0:
        new_mean = jnp.where(i == 0, mean, new_mean)
        new_spread = jnp.where(i == 0, spread, new_spread)
    packed[:, here] = new_mean
    packed[:, there] = new_spread
    return count


def add_count(i, kind, packed, count):
    channels = (packed.shape[1] - LANES) // 2
    lanes = slice(2 * channels, 2 * channels + LANES)
    wide_count = jnp.broadcast_to(count, (1, LANES))

    total = packed[:, lanes] + wide_count
    packed[:, lanes] = jnp.where(i == 0, wide_count, total) if kind == 0 else total


def add_sums(i, kind, packed, low, high, start):
    channels = (packed.shape[1] - LANES) // 2
    width = low.shape[1]
    here = slice(start, start + width)
    there = slice(channels + start, channels + start + width)

    new_low, new_high = packed[:, here] + low, packed[:, there] + high
    if kind == 0:
        new_low = jnp.where(i == 0, low, new_low)
        new_high = jnp.where(i == 0, high, new_high)
    packed[:, here] = new_low
    packed[:, there] = new_high
    if start == 0:
        packed[:, 2 * channels :] = jnp.zeros((1, LANES), FLOAT)


def reduce_stage(rows, inputs, weight, live):
    mid = weight.shape[1]

    def body(i, kind, given, fixed, made, totals):
        value = product(given[0][...], fixed[0][...])
        made[0][...] = value
        count = add_norm(i, kind, totals[0], value, fixed[1][...], 0)
        add_count(i, kind, totals[0], count)

    return rows.run(
        body,
        [inputs, weight, live],
        [(mid, FLOAT)],
        [(1, 2 * mid + LANES)],
        2 * rows.total() * weight.size,
        streamed=[0],
    )


def norm_kernel(crops, big, small, live, packed):
    channels = big.shape[1]
    weights = [None] + [live[low : low + ROWS, :] for low in range(0, crops, ROWS)]
    big_steps, small_steps = big.shape[0] // ROWS, small.shape[0] // crops

    def gather(value_of):
        def fold(value):
            return jnp.sum(value.reshape(-1, 8, channels), axis=0)

        def step(p, total):
            return total + fold(value_of(big[pl.ds(p * ROWS, ROWS), :]))

        total = lax.fori_loop(0, big_steps, step, jnp.zeros((8, channels), FLOAT), unroll=7)
        for k, weight in enumerate(weights[1:]):

            def step(p, part):
                return part + value_of(small[pl.ds(p * crops + k * ROWS, ROWS), :])

            part = lax.fori_loop(
                0, small_steps, step, jnp.zeros((ROWS, channels), FLOAT), unroll=True
            )
            total = total + fold(part * weight)
        return column_sum(total)

    count = big.shape[0] + small_steps * column_sum(live[:crops, :])
    mean = gather(lambda value: value) / count
    packed[:, :channels] = mean
    packed[:, channels : 2 * channels] = gather(lambda value: jnp.square(value - mean))
    packed[:, 2 * channels :] = jnp.broadcast_to(count, (1, LANES))


def norm_stage(rows, value, live):
    return call(
        lambda *refs: norm_kernel(rows.crops[1], *refs),
        shape((1, 2 * value[0].shape[1] + LANES)),
        [*value, live],
    )


def expand_stage(rows, second, scale, offset, weight, live):
    mid, wide = weight.shape

    def body(i, kind, given, fixed, made, totals):
        scale, offset, weight, live = fixed
        active = silu(given[0][...] * scale[...] + offset[...]).astype(HALF)
        made[1][...] = active
        for start in range(0, wide, CHUNK):
            columns = slice(start, start + CHUNK)
            value = product(active, weight[:, columns])
            made[0][:, columns] = value.astype(HALF)
            count = add_norm(i, kind, totals[0], value, live[...], start)
        add_count(i, kind, totals[0], count)

    return rows.run(
        body,
        [second, scale, offset, weight, live],
        [(wide, HALF, far_shape), (mid, HALF)],
        [(1, 2 * wide + LANES)],
        2 * rows.total() * weight.size,
    )


def pool_stage(rows, third, inputs, scale, offset):
    wide = scale.shape[1]

    def body(i, kind, given, fixed, made, totals):
        scale, offset = fixed
        steps, crops = rows.steps[kind], rows.crops[kind]
        step = i if kind == 0 else i - rows.steps[0]
        out = totals[kind]

        @pl.when(step == 0)
        def _():
            out[...] = jnp.zeros(out.shape, FLOAT)

        for start in range(0, wide, TILE):
            columns = slice(start, start + TILE)
            factor, shift = scale[:, columns], offset[:, columns]
            for low in range(0, crops, ROWS):
                total = out[low : low + ROWS, columns]
                for place in range(steps):
                    here = slice(place * crops + low, place * crops + low + ROWS)
                    residual = given[0][here, columns].astype(FLOAT) * factor + shift
                    residual = residual + given[1][here, columns].astype(FLOAT)
                    half = 0.5 * residual
                    total = total + (half * jnp.tanh(half) + half)
                out[low : low + ROWS, columns] = total

        @pl.when(step == steps - 1)
        def _():
            out[...] = out[...] * (1.0 / (steps * steps))

    return rows.run(
        body,
        [third, inputs, scale, offset],
        [],
        [(crops, wide) for crops in rows.crops],
        12 * rows.total() * wide,
        streamed=[0, 1],
    )


def residual_back_stage(rows, third, inputs, grads, scale, offset, mean, root, live, after):
    wide = scale.shape[1]

    def body(i, kind, given, fixed, made, totals):
        scale, offset, mean, root, live = fixed[2:]
        grads, crops = fixed[kind], rows.crops[kind]
        for start in range(0, wide, TILE):
            columns = slice(start, start + TILE)
            factor, shift, center = scale[:, columns], offset[:, columns], mean[:, columns]
            lows, highs = 0.0, 0.0
            for low in range(0, crops, ROWS):
                spread = grads[low : low + ROWS, columns]
                total, product_total = 0.0, 0.0
                for place in range(rows.steps[kind]):
                    here = slice(place * crops + low, place * crops + low + ROWS)
                    value = given[0][here, columns].astype(FLOAT)
                    residual = value * factor + shift + given[1][here, columns].astype(FLOAT)
                    grad = slope(residual) * spread
                    made[0][here, columns] = grad.astype(HALF)
                    total = total + grad
                    product_total = product_total + grad * (value - center)
                if kind == 1:
                    weight = live[low : low + ROWS, :]
                    total, product_total = total * weight, product_total * weight
                lows, highs = lows + column_sum(total), highs + column_sum(product_total)
            add_sums(i, kind, totals[0], lows, highs * root[:, columns], start)

    return rows.run(
        body,
        [third, inputs, *grads, scale, offset, mean, root, live],
        [(wide, HALF, far_shape)],
        [(1, 2 * wide + LANES)],
        16 * rows.total() * wide,
        after,
        streamed=[0, 1],
    )


def expand_back_stage(rows, grad, third, second, back, weight, norm, live, after):
    mid, wide = weight.shape

    def body(i, kind, given, fixed, made, totals):
        first, second, third, weight, scale, offset, mean, root, live = fixed
        total = jnp.zeros((rows.rows[kind], mid), FLOAT)
        for start in range(0, wide, CHUNK):
            columns = slice(start, start + CHUNK)
            value = (
                given[0][:, columns].astype(FLOAT) * first[:, columns]
                + given[1][:, columns].astype(FLOAT) * third[:, columns]
                + second[:, columns]
            )
            if kind == 1:
                value = value * live[...]
            value = value.astype(HALF)
            made[0][:, columns] = value
            total = total + product_outer(value, weight[:, columns])
        before = given[2][...]
        total = total * slope(before * scale[...] + offset[...])
        made[1][...] = total
        if kind == 1:
            total = total * live[...]
        high = column_sum(total * (before - mean[...])) * root[...]
        add_sums(i, kind, totals[0], column_sum(total), high, 0)

    return rows.run(
        body,
        [grad, third, second, *back, weight, *norm, live],
        [(wide, HALF, far_shape), (mid, FLOAT)],
        [(1, 2 * mid + LANES)],
        2 * rows.total() * weight.size,
        after,
        streamed=[0, 1],
    )


def slope_stage(rows, grad, value, norm, live, after):
    mid = grad[0].shape[1]

    def body(i, kind, given, fixed, made, totals):
        scale, offset, mean, root, live = fixed
        before = given[1][...]
        total = given[0][...] * slope(before * scale[...] + offset[...])
        made[0][...] = total
        if kind == 1:
            total = total * live[...]
        high = column_sum(total * (before - mean[...])) * root[...]
        add_sums(i, kind, totals[0], column_sum(total), high, 0)

    return rows.run(
        body,
        [grad, value, *norm, live],
        [(mid, FLOAT)],
        [(1, 2 * mid + LANES)],
        16 * rows.total() * mid,
        after,
    )


def norm_back_stage(rows, grad, value, back, live, after):
    mid = grad[0].shape[1]

    def body(i, kind, given, fixed, made, totals):
        first, second, third, live = fixed
        total = given[0][...] * first[...] + given[1][...] * third[...] + second[...]
        if kind == 1:
            total = total * live[...]
        made[0][...] = total.astype(HALF)

    return rows.run(
        body, [grad, value, *back, live], [(mid, HALF)], [], 6 * rows.total() * mid, after
    )[0]


def input_grad_stage(rows, grad, first, weight, after):
    wide, mid = weight.shape

    def body(i, kind, given, fixed, made, totals):
        first = given[1][...]
        for start in range(0, wide, CHUNK):
            columns = slice(start, start + CHUNK)
            value = product_outer(first, fixed[0][columns, :])
            made[0][:, columns] = (value + given[0][:, columns].astype(FLOAT)).astype(HALF)

    return rows.run(
        body,
        [grad, first, weight],
        [(wide, HALF, far_shape)],
        [],
        2 * rows.total() * weight.size,
        after,
        streamed=[0],
    )[0]


def hidden_kernel(big, small, weight, live, out, packed):
    j = pl.program_id(0)
    channels = (packed.shape[1] - LANES) // 2
    pooled = jnp.concatenate([big[...].astype(HALF), small[...].astype(HALF)])
    value = product(pooled, weight[...])
    out[...] = value
    count = column_sum(live[...])
    mean = column_sum(value * live[...]) / count
    spread = column_sum(jnp.square(value - mean) * live[...])
    packed[:, pl.ds(pl.multiple_of(j * CHUNK, CHUNK), CHUNK)] = mean
    packed[:, pl.ds(pl.multiple_of(channels + j * CHUNK, CHUNK), CHUNK)] = spread
    packed[:, 2 * channels :] = jnp.broadcast_to(count, (1, LANES))


def hidden_stage(big, small, weight, live):
    crops = live.shape[0]
    wide, channels = weight.shape
    return call(
        hidden_kernel,
        [shape((crops, channels)), shape((1, 2 * channels + LANES))],
        [big, small, weight, live],
        grid=(channels // CHUNK,),
        in_specs=[
            whole(big.shape),
            whole(small.shape),
            pl.BlockSpec((wide, CHUNK), lambda j: (0, j)),
            whole(live.shape),
        ],
        out_specs=[
            pl.BlockSpec((crops, CHUNK), lambda j: (0, j)),
            whole((1, 2 * channels + LANES)),
        ],
        flops=2 * crops * weight.size,
        streamed=[2],
    )


def lanes_of(dims):
    return lax.broadcasted_iota(jnp.int32, dims, 1)


def sums_by_view(batch, stored, views):
    row = lax.broadcasted_iota(jnp.int32, batch.shape, 0) % views
    size = stored.shape[0] // views
    return jnp.concatenate(
        [
            column_sum(jnp.where(row == v, batch, 0.0))
            + column_sum(stored[v * size : (v + 1) * size])
            for v in range(views)
        ],
        axis=1,
    )


def queue_kernel(proto, views, queue, prototypes, stored):
    rows = queue.shape[0] // views
    value = queue[...].astype(FLOAT)
    unit = value * lax.rsqrt(jnp.sum(value * value, axis=1, keepdims=True) + EPS_UNIT)
    scores = product_outer(unit.astype(HALF), prototypes[...])
    value = jnp.where(lanes_of(scores.shape) < proto, jnp.exp(scores / EPS_CODE), 0.0)
    size = stored.shape[0] // views
    stored[...] = jnp.zeros(stored.shape, FLOAT)
    for v in range(views):
        stored[v * size : v * size + rows, :] = value[v * rows : (v + 1) * rows]


def score_kernel(
    proto, views, big_rows, hidden, scale, offset, project, prototypes, stored,
    active_out, embedded_out, unit_out, scores_out, batch_out, sums,
):
    active = silu(hidden[...] * scale[...] + offset[...]).astype(HALF)
    active_out[...] = active
    embedded = product(active, project[...])
    embedded_out[...] = embedded
    root = lax.rsqrt(jnp.sum(embedded * embedded, axis=1, keepdims=True) + EPS_UNIT)
    unit = (embedded * root).astype(HALF)
    unit_out[...] = unit
    scores = product_outer(unit, prototypes[...])
    scores_out[...] = scores
    batch = scores[:big_rows]
    batch = jnp.where(lanes_of(batch.shape) < proto, jnp.exp(batch / EPS_CODE), 0.0)
    batch_out[...] = batch
    sums[...] = sums_by_view(batch, stored[...], views)


def balanced(proto, views, parts, batch, stored):
    totals = tree([part[...] for part in parts])
    width = batch.shape[1]
    totals = [totals[:, v * width : (v + 1) * width] for v in range(views)]
    totals = [jnp.where(lanes_of(t.shape) < proto, t, 1.0) for t in totals]
    row = lax.broadcasted_iota(jnp.int32, batch.shape, 0) % views
    own = jnp.zeros(batch.shape, FLOAT)
    for v in range(views):
        own = jnp.where(row == v, totals[v], own)
    batch = batch / own
    batch = batch / jnp.sum(batch, axis=1, keepdims=True)
    if stored is None:
        return batch, None
    size = stored.shape[0] // views
    stored = jnp.concatenate(
        [stored[v * size : (v + 1) * size] / totals[v] for v in range(views)]
    )
    sums = jnp.sum(stored, axis=1, keepdims=True)
    return batch, jnp.where(sums > 0.0, stored / jnp.where(sums > 0.0, sums, 1.0), 0.0)


def balance_kernel(proto, views, *refs):
    *parts, batch, stored, batch_out, stored_out, sums = refs
    batch, stored = balanced(proto, views, parts, batch[...], stored[...])
    batch_out[...] = batch
    stored_out[...] = stored
    sums[...] = sums_by_view(batch, stored, views)


def loss_kernel(proto, views, *refs):
    (
        *parts, batch, scores, share, live, embedded, hidden, scale, offset, mean, root, project, prototypes,
        grad_scores_out, grad_embedded_out, grad_out, packed,
    ) = refs
    codes, _ = balanced(proto, views, parts, batch[...], None)
    big = codes.shape[0]
    images = big // views
    slots = (scores.shape[0] - big) // images
    row = lax.broadcasted_iota(jnp.int32, codes.shape, 0) % views
    others = jnp.zeros(codes.shape, FLOAT)
    for turn in range(1, views):
        ahead = jnp.concatenate([codes[turn:], codes[:turn]])
        behind = jnp.concatenate([codes[turn - views :], codes[: turn - views]])
        others = others + jnp.where(row + turn < views, ahead, behind)
    both = codes + others
    targets = jnp.concatenate(
        [others]
        + [
            jnp.broadcast_to(both[k * views : k * views + 1], (slots, both.shape[1]))
            for k in range(images)
        ]
    )
    lanes = lanes_of(scores.shape)
    logits = jnp.where(lanes < proto, scores[...] / SOFTMAX_HEAT, -1e30)
    top = jnp.max(logits, axis=1, keepdims=True)
    powers = jnp.where(lanes < proto, jnp.exp(logits - top), 0.0)
    sums = jnp.sum(powers, axis=1, keepdims=True)
    logs = jnp.where(lanes < proto, logits - top - jnp.log(sums), 0.0)
    loss = -column_sum(jnp.sum(targets * logs, axis=1, keepdims=True) * share[...])
    mass = jnp.sum(targets, axis=1, keepdims=True)
    grad = (share[...] / SOFTMAX_HEAT) * (powers * (mass / sums) - targets)
    grad = grad.astype(HALF)
    grad_scores_out[...] = grad
    grad = product(grad, prototypes[...])
    value = embedded[...]
    scaled = lax.rsqrt(jnp.sum(value * value, axis=1, keepdims=True) + EPS_UNIT)
    unit = value * scaled
    grad = scaled * (grad - unit * jnp.sum(unit * grad, axis=1, keepdims=True))
    grad = grad.astype(HALF)
    grad_embedded_out[...] = grad
    channels = scale.shape[1]
    for start in range(0, channels, CHUNK):
        columns = slice(start, start + CHUNK)
        before = hidden[:, columns]
        part = product_outer(grad, project[columns, :])
        part = part * slope(before * scale[:, columns] + offset[:, columns])
        grad_out[:, columns] = part
        part = part * live[...]
        packed[:, columns] = column_sum(part)
        packed[:, channels + start : channels + start + CHUNK] = (
            column_sum(part * (before - mean[:, columns])) * root[:, columns]
        )
    packed[:, 2 * channels :] = jnp.broadcast_to(loss, (1, LANES))


def pooled_back_kernel(areas, big_rows, grad, hidden, live, first, second, third, weight, grad_out, big, small):
    value = grad[...] * first[...] + hidden[...] * third[...] + second[...]
    value = value * live[...]
    grad_out[...] = value
    part = product_outer(value.astype(HALF), weight[...])
    big[...] = part[:big_rows] / areas[0]
    small[...] = part[big_rows:] / areas[1]


def hidden_grad_kernel(blocks, me, left, right, out, held, sem):
    place = lax.rem(me[0], PLANE)
    width = left.shape[1] // blocks
    per = LANES // width
    planes = blocks // PLANE

    @pl.when(pl.program_id(0) == 0)
    def _():
        copies = []
        for k in range(planes):
            start = pl.multiple_of((k * PLANE + place) // per * LANES, LANES)
            copies.append(
                pltpu.make_async_copy(
                    left.at[:, pl.ds(start, LANES)],
                    held.at[:, pl.ds(k * LANES, LANES)],
                    sem.at[k],
                )
            )
        for copy in copies:
            copy.start()
        for copy in copies:
            copy.wait()

    value = product_inner(held[...].astype(HALF), right[...].astype(HALF))
    part = lax.rem(place, per)
    for k in range(planes):
        chosen = value[k * LANES : k * LANES + width]
        for other in range(1, per):
            start = k * LANES + other * width
            chosen = jnp.where(part == other, value[start : start + width], chosen)
        out[k * width : (k + 1) * width, :] = chosen


def hidden_grad_stage(left, right, devices, me, after):
    crops, height = left.shape
    width = right.shape[1]
    planes = devices // PLANE
    return call(
        lambda *refs: hidden_grad_kernel(devices, *refs),
        shape((height // PLANE, width)),
        [left, right],
        grid=(width // CHUNK,),
        in_specs=[
            pl.BlockSpec(memory_space=pl.ANY),
            pl.BlockSpec((crops, CHUNK), lambda j: (0, j)),
        ],
        out_specs=pl.BlockSpec((height // PLANE, CHUNK), lambda j: (0, j)),
        flops=2 * crops * height // PLANE * width,
        streamed=[0, 1],
        after=after,
        scalars=[me],
        scratch=[
            pltpu.VMEM((crops, planes * LANES), FLOAT),
            pltpu.SemaphoreType.DMA((planes,)),
        ],
    )


def head_grad_kernel(devices, active, grad_embedded, unit, grad_scores, out):
    project = product_inner(active[...], grad_embedded[...])
    proto = product_inner(unit[...], grad_scores[...])
    rows, lines = project.shape[0] // devices, proto.shape[0] // devices
    for k in range(devices):
        place = k % PLANE * (devices // PLANE) + k // PLANE
        half = rows // 2
        for part in range(2):
            start = k * rows + part * half
            out[place, :half, part * LANES : (part + 1) * LANES] = project[start : start + half]
        for part in range(proto.shape[1] // TILE):
            start = half + part * lines
            out[place, start : start + lines, :] = proto[
                k * lines : (k + 1) * lines, part * TILE : (part + 1) * TILE
            ]


def head_grad_stage(active, grad_embedded, unit, grad_scores, devices, after):
    rows = active.shape[1] * grad_embedded.shape[1] + unit.shape[1] * grad_scores.shape[1]
    return call(
        lambda *refs: head_grad_kernel(devices, *refs),
        shape((devices, rows // (devices * TILE), TILE)),
        [active, grad_embedded, unit, grad_scores],
        after=after,
    )


def conv(field, weight):
    return lax.conv_general_dilated(
        field,
        weight,
        (1, 1),
        ((1, 1), (1, 1)),
        dimension_numbers=("HWNC", "HWIO", "HWNC"),
        preferred_element_type=FLOAT,
    )


def conv_back(field, weight):
    return lax.conv_general_dilated(
        field,
        lax.rev(weight, (0, 1)),
        (1, 1),
        ((1, 1), (1, 1)),
        dimension_numbers=("HWNC", "HWOI", "HWNC"),
        preferred_element_type=FLOAT,
    )


def conv_filter(field, grad):
    return lax.conv_general_dilated(
        field,
        grad,
        (1, 1),
        ((1, 1), (1, 1)),
        dimension_numbers=("HWCN", "HWIO", "HWNC"),
        preferred_element_type=FLOAT,
    )


def local(
    big_crops,
    small_crops,
    small_count,
    w_reduce,
    w_spatial,
    w_expand,
    gain_mid,
    bias_mid,
    gain_wide,
    bias_wide,
    w_hidden,
    gain_head,
    bias_head,
    w_project,
    prototypes,
    queue,
):
    devices = lax.axis_size("dp")
    image_rows = small_count.shape[0]
    images = image_rows * devices
    big_rows, big_side = big_crops.shape[:2]
    small_rows, small_side = small_crops.shape[:2]
    views = big_rows // image_rows
    slots = small_rows // image_rows
    wide = big_crops.shape[3]
    mid = w_reduce.shape[1]
    hid = w_hidden.shape[1]
    proj, proto = prototypes.shape
    proto_wide = -(-proto // CHUNK) * CHUNK
    crops = big_rows + small_rows
    areas = (big_side * big_side, small_side * small_side)
    rows = Rows(big_side, big_rows, small_side, small_rows)
    sides = ((big_side, big_side, big_rows), (small_side, small_side, small_rows))
    planes = [[k * PLANE + j for j in range(PLANE)] for k in range(devices // PLANE)]
    stacks = [[k * PLANE + j for k in range(devices // PLANE)] for j in range(PLANE)]
    me = lax.axis_index("dp").astype(jnp.int32).reshape(1)

    slot_mask = (jnp.arange(slots)[None, :] < small_count[:, None]).astype(FLOAT)
    slot_flags = slot_mask.reshape(-1)
    live = jnp.tile(slot_flags, small_side)[:, None]
    crop_live = jnp.concatenate([jnp.ones((big_rows,), FLOAT), slot_flags])[:, None]
    share = 1.0 / (images * views * (views - 1.0 + small_count.astype(FLOAT)))
    share = jnp.concatenate(
        [jnp.repeat(share, views), jnp.repeat(share, slots) * slot_flags]
    )[:, None]

    def fields(pair):
        return [a.reshape(*s, a.shape[-1]) for a, s in zip(pair, sides)]

    def flat(pair):
        return tuple(a.reshape(-1, a.shape[-1]) for a in pair)

    inputs = flat((jnp.transpose(big_crops, (1, 2, 0, 3)), jnp.transpose(small_crops, (1, 2, 0, 3))))
    taps = jnp.transpose(w_spatial, (1, 0, 2))
    filters = taps.reshape(3, 3, mid, mid)
    lines = jnp.pad(jnp.transpose(prototypes), ((0, proto_wide - proto), (0, 0)))

    first, packed = reduce_stage(rows, inputs, w_reduce, live)
    scale_one, offset_one, mean_one, root_one, pixel_count = settle_norm(
        packed, gain_mid[0], bias_mid[0], devices
    )
    mid_one = fields([silu(a * scale_one + offset_one).astype(HALF) for a in first])
    second = flat([conv(a, filters) for a in mid_one])
    packed = norm_stage(rows, second, live)
    scale_two, offset_two, mean_two, root_two, _ = settle_norm(
        packed, gain_mid[1], bias_mid[1], devices
    )
    third, mid_two, packed = expand_stage(rows, second, scale_two, offset_two, w_expand, live)
    scale_three, offset_three, mean_three, root_three, _ = settle_norm(
        packed, gain_wide, bias_wide, devices
    )
    pooled_big, pooled_small = pool_stage(rows, third, inputs, scale_three, offset_three)

    hidden, packed = hidden_stage(pooled_big, pooled_small, w_hidden, crop_live)
    scale_head, offset_head, mean_head, root_head, crop_count = settle_norm(
        packed, gain_head, bias_head, devices
    )
    plane_pooled = lax.all_gather(
        jnp.concatenate([pooled_big, pooled_small]), "dp", axis_index_groups=planes, tiled=True
    )
    stored_rows = views * (-(-queue.shape[1] // 8) * 8)
    stored = call(
        lambda *refs: queue_kernel(proto, views, *refs),
        shape((stored_rows, proto_wide)),
        [queue.reshape(-1, proj), lines],
    )
    active, embedded, unit, scores, batch, sums = call(
        lambda *refs: score_kernel(proto, views, big_rows, *refs),
        [
            shape((crops, hid), HALF),
            shape((crops, proj)),
            shape((crops, proj), HALF),
            shape((crops, proto_wide)),
            shape((big_rows, proto_wide)),
            shape((1, views * proto_wide)),
        ],
        [hidden, scale_head, offset_head, w_project, lines, stored],
    )
    for step in range(ITERS - 1):
        batch, stored, sums = call(
            lambda *refs: balance_kernel(proto, views, *refs),
            [shape(batch.shape), shape(stored.shape), shape(sums.shape)],
            [*sum_parts(sums, devices), batch, stored],
            )

    loss_outs = [
        shape((crops, proto_wide), HALF),
        shape((crops, proj), HALF),
        shape((crops, hid)),
        shape((1, 2 * hid + LANES)),
    ]
    parts = sum_parts(sums, devices)
    loss_args = [
        batch,
        scores,
        share,
        crop_live,
        embedded,
        hidden,
        scale_head,
        offset_head,
        mean_head,
        root_head,
        w_project,
        lines,
    ]
    grad_scores, grad_embedded, grad_active, packed = call(
        lambda *refs: loss_kernel(proto, views, *refs),
        loss_outs,
        [*parts, *loss_args],
        grid=(1,),
        in_specs=[whole(a.shape) for a in (*parts, *loss_args)],
        out_specs=[whole(a.shape) for a in loss_outs],
        streamed=range(len(parts), len(parts) + len(loss_args)),
    )
    made = {}

    def head_work(mark):
        made["head"] = head_grad_stage(
            active, grad_embedded, unit, grad_scores, devices, [mark]
        )
        return [Far(made["head"])]

    *back, gain_head_grad, bias_head_grad, loss = settle_back(
        packed, gain_head, mean_head, root_head, crop_count, devices, [head_work]
    )
    grad_hidden, *grad_pooled = call(
        lambda *refs: pooled_back_kernel(areas, big_rows, *refs),
        [shape((crops, hid)), shape((big_rows, wide)), shape((small_rows, wide))],
        [grad_active, hidden, crop_live, *back, w_hidden],
        grid=(wide // CHUNK,),
        in_specs=[
            whole((crops, hid)),
            whole((crops, hid)),
            whole((crops, 1)),
            whole((1, hid)),
            whole((1, hid)),
            whole((1, hid)),
            pl.BlockSpec((CHUNK, hid), lambda j: (j, 0)),
        ],
        out_specs=[
            whole((crops, hid)),
            pl.BlockSpec((big_rows, CHUNK), lambda j: (0, j)),
            pl.BlockSpec((small_rows, CHUNK), lambda j: (0, j)),
        ],
        flops=2 * crops * w_hidden.size,
        streamed=[6],
    )
    plane_grad = lax.all_gather(grad_hidden, "dp", axis_index_groups=planes, tiled=True)

    grad_residual, packed = residual_back_stage(
        rows,
        third,
        inputs,
        grad_pooled,
        scale_three,
        offset_three,
        mean_three,
        root_three,
        live,
        [],
    )
    *back, gain_three, bias_three, _ = settle_back(
        packed, gain_wide, mean_three, root_three, pixel_count, devices
    )
    grad_third, grad_two, packed = expand_back_stage(
        rows,
        grad_residual,
        third,
        second,
        back,
        w_expand,
        [scale_two, offset_two, mean_two, root_two],
        live,
        [],
    )

    def expand_work(mark):
        made["expand"] = weight_grad(mid_two, grad_third, devices, me, 1, [mark], [1, 3])
        return [made["expand"][0]]

    def hidden_work(mark):
        made["hidden"] = hidden_grad_stage(plane_pooled, plane_grad, devices, me, [mark])
        return [made["hidden"]]

    *back, gain_two, bias_two, _ = settle_back(
        packed,
        gain_mid[1],
        mean_two,
        root_two,
        pixel_count,
        devices,
        [expand_work, hidden_work],
    )
    expand_sum = Scatter(*made["expand"], devices, me)
    hidden_grad = lax.psum_scatter(
        made["hidden"], "dp", scatter_dimension=0, axis_index_groups=stacks, tiled=True
    )
    head_part = lax.psum_scatter(
        made["head"], "dp", scatter_dimension=0, axis_index_groups=planes, tiled=True
    )
    head_grad = lax.psum_scatter(
        head_part, "dp", scatter_dimension=0, axis_index_groups=stacks, tiled=True
    )
    grad_second = norm_back_stage(
        rows, grad_two, second, back, live, [expand_sum.go([back[0]])]
    )
    grad_mid_one = flat([conv_back(a, filters) for a in fields(grad_second)])
    grad_one, packed = slope_stage(
        rows,
        grad_mid_one,
        first,
        [scale_one, offset_one, mean_one, root_one],
        live,
        [*expand_sum.got, Far(head_part)],
    )

    def big_work(mark):
        grad = tie(grad_second[0], [mark])
        made["big"] = conv_filter(mid_one[0], fields((grad, grad_second[1]))[0])
        return [made["big"]]

    def small_work(mark):
        grad = tie(grad_second[1], [mark])
        part = made["big"] + conv_filter(mid_one[1], fields((grad_second[0], grad))[1])
        made["spatial"] = part.reshape(9, devices, mid // devices, mid)
        made["send"] = send_rows(made["spatial"], me, [])
        return [Far(made["send"])]

    *back, gain_one, bias_one, _ = settle_back(
        packed,
        gain_mid[0],
        mean_one,
        root_one,
        pixel_count,
        devices,
        [big_work, small_work],
    )
    spatial_sum = Scatter(made["spatial"], made["send"], devices, me)
    mark = spatial_sum.go([back[0]])
    mark = expand_sum.go([mark])
    grad_first = norm_back_stage(rows, grad_one, first, back, live, [mark])
    reduce_keep, reduce_send = weight_grad(inputs, grad_first, devices, me, 0, (), [0, 2])
    grad_inputs = input_grad_stage(rows, grad_residual, grad_first, w_reduce, [reduce_keep])
    grad_big, grad_small = fields(grad_inputs)
    reduce_sum = Scatter(reduce_keep, reduce_send, devices, me)
    head_grad = head_grad[0]
    mark = spatial_sum.go([Far(grad_inputs[0])])
    mark = expand_sum.go([mark])
    mark = reduce_sum.go([mark])
    mark = expand_sum.go([mark])
    for part in (spatial_sum, reduce_sum) * 4:
        if not part.complete():
            mark = part.go([mark])
    ends = w_project.shape[0] // (2 * devices)
    project_grad = jnp.concatenate([head_grad[:ends, :LANES], head_grad[:ends, LANES:]])
    proto_grad = head_grad[ends:].reshape(-1, proj // devices, TILE)
    proto_grad = jnp.transpose(proto_grad, (1, 0, 2)).reshape(proj // devices, -1)[:, :proto]
    expand_grad = expand_sum.end()[0]
    spatial_grad = spatial_sum.end()
    reduce_grad = reduce_sum.end()[0]
    return (
        loss[0, 0],
        jnp.transpose(grad_big, (2, 0, 1, 3)),
        jnp.transpose(grad_small, (2, 0, 1, 3)),
        reduce_grad,
        jnp.transpose(spatial_grad, (1, 0, 2)),
        expand_grad,
        jnp.concatenate([gain_one, gain_two]),
        jnp.concatenate([bias_one, bias_two]),
        gain_three[0],
        bias_three[0],
        hidden_grad,
        gain_head_grad[0],
        bias_head_grad[0],
        project_grad,
        proto_grad,
    )


def solution(mesh):
    placed = (
        P("dp", None, None, None),
        P("dp", None, None, None),
        P("dp"),
        P(),
        P(),
        P(),
        P(),
        P(),
        P(),
        P(),
        P(),
        P(),
        P(),
        P(),
        P(),
        P(None, "dp", None),
    )
    return jax.shard_map(
        local,
        mesh=mesh,
        in_specs=placed,
        out_specs=(
            P(),
            P("dp", None, None, None),
            P("dp", None, None, None),
            P("dp", None),
            P("dp", None, None),
            P("dp", None),
            P(),
            P(),
            P(),
            P(),
            P("dp", None),
            P(),
            P(),
            P("dp", None),
            P("dp", None),
        ),
        check_vma=False,
    )
```
